128 devices in a mesh: pt: 8 (over y, core), cl: 16 (over z, x).
Axes of the slice: x: 4, y: 4, z: 4, core: 2. Of those that a mesh axis runs over, the one named last changes fastest.
Arguments:
- cam_jac: float32 [2, 4, 2, 9, 32768], P(None, None, None, None, ('pt', 'cl')), may hold values from -160 to 160
- pt_jac: float32 [2, 4, 2, 3, 32768], P(None, None, None, None, ('pt', 'cl')), may hold values from -40 to 40
- residual: float32 [2, 4, 2, 32768], P(None, None, None, ('pt', 'cl')), may hold values from -48 to 48
- cam_ids: int32 [2, 4, 32768], P(None, None, ('pt', 'cl')), may hold values from 0 to 127, as said below
- obs_count: int32 [2, 32768], P(None, ('pt', 'cl')), may hold values from 1 to 4
- clusters: int32 [32768, 2], P(('pt', 'cl')), may hold values from 0 to 15, as said below
- owner_map: int32 [16], replicated, may hold values from 0 to 15, each once
- prev_step: float32 [16, 9, 128], replicated, may hold values from -6 to 6
- damping: float32 [1], replicated, may hold values from 0.5 to 2
Outputs:
- camera_step: float32 [16, 9, 128], P('cl')
- point_step: float32 [3, 32768], P(None, ('pt', 'cl'))
The draws below stay inside these ranges and needn't reach their ends.
Inputs may be any that keep to these rules, and one draw needn't show every extreme that they name: Each point names two different clusters. Among the 256 points of one device no cluster is named by more than 64 points, and one cluster is named by exactly 64 points of every device. `cam_ids`: in each cluster, the 4 slots of a point name 4 consecutive cameras in slot order, counted cyclically modulo 128.
All inputs are finite; a program needn't handle non-finite values.
Results may differ from the reference program's by a relative error of at most 0.0003.
Values sent between devices are 32-bit elements; how exact they have to be, the bound alone decides.
No kernel may reach another device: no remote copies, remote signals or barrier semaphores. Data moves between devices by JAX's collectives and lax.ppermute only.
A program may use at most 128 MiB of HBM per device.

```python
import math
import jax
import jax.numpy as jnp
from jax import lax

PTS_DEV = 256
CAMS = 128
PARAMS = 9
KS = 4
NCL = 16
NPTS = 32768


def draw_clusters(key, part):
    capacity = PTS_DEV // 4
    blocks = NPTS // PTS_DEV
    favored_key, block_key = jax.random.split(jax.random.fold_in(key, 7))
    favored = jax.random.randint(favored_key, (), 0, NCL).astype(jnp.int32)
    block_keys = jax.random.split(block_key, blocks)

    def one_block(subkey):
        mix_key, row_key = jax.random.split(subkey)
        labels = (jnp.arange((NCL - 1) * capacity, dtype=jnp.int32) // capacity + favored + 1) % NCL
        labels = jax.random.permutation(mix_key, labels)
        taken = labels[:2 * PTS_DEV - capacity]
        first_rest = taken[:capacity]
        paired = jnp.sort(taken[capacity:])
        half = PTS_DEV - capacity
        left = jnp.concatenate([jnp.full((capacity,), favored, jnp.int32), paired[:half]])
        right = jnp.concatenate([first_rest, paired[half:]])
        table = jnp.stack([left, right], axis=1)
        shuffle = jax.random.permutation(row_key, PTS_DEV)
        return table[shuffle]
    return jax.vmap(one_block)(block_keys).reshape(NPTS, 2).astype(jnp.int32)


def jacobian_pair(key):
    base = jax.random.fold_in(key, 101)
    point_key, noise_key = jax.random.split(base, 2)
    point_part = jax.random.normal(point_key, (2, KS, 2, 3, NPTS), jnp.float32)
    noise_part = jax.random.normal(noise_key, (2, KS, 2, PARAMS, NPTS), jnp.float32)
    point_jac = jnp.clip(point_part, -6.0, 6.0)
    camera_jac = jnp.clip(noise_part, -6.0, 6.0)
    return (camera_jac, point_jac)


def draw_cam_jac(key, part):
    return jacobian_pair(key)[0]


def draw_pt_jac(key, part):
    return jacobian_pair(key)[1]


def draw_cam_ids(key, part):
    first_cam = jax.random.randint(jax.random.fold_in(key, 202), (2, NPTS), 0, CAMS).astype(jnp.int32)
    offsets = jnp.arange(KS, dtype=jnp.int32)[None, :, None]
    return ((first_cam[:, None, :] + offsets) % CAMS).astype(jnp.int32)


def set_ends(entries, key, smallest, largest):
    place = [jax.random.randint(jax.random.fold_in(key, axis), (), 0, length) for axis, length in enumerate(entries.shape)]
    longest = entries.shape.index(max(entries.shape))
    next_to = place[:longest] + [(place[longest] + 1) % entries.shape[longest]] + place[longest + 1:]
    return entries.at[tuple(place)].set(smallest).at[tuple(next_to)].set(largest)


def shard_levels(stream_key, dims, cuts, least, largest):
    def one(axis_at, blocks):
        steps = jax.random.uniform(jax.random.fold_in(jax.random.fold_in(stream_key, 6), axis_at), (blocks,), jnp.float32, least / len(cuts), largest / len(cuts))
        return jnp.repeat(jnp.exp(steps), dims[axis_at] // blocks).reshape((-1,) + (1,) * (len(dims) - axis_at - 1))

    gain = one(*cuts[0])
    for cut in cuts[1:]:
        gain = gain * one(*cut)
    return gain


def bell_draw(own_key, extent, deviation, bound, shards=(), kind=jnp.bfloat16):
    drawn = deviation * jax.random.normal(own_key, extent, jnp.float32)
    if shards:
        drawn = drawn * shard_levels(own_key, extent, shards, -0.22, 0.18)
    return jnp.clip(drawn, -bound, bound).astype(kind)


def setup_inputs(seed: int = 0) -> dict:
    streams_of = jax.random.split(jax.random.key(seed), 10)
    cam_jac = draw_cam_jac(jax.random.fold_in(streams_of[9], 71), 0)
    pt_jac = draw_pt_jac(jax.random.fold_in(streams_of[9], 71), 0)
    residual = bell_draw(streams_of[2], (2, KS, 2, NPTS), 8.0, 48.0, ((3, 128),), jnp.float32)
    cam_ids = draw_cam_ids(jax.random.fold_in(streams_of[9], 71), 0)
    obs_count = set_ends(jax.random.randint(streams_of[4], (2, NPTS), 1, KS + 1), jax.random.fold_in(streams_of[4], 1), 1, KS).astype(jnp.int32)
    clusters = draw_clusters(jax.random.fold_in(streams_of[9], 71), 0)
    owner_map = jax.random.permutation(streams_of[6], NCL).astype(jnp.int32)
    prev_step = bell_draw(streams_of[7], (NCL, PARAMS, CAMS), 1.0, 6.0, (), jnp.float32)
    damping = jnp.clip(jnp.exp(jax.random.uniform(streams_of[8], (1,), jnp.float32, math.log(0.5), math.log(2.0))), 0.5, 2.0)
    return dict(cam_jac=cam_jac, pt_jac=pt_jac, residual=residual, cam_ids=cam_ids, obs_count=obs_count, clusters=clusters, owner_map=owner_map, prev_step=prev_step, damping=damping)


highest = lax.Precision.HIGHEST

def lower_solve(factor, first, second, third):
    diag_one, low_ba, low_ca, diag_two, low_cb, diag_three = factor
    out_one = first / diag_one
    out_two = (second - low_ba * out_one) / diag_two
    out_three = (third - low_ca * out_one - low_cb * out_two) / diag_three
    return (out_one, out_two, out_three)

def upper_solve(factor, first, second, third):
    diag_one, low_ba, low_ca, diag_two, low_cb, diag_three = factor
    out_three = third / diag_three
    out_two = (second - low_cb * out_three) / diag_two
    out_one = (first - low_ba * out_two - low_ca * out_three) / diag_one
    return (out_one, out_two, out_three)

def point_terms(cam_jac, pt_jac, residual, cam_ids, obs_count, clusters, prev_step, damping):
    slots = cam_jac.shape[1]
    params = prev_step.shape[1]
    cams = prev_step.shape[2]
    live = (jnp.arange(slots, dtype=jnp.int32)[None, :, None] < obs_count[:, None, :]).astype(jnp.float32)
    jac_cam = cam_jac * live[:, :, None, None, :]
    jac_point = pt_jac * live[:, :, None, None, :]
    resid = residual * live[:, :, None, :]
    normal = jnp.einsum('skmap,skmbp->abp', jac_point, jac_point, precision=highest)
    normal = normal + damping[0] * jnp.eye(3, dtype=jnp.float32)[:, :, None]
    diag_one = jnp.sqrt(normal[0, 0])
    low_ba = normal[1, 0] / diag_one
    low_ca = normal[2, 0] / diag_one
    diag_two = jnp.sqrt(normal[1, 1] - low_ba * low_ba)
    low_cb = (normal[2, 1] - low_ca * low_ba) / diag_two
    diag_three = jnp.sqrt(normal[2, 2] - low_ca * low_ca - low_cb * low_cb)
    factor = (diag_one, low_ba, low_ca, diag_two, low_cb, diag_three)
    coupling = jnp.einsum('skmip,skmap->skiap', jac_cam, jac_point, precision=highest)
    coeffs = jnp.stack(lower_solve(factor, coupling[:, :, :, 0], coupling[:, :, :, 1], coupling[:, :, :, 2]), axis=3)
    grad_point = jnp.einsum('skmap,skmp->ap', jac_point, resid, precision=highest)
    reduced = jnp.stack(lower_solve(factor, grad_point[0], grad_point[1], grad_point[2]), axis=0)
    flat_prev = prev_step.transpose(1, 0, 2).reshape(params, -1)
    lookup = clusters.T[:, None, :] * cams + cam_ids
    prev_cols = jnp.moveaxis(flat_prev[:, lookup], 0, 2)
    carried = jnp.einsum('skiap,skip->sap', coeffs, prev_cols, precision=highest)
    mixed = reduced[None] + carried[::-1]
    rhs_terms = jnp.einsum('skiap,sap->skip', coeffs, mixed, precision=highest) - jnp.einsum('skmip,skmp->skip', jac_cam, resid, precision=highest)
    return (jac_cam, coeffs, rhs_terms, factor, reduced)

def point_update(coeffs, factor, reduced, flat_steps, lookup):
    step_cols = jnp.moveaxis(flat_steps[:, lookup], 0, 2)
    total = reduced + jnp.einsum('skiap,skip->ap', coeffs, step_cols, precision=highest)
    solved = upper_solve(factor, total[0], total[1], total[2])
    return -jnp.stack(solved, axis=0)

def reference(cam_jac, pt_jac, residual, cam_ids, obs_count, clusters, owner_map, prev_step, damping):
    jac_cam, coeffs, rhs_terms, factor, reduced = point_terms(cam_jac, pt_jac, residual, cam_ids, obs_count, clusters, prev_step, damping)
    groups = prev_step.shape[0]
    params = prev_step.shape[1]
    cams = prev_step.shape[2]
    order = params * cams
    slots = cam_jac.shape[1]
    npts = cam_jac.shape[-1]
    width = min(npts, PTS_DEV * 8)
    count = npts // width
    component = jnp.arange(params, dtype=jnp.int32)
    slot_eye = jnp.eye(slots, dtype=jnp.float32)

    def add_block(matrix, block):
        start = (block * width).astype(jnp.int32)
        cam_block = lax.dynamic_slice_in_dim(cam_ids, start, width, 2)
        clus_block = lax.dynamic_slice_in_dim(clusters, start, width, 0).T
        jac_block = lax.dynamic_slice_in_dim(jac_cam, start, width, 4)
        coef_block = lax.dynamic_slice_in_dim(coeffs, start, width, 4)
        self_gram = jnp.einsum('skmip,skmjp->skijp', jac_block, jac_block, precision=highest)
        cross_gram = jnp.einsum('skiap,sljap->sklijp', coef_block, coef_block, precision=highest)
        values = slot_eye[None, :, :, None, None, None] * self_gram[:, :, None] - cross_gram
        row_index = component[None, None, None, :, None, None] * cams + cam_block[:, :, None, None, None, :]
        col_index = component[None, None, None, None, :, None] * cams + cam_block[:, None, :, None, None, :]
        places = (clus_block[:, None, None, None, None, :] * order + row_index) * order + col_index
        return (matrix.at[places.reshape(-1)].add(values.reshape(-1)), None)
    matrix, unused = lax.scan(add_block, jnp.zeros((groups * order * order,), jnp.float32), jnp.arange(count, dtype=jnp.int32))
    rhs_places = (clusters.T[:, None, None, :] * params + component[None, None, :, None]) * cams + cam_ids[:, :, None, :]
    right_side = jnp.zeros((groups * order,), jnp.float32).at[rhs_places.reshape(-1)].add(rhs_terms.reshape(-1))
    matrix = matrix.reshape(groups, order, order) + damping[0] * jnp.eye(order, dtype=jnp.float32)
    right_side = right_side.reshape(groups, order)

    def solve_one(pair):
        chol = jnp.linalg.cholesky(pair[0])
        return jax.scipy.linalg.cho_solve((chol, True), pair[1])
    steps = lax.map(solve_one, (matrix, right_side)).reshape(groups, params, cams)
    camera_step = jnp.zeros_like(steps).at[owner_map].set(steps)
    flat_steps = steps.transpose(1, 0, 2).reshape(params, -1)
    lookup = clusters.T[:, None, :] * cams + cam_ids
    point_step = point_update(coeffs, factor, reduced, flat_steps, lookup)
    return (camera_step, point_step)
```

```python
import jax
import jax.numpy as jnp
from jax import lax
from jax.experimental import pallas as pl
from jax.experimental.pallas import tpu as pltpu
from jax.sharding import PartitionSpec as P

f32 = jnp.float32
bf16 = jnp.bfloat16
LANES = 128
SLOTS = 4
PARAMS = 9
GROUPS = 32
UNK = 27
DIAG = 45
ROW_Q = 45
ROW_D = (0, 54, 135, 216)
BAND = 304
HALF = BAND // 2
PACK = 56
VMEM_LIMIT = 56 * 1024 * 1024


def split3(value):
    high = value.astype(bf16)
    rest = value - high.astype(f32)
    mid = rest.astype(bf16)
    low = (rest - mid.astype(f32)).astype(bf16)
    return high, mid, low


def dot_nt(left, right):
    return lax.dot_general(left, right, (((1,), (1,)), ((), ())), preferred_element_type=f32)


def iota(shape, dim):
    return lax.broadcasted_iota(jnp.int32, shape, dim)


def lanes_from(value, index):
    return jnp.take_along_axis(value, index, axis=1)


def spread_row(chunk, row):
    return jnp.broadcast_to(chunk[row : row + 1, :], (8, LANES))


def lookup_dot(table, masks, cam_ref, jac_ref, out_ref):
    for half in range(2):
        cols = slice(half * LANES, (half + 1) * LANES)
        for s in range(2):
            for k in range(SLOTS):
                index = jnp.broadcast_to(cam_ref[s, k : k + 1, cols], (16, LANES))
                sums = [None, None]
                for i in range(PARAMS):
                    got = jnp.concatenate(
                        [
                            lanes_from(table[i][0:8], index[0:8]),
                            lanes_from(table[i][8:16], index[8:16]),
                        ],
                        axis=0,
                    )
                    for m in range(2):
                        row = k * PARAMS + i
                        term = got * jac_ref[m, s, row : row + 1, cols]
                        sums[m] = term if sums[m] is None else sums[m] + term
                for m in range(2):
                    row = s * 8 + m * 4 + k
                    picked = jnp.sum(sums[m] * masks[s][half], axis=0, keepdims=True)
                    out_ref[row : row + 1, cols] = picked


def cluster_masks(cluster_rows):
    masks = []
    for s in range(2):
        per_half = []
        for half in range(2):
            row = cluster_rows[s : s + 1, half * LANES : (half + 1) * LANES]
            per_half.append((iota((16, LANES), 0) == row).astype(f32))
        masks.append(per_half)
    return masks


def points_kernel(
    owner_ref,
    damp_ref,
    jac_ref,
    jp_ref,
    res_ref,
    cam_ref,
    count_ref,
    clus_ref,
    prev_ref,
    send_ref,
    proj_ref,
    fact_ref,
    dots,
    packed,
):
    npts = 2 * LANES
    clus = clus_ref[...]
    dest = jnp.zeros_like(clus)
    for c in range(16):
        dest = jnp.where(clus == c, owner_ref[c], dest)
    slot_row = iota((8, npts), 0) % 4
    live = jnp.concatenate(
        [(slot_row < count_ref[s : s + 1, :]).astype(f32) for s in range(2)], axis=0
    )
    jp = [jp_ref[a] * live for a in range(3)]
    res = res_ref[...] * live

    def total(value):
        return jnp.sum(value, axis=0, keepdims=True)

    damp = damp_ref[0]
    inv1 = 1.0 / jnp.sqrt(total(jp[0] * jp[0]) + damp)
    l21 = total(jp[1] * jp[0]) * inv1
    l31 = total(jp[2] * jp[0]) * inv1
    inv2 = 1.0 / jnp.sqrt(total(jp[1] * jp[1]) + damp - l21 * l21)
    l32 = (total(jp[2] * jp[1]) - l31 * l21) * inv2
    inv3 = 1.0 / jnp.sqrt(total(jp[2] * jp[2]) + damp - l31 * l31 - l32 * l32)
    p1 = jp[0] * inv1
    p2 = (jp[1] - l21 * p1) * inv2
    p3 = (jp[2] - l31 * p1 - l32 * p2) * inv3
    proj = [p1, p2, p3]
    grad = [total(jp[a] * res) for a in range(3)]
    h1 = grad[0] * inv1
    h2 = (grad[1] - l21 * h1) * inv2
    h3 = (grad[2] - l31 * h1 - l32 * h2) * inv3
    h = [h1, h2, h3]
    for a in range(3):
        proj_ref[a] = proj[a]
    for n, row in enumerate([inv1, inv2, inv3, l21, l31, l32, h1, h2, h3]):
        fact_ref[n : n + 1, :] = row

    masks = cluster_masks(clus)
    table = [prev_ref[i] for i in range(PARAMS)]
    lookup_dot(table, masks, cam_ref, jac_ref, dots)
    dot_all = dots[...]
    wt = -res
    for a in range(3):
        terms = proj[a] * dot_all
        carried = [jnp.sum(terms[8 * s : 8 * s + 8], axis=0, keepdims=True) for s in range(2)]
        mixed = jnp.concatenate(
            [jnp.broadcast_to(h[a] + carried[1 - s], (8, npts)) for s in range(2)], axis=0
        )
        wt = wt + proj[a] * mixed

    for s in range(2):
        cols = slice(s * npts, (s + 1) * npts)
        for m in range(2):
            base = m * PACK
            for k in range(SLOTS):
                on = live[s * 8 + m * 4 + k : s * 8 + m * 4 + k + 1, :]
                packed[base + 9 * k : base + 9 * k + 9, cols] = (
                    jac_ref[m, s, 9 * k : 9 * k + 9, :] * on
                )
            rows = slice(s * 8 + m * 4, s * 8 + m * 4 + 4)
            for a in range(3):
                packed[base + 36 + 4 * a : base + 40 + 4 * a, cols] = proj[a][rows]
            packed[base + 48 : base + 52, cols] = wt[rows]
            packed[base + 52 : base + 53, cols] = cam_ref[s, 0:1, :].astype(f32)
            packed[base + 53 : base + 56, cols] = jnp.zeros((3, npts), f32)

    dest_row = jnp.concatenate([dest[0:1], dest[1:2]], axis=1)
    hot = (iota((16, 2 * npts), 0) == dest_row).astype(f32)
    before = (iota((2 * npts, 2 * npts), 1) < iota((2 * npts, 2 * npts), 0)).astype(bf16)
    earlier = dot_nt(hot.astype(bf16), before)
    place = jnp.sum(earlier * hot, axis=0, keepdims=True)
    slot = dest_row * 64 + place.astype(jnp.int32)
    parts = split3(packed[...])
    left = jnp.concatenate(parts, axis=0)
    low_half = iota((PACK, LANES), 1) < 64
    for pair in range(8):
        slots = iota((LANES, 2 * npts), 0) + pair * LANES
        pick = (slots == slot).astype(f32).astype(bf16)
        got = dot_nt(left, pick)
        full = got[0 : 2 * PACK] + got[2 * PACK : 4 * PACK] + got[4 * PACK : 6 * PACK]
        first = full[0:PACK]
        second = full[PACK : 2 * PACK]
        first_r = pltpu.roll(first, 64, 1)
        second_r = pltpu.roll(second, 64, 1)
        send_ref[2 * pair] = jnp.where(low_half, first, second_r)
        send_ref[2 * pair + 1] = jnp.where(low_half, first_r, second)


def band_kernel(core_ref, recv_ref, keep_ref, give_ref, rows, wide, hots):
    low_half = iota((8, LANES), 1) < 64
    quant = [[], []]
    for r in range(53):
        even = recv_ref[pl.ds(r, 8, stride=2 * PACK), :]
        odd = recv_ref[pl.ds(PACK + r, 8, stride=2 * PACK), :]
        even_r = pltpu.roll(even, 64, 1)
        odd_r = pltpu.roll(odd, 64, 1)
        quant[0].append(jnp.where(low_half, even, odd_r))
        quant[1].append(jnp.where(low_half, even_r, odd))

    def jac(k, m, i):
        return quant[m][9 * k + i]

    def proj(k, m, a):
        return quant[m][36 + 4 * a + k]

    def wt(k, m):
        return quant[m][48 + k]

    cam = quant[0][52].astype(jnp.int32)
    camera_of = 4 * (iota((LANES, LANES), 0) % GROUPS) + iota((LANES, LANES), 0) // GROUPS
    for b in range(8):
        cam_b = jnp.broadcast_to(cam[b : b + 1, :], (LANES, LANES))
        for k in range(SLOTS):
            hots[k, :, b * LANES : (b + 1) * LANES] = (
                (camera_of == (cam_b + k) % LANES).astype(f32).astype(bf16)
            )

    sizes = [304, 224, 144, 64]
    out = None
    for k in range(SLOTS):
        count = 0

        def put(row, value):
            rows[8 * row : 8 * row + 8, :] = value

        for dist in range(SLOTS - k):
            other = k + dist
            mix = [[None, None], [None, None]]
            for m in range(2):
                for n in range(2):
                    if dist == 0 and n < m:
                        mix[m][n] = mix[n][m]
                        continue
                    acc = proj(k, m, 0) * proj(other, n, 0)
                    acc = acc + proj(k, m, 1) * proj(other, n, 1)
                    acc = acc + proj(k, m, 2) * proj(other, n, 2)
                    same = dist == 0 and m == n
                    mix[m][n] = (1.0 - acc) if same else -acc
            for j in range(PARAMS):
                left = [
                    mix[m][0] * jac(other, 0, j) + mix[m][1] * jac(other, 1, j) for m in range(2)
                ]
                for i in range(PARAMS):
                    if dist == 0 and i > j:
                        continue
                    value = jac(k, 0, i) * left[0] + jac(k, 1, i) * left[1]
                    if dist == 0:
                        row = i * 9 - i * (i - 1) // 2 + (j - i)
                    else:
                        row = ROW_D[dist] + i * 9 + j
                    put(row, value)
                    count += 1
        for i in range(PARAMS):
            put(ROW_Q + i, jac(k, 0, i) * wt(k, 0) + jac(k, 1, i) * wt(k, 1))
            count += 1
        size = sizes[k]
        for row in range(count, size):
            put(row, jnp.zeros((8, LANES), f32))
        for b in range(8):
            piece = rows[pl.ds(b, size, stride=8), :]
            for n, part in enumerate(split3(piece)):
                wide[n, 0:size, b * LANES : (b + 1) * LANES] = part
        hot = hots[k]
        got = dot_nt(wide[0, 0:size, :], hot)
        got = got + dot_nt(wide[1, 0:size, :], hot)
        got = got + dot_nt(wide[2, 0:size, :], hot)
        if out is None:
            out = got
        else:
            out = jnp.concatenate([out[0:size] + got, out[size:]], axis=0)
    core = core_ref[0]
    low, high = out[0:HALF], out[HALF:BAND]
    keep_ref[...] = jnp.where(core == 0, low, high)
    give_ref[...] = jnp.where(core == 0, high, low)


def factor(size, diag, side, side_chunks):
    chunks = len(diag[0])
    inverse = []
    for k in range(size):
        pivot = spread_row(diag[k][k // 8], k % 8)
        root = lax.rsqrt(pivot)
        root = root * (1.5 - 0.5 * pivot * root * root)
        inverse.append(root)
        for v in range(k // 8, chunks):
            diag[k][v] = diag[k][v] * root
        for e in side_chunks:
            side[k][e] = side[k][e] * root
        for r in range(k + 1, size):
            coef = spread_row(diag[k][r // 8], r % 8)
            for v in range(r // 8, chunks):
                diag[r][v] = diag[r][v] - coef * diag[k][v]
            for e in side_chunks:
                side[r][e] = side[r][e] - coef * side[k][e]
    return inverse


def schur(size, side, lane):
    within = lane % GROUPS
    results = []
    for which in range(2):
        full = []
        for r in range(size):
            full.append(
                [
                    lanes_from(side[r][v % 2], within + GROUPS * (2 * which + v // 2))
                    for v in range(4)
                ]
            )
        per_a = []
        for a in range(UNK):
            acc = [None, None]
            for r in range(size):
                coef = spread_row(full[r][a // 8], a % 8)
                for e in range(2):
                    term = coef * side[r][e]
                    acc[e] = term if acc[e] is None else acc[e] + term
            per_a.append(acc)
        results.append(per_a)
    return results


def apply_schur(left, right, diag, side, lane, down, up, keep):
    within = lane % GROUPS
    part = lane // GROUPS
    from_down = (within - down + GROUPS) % GROUPS
    from_up = (within + up) % GROUPS
    pack_down = part * GROUPS + from_down
    pack_up = part * GROUPS + from_up
    is_left = part < 2
    is_rhs = jnp.logical_and(part == 1, iota((8, LANES), 0) == 3)
    for a in range(UNK):
        fresh = []
        for e in range(2):
            by_down = lanes_from(right[a][e], pack_down)
            by_up = lanes_from(left[a][e], pack_up)
            new = -jnp.where(is_left, by_down, by_up)
            if keep:
                new = new + side[a][e]
                if e == 1:
                    new = new - jnp.where(is_rhs, by_up, 0.0)
            elif e == 1:
                new = new + jnp.where(is_rhs, side[a][e] - by_up, 0.0)
            fresh.append(new)
        for v in range(a // 8, 4):
            own = lanes_from(right[a][v % 2], from_down + GROUPS * (2 + v // 2))
            other = lanes_from(left[a][v % 2], from_up + GROUPS * (v // 2))
            diag[a][v] = diag[a][v] - own - other
        side[a] = fresh


def solve_kernel(
    core_ref, damp_ref, mine_ref, other_ref, step_ref, cast_ref, rep, back, dmat, lmat, umat, smat, xrow, d0, l0, u0
):
    lane = iota((8, LANES), 1)
    within = lane % GROUPS
    part = lane // GROUPS
    core = core_ref[0]
    low = jnp.where(core == 0, mine_ref[...], other_ref[...])
    high = jnp.where(core == 0, other_ref[...], mine_ref[...])
    row = iota((HALF, LANES), 0)
    on_diag = row < 0
    for i in range(PARAMS):
        on_diag = jnp.logical_or(on_diag, row == i * 9 - i * (i - 1) // 2)
    low = low + jnp.where(on_diag, damp_ref[0], 0.0)
    first_rows = HALF // 8
    for n in range(BAND // 8):
        chunk = low[8 * n : 8 * n + 8] if n < first_rows else high[8 * n - HALF : 8 * n - HALF + 8]
        for r in range(4):
            rep[r, 8 * n : 8 * n + 8, :] = lanes_from(chunk, within + GROUPS * r)
            if r > 0:
                back[r - 1, 8 * n : 8 * n + 8, :] = lanes_from(
                    chunk, (within + GROUPS - 1) % GROUPS + GROUPS * r
                )
    zero = jnp.zeros((UNK, 32, LANES), f32)
    dmat[...] = zero
    lmat[...] = zero
    umat[...] = zero
    d0[...] = jnp.zeros_like(d0)
    l0[...] = jnp.zeros_like(l0)
    u0[...] = jnp.zeros_like(u0)

    def tri(i):
        return i * 9 - i * (i - 1) // 2

    for i in range(PARAMS):
        d0[i, i:9, :] = rep[0, tri(i) : tri(i) + 9 - i, :]
        for d in range(1, 4):
            u0[i, 9 * d - 9 : 9 * d, :] = rep[0, ROW_D[d] + 9 * i : ROW_D[d] + 9 * i + 9, :]
            l0[i, 27 - 9 * d : 36 - 9 * d, :] = back[3 - d, pl.ds(ROW_D[d] + i, 9, stride=9), :]
        l0[i, 27:28, :] = rep[0, ROW_Q + i : ROW_Q + i + 1, :]
        for r in range(1, 4):
            row = 9 * r - 9 + i
            dmat[row, row : 9 * r, :] = rep[r, tri(i) : tri(i) + 9 - i, :]
            for q in range(r + 1, 4):
                base = ROW_D[q - r] + 9 * i
                dmat[row, 9 * q - 9 : 9 * q, :] = rep[r, base : base + 9, :]
            for q in range(1, 4):
                if q < r:
                    base = ROW_D[4 + q - r] + 9 * i
                    umat[row, 9 * q - 9 : 9 * q, :] = rep[r, base : base + 9, :]
                if q > r:
                    base = ROW_D[4 + r - q] + i
                    lmat[row, 9 * q - 9 : 9 * q, :] = back[q - 1, pl.ds(base, 9, stride=9), :]
            lmat[row, 27:28, :] = rep[r, ROW_Q + i : ROW_Q + i + 1, :]

    def pack(lm, um):
        return [
            jnp.where(
                part == 0,
                lm[8 * e : 8 * e + 8],
                jnp.where(
                    part == 1,
                    lm[16 + 8 * e : 24 + 8 * e],
                    jnp.where(part == 2, um[8 * e : 8 * e + 8], um[16 + 8 * e : 24 + 8 * e]),
                ),
            )
            for e in range(2)
        ]

    def chunked(value, count):
        return [value[8 * v : 8 * v + 8] for v in range(count)]

    diag0 = [chunked(d0[i], 2) for i in range(PARAMS)]
    side0 = [pack(l0[i], u0[i]) for i in range(PARAMS)]
    inv0 = factor(PARAMS, diag0, side0, (0, 1))
    left, right = schur(PARAMS, side0, lane)
    diag = [chunked(dmat[a], 4) for a in range(UNK)]
    side = [pack(lmat[a], umat[a]) for a in range(UNK)]
    apply_schur(left, right, diag, side, lane, 0, 1, True)
    for a in range(UNK):
        for v in range(4):
            dmat[a, 8 * v : 8 * v + 8, :] = diag[a][v]
        for e in range(2):
            smat[a, 8 * e : 8 * e + 8, :] = side[a][e]

    def level(step, carry):
        stride = lax.shift_left(jnp.int32(1), step)
        diag_in = [chunked(dmat[a], 4) for a in range(UNK)]
        side_in = [chunked(smat[a], 2) for a in range(UNK)]
        diag = [list(row) for row in diag_in]
        side = [list(row) for row in side_in]
        factor(UNK, diag, side, (0, 1))
        left, right = schur(UNK, side, lane)
        diag = [list(row) for row in diag_in]
        side = [list(row) for row in side_in]
        apply_schur(left, right, diag, side, lane, stride, stride, False)
        for a in range(UNK):
            for v in range(4):
                dmat[a, 8 * v : 8 * v + 8, :] = diag[a][v]
            for e in range(2):
                smat[a, 8 * e : 8 * e + 8, :] = side[a][e]
        return carry

    lax.fori_loop(0, 5, level, jnp.int32(0))

    diag = [chunked(dmat[a], 4) for a in range(UNK)]
    side = [chunked(smat[a], 2) for a in range(UNK)]
    for a in range(UNK):
        for v in range(a // 8, 4):
            from_l = lanes_from(side[a][v % 2], within + GROUPS * (v // 2))
            from_u = lanes_from(side[a][v % 2], within + GROUPS * (2 + v // 2))
            diag[a][v] = diag[a][v] + from_l + from_u
    inverse = factor(UNK, diag, side, (1,))
    todo = [spread_row(lanes_from(side[a][1], within + GROUPS), 3) for a in range(UNK)]
    value = [None] * UNK
    for k in range(UNK - 1, -1, -1):
        value[k] = todo[k] * inverse[k]
        for r in range(k):
            todo[r] = todo[r] - spread_row(diag[r][k // 8], k % 8) * value[k]
    for a in range(UNK):
        xrow[a : a + 1, :] = value[a][0:1]
    xrow[UNK:32, :] = jnp.zeros((5, LANES), f32)
    own = chunked(xrow[...], 4)
    prev = [lanes_from(c, (lane + LANES - 1) % LANES) for c in own]
    both = pack(jnp.concatenate(prev, axis=0), jnp.concatenate(own, axis=0))
    todo0 = []
    for i in range(PARAMS):
        terms = side0[i][0] * both[0] + side0[i][1] * both[1]
        terms = terms + pltpu.roll(terms, 64, 1)
        terms = terms + pltpu.roll(terms, 32, 1)
        rhs = spread_row(lanes_from(side0[i][1], within + GROUPS), 3)
        summed = jnp.broadcast_to(jnp.sum(terms, axis=0, keepdims=True), (8, LANES))
        todo0.append(rhs - summed)
    value0 = [None] * PARAMS
    for k in range(PARAMS - 1, -1, -1):
        value0[k] = todo0[k] * inv0[k]
        for r in range(k):
            todo0[r] = todo0[r] - spread_row(diag0[r][k // 8], k % 8) * value0[k]
    camera = (lane % 4) * GROUPS + lane // 4
    for i in range(PARAMS):
        row = jnp.where(
            part == 0,
            value0[i],
            jnp.where(part == 1, value[i], jnp.where(part == 2, value[9 + i], value[18 + i])),
        )
        step_ref[i : i + 1, :] = lanes_from(row, camera)[0:1]
    for dest in range(16):
        cast_ref[dest, 0:PARAMS, :] = step_ref[...]
        cast_ref[dest, PARAMS:16, :] = jnp.zeros((16 - PARAMS, LANES), f32)


def update_kernel(owner_ref, all_ref, jac_ref, proj_ref, fact_ref, cam_ref, clus_ref, out_ref, dots):
    clus = clus_ref[...]
    dest = jnp.zeros_like(clus)
    for c in range(16):
        dest = jnp.where(clus == c, owner_ref[c], dest)
    masks = cluster_masks(dest)
    table = [all_ref[pl.ds(i, 16, stride=16), :] for i in range(PARAMS)]
    lookup_dot(table, masks, cam_ref, jac_ref, dots)
    dot_all = dots[...]

    def fact(n):
        return fact_ref[n : n + 1, :]

    tot = [fact(6 + a) + jnp.sum(proj_ref[a] * dot_all, axis=0, keepdims=True) for a in range(3)]
    x3 = tot[2] * fact(2)
    x2 = (tot[1] - fact(5) * x3) * fact(1)
    x1 = (tot[0] - fact(3) * x2 - fact(4) * x3) * fact(0)
    out_ref[0:1, :] = -x1
    out_ref[1:2, :] = -x2
    out_ref[2:3, :] = -x3


def smem():
    return pl.BlockSpec(memory_space=pltpu.SMEM)


def vmem():
    return pl.BlockSpec(memory_space=pltpu.VMEM)


def params():
    return pltpu.CompilerParams(vmem_limit_bytes=VMEM_LIMIT)


def run_points(owner_map, damping, jac, jp, res, cam_ids, obs_count, clus, prev):
    npts = 256
    return pl.pallas_call(
        points_kernel,
        out_shape=(
            jax.ShapeDtypeStruct((16, PACK, LANES), f32),
            jax.ShapeDtypeStruct((3, 16, npts), f32),
            jax.ShapeDtypeStruct((9, npts), f32),
        ),
        in_specs=[smem(), smem()] + [vmem()] * 7,
        out_specs=(vmem(), vmem(), vmem()),
        scratch_shapes=[pltpu.VMEM((16, npts), f32), pltpu.VMEM((2 * PACK, 2 * npts), f32)],
        compiler_params=params(),
        name="points",
    )(owner_map, damping, jac, jp, res, cam_ids, obs_count, clus, prev)


def run_band(core, recv):
    return pl.pallas_call(
        band_kernel,
        out_shape=(
            jax.ShapeDtypeStruct((HALF, LANES), f32),
            jax.ShapeDtypeStruct((HALF, LANES), f32),
        ),
        in_specs=[smem(), vmem()],
        out_specs=(vmem(), vmem()),
        scratch_shapes=[
            pltpu.VMEM((BAND * 8, LANES), f32),
            pltpu.VMEM((3, BAND, 1024), bf16),
            pltpu.VMEM((4, LANES, 1024), bf16),
        ],
        compiler_params=params(),
        name="band",
    )(core, recv)


def run_solve(core, damping, mine, other):
    return pl.pallas_call(
        solve_kernel,
        out_shape=(
            jax.ShapeDtypeStruct((PARAMS, LANES), f32),
            jax.ShapeDtypeStruct((16, 16, LANES), f32),
        ),
        in_specs=[smem(), smem(), vmem(), vmem()],
        out_specs=(vmem(), vmem()),
        scratch_shapes=[
            pltpu.VMEM((4, BAND, LANES), f32),
            pltpu.VMEM((3, BAND, LANES), f32),
            pltpu.VMEM((UNK, 32, LANES), f32),
            pltpu.VMEM((UNK, 32, LANES), f32),
            pltpu.VMEM((UNK, 32, LANES), f32),
            pltpu.VMEM((UNK, 16, LANES), f32),
            pltpu.VMEM((32, LANES), f32),
            pltpu.VMEM((PARAMS, 16, LANES), f32),
            pltpu.VMEM((PARAMS, 32, LANES), f32),
            pltpu.VMEM((PARAMS, 32, LANES), f32),
        ],
        compiler_params=params(),
        name="solve",
    )(core, damping, mine, other)


def run_update(owner_map, everything, jac, proj, fact, cam_ids, clus):
    return pl.pallas_call(
        update_kernel,
        out_shape=jax.ShapeDtypeStruct((3, 256), f32),
        in_specs=[smem()] + [vmem()] * 6,
        out_specs=vmem(),
        scratch_shapes=[pltpu.VMEM((16, 256), f32)],
        compiler_params=params(),
        name="update",
    )(owner_map, everything, jac, proj, fact, cam_ids, clus)


def sum_over_points(keep, give, ring):
    swap = [(i, i ^ 1) for i in range(ring)]
    half = keep + lax.ppermute(give, "pt", swap)
    moved = [
        lax.ppermute(half, "pt", [(i, (i + 2 * d) % ring) for i in range(ring)]) for d in range(1, 4)
    ]
    mine = (half + moved[1]) + (moved[0] + moved[2])
    return mine, lax.ppermute(mine, "pt", swap)


def per_device(
    cam_jac, pt_jac, residual, cam_ids, obs_count, clusters, owner_map, prev_step, damping
):
    npts = cam_jac.shape[-1]
    core = (lax.axis_index("pt") % 2).astype(jnp.int32).reshape(1)
    jac = cam_jac.transpose(2, 0, 1, 3, 4).reshape(2, 2, SLOTS * PARAMS, npts)
    jp = pt_jac.transpose(3, 0, 2, 1, 4).reshape(3, 16, npts)
    res = residual.transpose(0, 2, 1, 3).reshape(16, npts)
    clus = clusters.T
    send, proj, fact = run_points(
        owner_map, damping, jac, jp, res, cam_ids, obs_count, clus, prev_step.transpose(1, 0, 2)
    )
    recv = lax.all_to_all(send, "cl", split_axis=0, concat_axis=0, tiled=True)
    keep, give = run_band(core, recv.reshape(16 * PACK, LANES))
    mine, other = sum_over_points(keep, give, lax.axis_size("pt"))
    step, cast = run_solve(core, damping, mine, other)
    everything = lax.all_to_all(cast, "cl", split_axis=0, concat_axis=0, tiled=True)
    point_step = run_update(
        owner_map, everything.reshape(256, LANES), jac, proj, fact, cam_ids, clus
    )
    return (step[None], point_step)


def solution(mesh):
    in_specs = (
        P(None, None, None, None, ("pt", "cl")),
        P(None, None, None, None, ("pt", "cl")),
        P(None, None, None, ("pt", "cl")),
        P(None, None, ("pt", "cl")),
        P(None, ("pt", "cl")),
        P(("pt", "cl"), None),
        P(),
        P(),
        P(),
    )
    out_specs = (P("cl", None, None), P(None, ("pt", "cl")))
    return jax.shard_map(
        per_device, mesh=mesh, in_specs=in_specs, out_specs=out_specs, check_vma=False
    )
```

```python
import jax
import jax.numpy as jnp
from jax import lax
from jax.experimental import pallas as pl
from jax.experimental.pallas import tpu as pltpu
from jax.sharding import PartitionSpec as P

f32 = jnp.float32
bf16 = jnp.bfloat16
LANES = 128
SLOTS = 4
PARAMS = 9
GROUPS = 32
UNK = 27
DIAG = 45
ROW_Q = 45
ROW_D = (0, 54, 135, 216)
BAND = 304
HALF = BAND // 2
PACK = 56
MIB = 1024 * 1024


def split3(value):
    high = value.astype(bf16)
    rest = value - high.astype(f32)
    mid = rest.astype(bf16)
    low = (rest - mid.astype(f32)).astype(bf16)
    return high, mid, low


def dot_nt(left, right):
    return lax.dot_general(left, right, (((1,), (1,)), ((), ())), preferred_element_type=f32)


def iota(shape, dim):
    return lax.broadcasted_iota(jnp.int32, shape, dim)


def lanes_from(value, index):
    return jnp.take_along_axis(value, index, axis=1)


def spread_row(chunk, row):
    return jnp.broadcast_to(chunk[row : row + 1, :], (8, LANES))


def lookup_dot(table, last, masks, cam_ref, jac_ref, out_ref):
    for half in range(2):
        cols = slice(half * LANES, (half + 1) * LANES)
        for s in range(2):
            rows, picks = masks[s][half]
            for k in range(SLOTS):
                index = jnp.broadcast_to(cam_ref[s, k : k + 1, cols], (8, LANES))
                chosen = lanes_from(table[0], index)
                for c in range(1, 16):
                    chosen = jnp.where(picks[c], lanes_from(table[c], index), chosen)
                ninth = lanes_from(last[0], index) * rows[0] + lanes_from(last[1], index) * rows[1]
                for m in range(2):
                    base = s * SLOTS * PARAMS + k * PARAMS
                    terms = chosen * jac_ref[m, base : base + 8, cols]
                    terms = terms + ninth * jac_ref[m, base + 8 : base + 9, cols]
                    row = s * 8 + m * 4 + k
                    out_ref[row : row + 1, cols] = jnp.sum(terms, axis=0, keepdims=True)


def cluster_masks(cluster_rows):
    masks = []
    for s in range(2):
        per_half = []
        for half in range(2):
            row = cluster_rows[s : s + 1, half * LANES : (half + 1) * LANES]
            row = jnp.broadcast_to(row, (8, LANES))
            rows = [(iota((8, LANES), 0) + 8 * n == row).astype(f32) for n in range(2)]
            per_half.append((rows, [row == c for c in range(16)]))
        masks.append(per_half)
    return masks


def points_kernel(
    owner_ref,
    damp_ref,
    jac_hbm,
    jp_hbm,
    res_hbm,
    cam_hbm,
    count_hbm,
    clus_hbm,
    prev_hbm,
    send_ref,
    proj_ref,
    fact_ref,
    jm_ref,
    dots,
    packed,
    jac_ref,
    jp_ref,
    res_ref,
    cam_ref,
    count_ref,
    clus_ref,
    prev_ref,
    arrived,
):
    pairs = [
        (clus_hbm, clus_ref),
        (count_hbm, count_ref),
        (jp_hbm, jp_ref),
        (res_hbm, res_ref),
        (cam_hbm, cam_ref),
        (prev_hbm, prev_ref),
        (jac_hbm, jac_ref),
    ]
    copies = [
        pltpu.make_async_copy(source, target, arrived.at[n])
        for n, (source, target) in enumerate(pairs)
    ]
    for copy in copies:
        copy.start()
    for copy in copies:
        copy.wait()
    npts = 2 * LANES
    for m in range(2):
        jm_ref[m] = jac_ref[:, m, :]
    clus = clus_ref[...]
    dest = jnp.zeros_like(clus)
    for c in range(16):
        dest = jnp.where(clus == c, owner_ref[c], dest)
    slot_row = iota((8, npts), 0) % 4
    live = jnp.concatenate(
        [(slot_row < count_ref[s : s + 1, :]).astype(f32) for s in range(2)], axis=0
    )

    def by_slot(ref, step, first):
        rows = [
            ref[step * (4 * s + k) + first, m : m + 1, :]
            for s in range(2)
            for m in range(2)
            for k in range(SLOTS)
        ]
        return jnp.concatenate(rows, axis=0) * live

    jp = [by_slot(jp_ref, 3, a) for a in range(3)]
    res = by_slot(res_ref, 1, 0)

    def total(value):
        return jnp.sum(value, axis=0, keepdims=True)

    damp = damp_ref[0]
    inv1 = 1.0 / jnp.sqrt(total(jp[0] * jp[0]) + damp)
    l21 = total(jp[1] * jp[0]) * inv1
    l31 = total(jp[2] * jp[0]) * inv1
    inv2 = 1.0 / jnp.sqrt(total(jp[1] * jp[1]) + damp - l21 * l21)
    l32 = (total(jp[2] * jp[1]) - l31 * l21) * inv2
    inv3 = 1.0 / jnp.sqrt(total(jp[2] * jp[2]) + damp - l31 * l31 - l32 * l32)
    p1 = jp[0] * inv1
    p2 = (jp[1] - l21 * p1) * inv2
    p3 = (jp[2] - l31 * p1 - l32 * p2) * inv3
    proj = [p1, p2, p3]
    grad = [total(jp[a] * res) for a in range(3)]
    h1 = grad[0] * inv1
    h2 = (grad[1] - l21 * h1) * inv2
    h3 = (grad[2] - l31 * h1 - l32 * h2) * inv3
    h = [h1, h2, h3]
    for a in range(3):
        proj_ref[a] = proj[a]
    for n, row in enumerate([inv1, inv2, inv3, l21, l31, l32, h1, h2, h3]):
        fact_ref[n : n + 1, :] = row

    masks = cluster_masks(clus)
    table = [prev_ref[pl.ds(c, 8, stride=16), :] for c in range(16)]
    last = [prev_ref[128:136, :], prev_ref[136:144, :]]
    lookup_dot(table, last, masks, cam_ref, jm_ref, dots)
    dot_all = dots[...]
    wt = -res
    for a in range(3):
        terms = proj[a] * dot_all
        carried = [jnp.sum(terms[8 * s : 8 * s + 8], axis=0, keepdims=True) for s in range(2)]
        mixed = jnp.concatenate(
            [jnp.broadcast_to(h[a] + carried[1 - s], (8, npts)) for s in range(2)], axis=0
        )
        wt = wt + proj[a] * mixed

    for s in range(2):
        cols = slice(s * npts, (s + 1) * npts)
        for m in range(2):
            base = m * PACK
            for k in range(SLOTS):
                on = live[s * 8 + m * 4 + k : s * 8 + m * 4 + k + 1, :]
                packed[base + 9 * k : base + 9 * k + 9, cols] = (
                    jm_ref[m, 36 * s + 9 * k : 36 * s + 9 * k + 9, :] * on
                )
            rows = slice(s * 8 + m * 4, s * 8 + m * 4 + 4)
            for a in range(3):
                packed[base + 36 + 4 * a : base + 40 + 4 * a, cols] = proj[a][rows]
            packed[base + 48 : base + 52, cols] = wt[rows]
            packed[base + 52 : base + 53, cols] = cam_ref[s, 0:1, :].astype(f32)
            packed[base + 53 : base + 56, cols] = jnp.zeros((3, npts), f32)

    dest_row = jnp.concatenate([dest[0:1], dest[1:2]], axis=1)
    hot = (iota((16, 2 * npts), 0) == dest_row).astype(f32)
    before = (iota((2 * npts, 2 * npts), 1) < iota((2 * npts, 2 * npts), 0)).astype(bf16)
    earlier = dot_nt(hot.astype(bf16), before)
    place = jnp.sum(earlier * hot, axis=0, keepdims=True)
    slot = dest_row * 64 + place.astype(jnp.int32)
    parts = split3(packed[...])
    left = jnp.concatenate(parts, axis=0)
    low_half = iota((PACK, LANES), 1) < 64
    for pair in range(8):
        slots = iota((LANES, 2 * npts), 0) + pair * LANES
        pick = (slots == slot).astype(f32).astype(bf16)
        got = dot_nt(left, pick)
        full = got[0 : 2 * PACK] + got[2 * PACK : 4 * PACK] + got[4 * PACK : 6 * PACK]
        first = full[0:PACK]
        second = full[PACK : 2 * PACK]
        first_r = pltpu.roll(first, 64, 1)
        second_r = pltpu.roll(second, 64, 1)
        send_ref[2 * pair] = jnp.where(low_half, first, second_r)
        send_ref[2 * pair + 1] = jnp.where(low_half, first_r, second)


def band_kernel(core_ref, recv_ref, keep_ref, give_ref, rows, wide, hots):
    low_half = iota((8, LANES), 1) < 64
    quant = [[], []]
    for r in range(53):
        even = recv_ref[pl.ds(r, 8, stride=2 * PACK), :]
        odd = recv_ref[pl.ds(PACK + r, 8, stride=2 * PACK), :]
        even_r = pltpu.roll(even, 64, 1)
        odd_r = pltpu.roll(odd, 64, 1)
        quant[0].append(jnp.where(low_half, even, odd_r))
        quant[1].append(jnp.where(low_half, even_r, odd))

    def jac(k, m, i):
        return quant[m][9 * k + i]

    def proj(k, m, a):
        return quant[m][36 + 4 * a + k]

    def wt(k, m):
        return quant[m][48 + k]

    cam = quant[0][52].astype(jnp.int32)
    camera_of = 4 * (iota((LANES, LANES), 0) % GROUPS) + iota((LANES, LANES), 0) // GROUPS
    for b in range(8):
        cam_b = jnp.broadcast_to(cam[b : b + 1, :], (LANES, LANES))
        for k in range(SLOTS):
            hots[k, :, b * LANES : (b + 1) * LANES] = (
                (camera_of == (cam_b + k) % LANES).astype(f32).astype(bf16)
            )

    sizes = [304, 224, 144, 64]
    starts = [0, 304, 528, 672]
    out = None
    for k in range(SLOTS):
        count = 0

        def put(row, value, k=k):
            at = 8 * (starts[k] + row)
            rows[at : at + 8, :] = value

        for dist in range(SLOTS - k):
            other = k + dist
            mix = [[None, None], [None, None]]
            for m in range(2):
                for n in range(2):
                    if dist == 0 and n < m:
                        mix[m][n] = mix[n][m]
                        continue
                    acc = proj(k, m, 0) * proj(other, n, 0)
                    acc = acc + proj(k, m, 1) * proj(other, n, 1)
                    acc = acc + proj(k, m, 2) * proj(other, n, 2)
                    same = dist == 0 and m == n
                    mix[m][n] = (1.0 - acc) if same else -acc
            for j in range(PARAMS):
                left = [
                    mix[m][0] * jac(other, 0, j) + mix[m][1] * jac(other, 1, j) for m in range(2)
                ]
                for i in range(PARAMS):
                    if dist == 0 and i > j:
                        continue
                    value = jac(k, 0, i) * left[0] + jac(k, 1, i) * left[1]
                    if dist == 0:
                        row = i * 9 - i * (i - 1) // 2 + (j - i)
                    else:
                        row = ROW_D[dist] + i * 9 + j
                    put(row, value)
                    count += 1
        for i in range(PARAMS):
            put(ROW_Q + i, jac(k, 0, i) * wt(k, 0) + jac(k, 1, i) * wt(k, 1))
            count += 1
        size = sizes[k]
        for row in range(count, size):
            put(row, jnp.zeros((8, LANES), f32))
        for b in range(8):
            piece = rows[pl.ds(8 * starts[k] + b, size, stride=8), :]
            for n, part in enumerate(split3(piece)):
                wide[n, starts[k] : starts[k] + size, b * LANES : (b + 1) * LANES] = part
        hot = hots[k]
        got = dot_nt(wide[0, starts[k] : starts[k] + size, :], hot)
        got = got + dot_nt(wide[1, starts[k] : starts[k] + size, :], hot)
        got = got + dot_nt(wide[2, starts[k] : starts[k] + size, :], hot)
        if out is None:
            out = got
        else:
            out = jnp.concatenate([out[0:size] + got, out[size:]], axis=0)
    core = core_ref[0]
    low, high = out[0:HALF], out[HALF:BAND]
    keep_ref[...] = jnp.where(core == 0, low, high)
    give_ref[...] = jnp.where(core == 0, high, low)


def factor(size, diag, side, side_chunks):
    chunks = len(diag[0])
    inverse = []
    for k in range(size):
        pivot = spread_row(diag[k][k // 8], k % 8)
        root = lax.rsqrt(pivot)
        root = root * (1.5 - 0.5 * pivot * root * root)
        inverse.append(root)
        for v in range(k // 8, chunks):
            diag[k][v] = diag[k][v] * root
        for e in side_chunks:
            side[k][e] = side[k][e] * root
        for r in range(k + 1, size):
            coef = spread_row(diag[k][r // 8], r % 8)
            for v in range(r // 8, chunks):
                diag[r][v] = diag[r][v] - coef * diag[k][v]
            for e in side_chunks:
                side[r][e] = side[r][e] - coef * side[k][e]
    return inverse


def schur(size, side, lane):
    within = lane % GROUPS
    results = []
    for which in range(2):
        full = []
        for r in range(size):
            full.append(
                [
                    lanes_from(side[r][v % 2], within + GROUPS * (2 * which + v // 2))
                    for v in range(4)
                ]
            )
        per_a = []
        for a in range(UNK):
            acc = [None, None]
            for r in range(size):
                coef = spread_row(full[r][a // 8], a % 8)
                for e in range(2):
                    term = coef * side[r][e]
                    acc[e] = term if acc[e] is None else acc[e] + term
            per_a.append(acc)
        results.append(per_a)
    return results


def apply_schur(left, right, diag, side, lane, down, up, keep):
    within = lane % GROUPS
    part = lane // GROUPS
    from_down = (within - down + GROUPS) % GROUPS
    from_up = (within + up) % GROUPS
    pack_down = part * GROUPS + from_down
    pack_up = part * GROUPS + from_up
    is_left = part < 2
    is_rhs = jnp.logical_and(part == 1, iota((8, LANES), 0) == 3)
    for a in range(UNK):
        fresh = []
        for e in range(2):
            by_down = lanes_from(right[a][e], pack_down)
            by_up = lanes_from(left[a][e], pack_up)
            new = -jnp.where(is_left, by_down, by_up)
            if keep:
                new = new + side[a][e]
                if e == 1:
                    new = new - jnp.where(is_rhs, by_up, 0.0)
            elif e == 1:
                new = new + jnp.where(is_rhs, side[a][e] - by_up, 0.0)
            fresh.append(new)
        for v in range(a // 8, 4):
            own = lanes_from(right[a][v % 2], from_down + GROUPS * (2 + v // 2))
            other = lanes_from(left[a][v % 2], from_up + GROUPS * (v // 2))
            diag[a][v] = diag[a][v] - own - other
        side[a] = fresh


def solve_kernel(
    core_ref, damp_ref, mine_ref, other_ref, step_ref, cast_ref, rep, back, dmat, lmat, umat, smat, xrow, d0, l0, u0
):
    lane = iota((8, LANES), 1)
    within = lane % GROUPS
    part = lane // GROUPS
    core = core_ref[0]
    low = jnp.where(core == 0, mine_ref[...], other_ref[...])
    high = jnp.where(core == 0, other_ref[...], mine_ref[...])
    row = iota((HALF, LANES), 0)
    on_diag = row < 0
    for i in range(PARAMS):
        on_diag = jnp.logical_or(on_diag, row == i * 9 - i * (i - 1) // 2)
    low = low + jnp.where(on_diag, damp_ref[0], 0.0)
    first_rows = HALF // 8
    for n in range(BAND // 8):
        chunk = low[8 * n : 8 * n + 8] if n < first_rows else high[8 * n - HALF : 8 * n - HALF + 8]
        for r in range(4):
            rep[r, 8 * n : 8 * n + 8, :] = lanes_from(chunk, within + GROUPS * r)
            if r > 0:
                back[r - 1, 8 * n : 8 * n + 8, :] = lanes_from(
                    chunk, (within + GROUPS - 1) % GROUPS + GROUPS * r
                )
    zero = jnp.zeros((UNK, 32, LANES), f32)
    dmat[...] = zero
    lmat[...] = zero
    umat[...] = zero
    d0[...] = jnp.zeros_like(d0)
    l0[...] = jnp.zeros_like(l0)
    u0[...] = jnp.zeros_like(u0)

    def tri(i):
        return i * 9 - i * (i - 1) // 2

    for i in range(PARAMS):
        d0[i, i:9, :] = rep[0, tri(i) : tri(i) + 9 - i, :]
        for d in range(1, 4):
            u0[i, 9 * d - 9 : 9 * d, :] = rep[0, ROW_D[d] + 9 * i : ROW_D[d] + 9 * i + 9, :]
            l0[i, 27 - 9 * d : 36 - 9 * d, :] = back[3 - d, pl.ds(ROW_D[d] + i, 9, stride=9), :]
        l0[i, 27:28, :] = rep[0, ROW_Q + i : ROW_Q + i + 1, :]
        for r in range(1, 4):
            row = 9 * r - 9 + i
            dmat[row, row : 9 * r, :] = rep[r, tri(i) : tri(i) + 9 - i, :]
            for q in range(r + 1, 4):
                base = ROW_D[q - r] + 9 * i
                dmat[row, 9 * q - 9 : 9 * q, :] = rep[r, base : base + 9, :]
            for q in range(1, 4):
                if q < r:
                    base = ROW_D[4 + q - r] + 9 * i
                    umat[row, 9 * q - 9 : 9 * q, :] = rep[r, base : base + 9, :]
                if q > r:
                    base = ROW_D[4 + r - q] + i
                    lmat[row, 9 * q - 9 : 9 * q, :] = back[q - 1, pl.ds(base, 9, stride=9), :]
            lmat[row, 27:28, :] = rep[r, ROW_Q + i : ROW_Q + i + 1, :]

    def pack(lm, um):
        return [
            jnp.where(
                part == 0,
                lm[8 * e : 8 * e + 8],
                jnp.where(
                    part == 1,
                    lm[16 + 8 * e : 24 + 8 * e],
                    jnp.where(part == 2, um[8 * e : 8 * e + 8], um[16 + 8 * e : 24 + 8 * e]),
                ),
            )
            for e in range(2)
        ]

    def chunked(value, count):
        return [value[8 * v : 8 * v + 8] for v in range(count)]

    diag0 = [chunked(d0[i], 2) for i in range(PARAMS)]
    side0 = [pack(l0[i], u0[i]) for i in range(PARAMS)]
    inv0 = factor(PARAMS, diag0, side0, (0, 1))
    left, right = schur(PARAMS, side0, lane)
    diag = [chunked(dmat[a], 4) for a in range(UNK)]
    side = [pack(lmat[a], umat[a]) for a in range(UNK)]
    apply_schur(left, right, diag, side, lane, 0, 1, True)
    for a in range(UNK):
        for v in range(4):
            dmat[a, 8 * v : 8 * v + 8, :] = diag[a][v]
        for e in range(2):
            smat[a, 8 * e : 8 * e + 8, :] = side[a][e]

    def level(step, carry):
        stride = lax.shift_left(jnp.int32(1), step)
        diag_in = [chunked(dmat[a], 4) for a in range(UNK)]
        side_in = [chunked(smat[a], 2) for a in range(UNK)]
        diag = [list(row) for row in diag_in]
        side = [list(row) for row in side_in]
        factor(UNK, diag, side, (0, 1))
        left, right = schur(UNK, side, lane)
        diag = [list(row) for row in diag_in]
        side = [list(row) for row in side_in]
        apply_schur(left, right, diag, side, lane, stride, stride, False)
        for a in range(UNK):
            for v in range(4):
                dmat[a, 8 * v : 8 * v + 8, :] = diag[a][v]
            for e in range(2):
                smat[a, 8 * e : 8 * e + 8, :] = side[a][e]
        return carry

    lax.fori_loop(0, 5, level, jnp.int32(0))

    diag = [chunked(dmat[a], 4) for a in range(UNK)]
    side = [chunked(smat[a], 2) for a in range(UNK)]
    for a in range(UNK):
        for v in range(a // 8, 4):
            from_l = lanes_from(side[a][v % 2], within + GROUPS * (v // 2))
            from_u = lanes_from(side[a][v % 2], within + GROUPS * (2 + v // 2))
            diag[a][v] = diag[a][v] + from_l + from_u
    inverse = factor(UNK, diag, side, (1,))
    todo = [spread_row(lanes_from(side[a][1], within + GROUPS), 3) for a in range(UNK)]
    value = [None] * UNK
    for k in range(UNK - 1, -1, -1):
        value[k] = todo[k] * inverse[k]
        for r in range(k):
            todo[r] = todo[r] - spread_row(diag[r][k // 8], k % 8) * value[k]
    for a in range(UNK):
        xrow[a : a + 1, :] = value[a][0:1]
    xrow[UNK:32, :] = jnp.zeros((5, LANES), f32)
    own = chunked(xrow[...], 4)
    prev = [lanes_from(c, (lane + LANES - 1) % LANES) for c in own]
    both = pack(jnp.concatenate(prev, axis=0), jnp.concatenate(own, axis=0))
    todo0 = []
    for i in range(PARAMS):
        terms = side0[i][0] * both[0] + side0[i][1] * both[1]
        terms = terms + pltpu.roll(terms, 64, 1)
        terms = terms + pltpu.roll(terms, 32, 1)
        rhs = spread_row(lanes_from(side0[i][1], within + GROUPS), 3)
        summed = jnp.broadcast_to(jnp.sum(terms, axis=0, keepdims=True), (8, LANES))
        todo0.append(rhs - summed)
    value0 = [None] * PARAMS
    for k in range(PARAMS - 1, -1, -1):
        value0[k] = todo0[k] * inv0[k]
        for r in range(k):
            todo0[r] = todo0[r] - spread_row(diag0[r][k // 8], k % 8) * value0[k]
    camera = (lane % 4) * GROUPS + lane // 4
    for i in range(PARAMS):
        row = jnp.where(
            part == 0,
            value0[i],
            jnp.where(part == 1, value[i], jnp.where(part == 2, value[9 + i], value[18 + i])),
        )
        step_ref[i : i + 1, :] = lanes_from(row, camera)[0:1]
    for dest in range(16):
        cast_ref[dest, 0:PARAMS, :] = step_ref[...]
        cast_ref[dest, PARAMS:16, :] = jnp.zeros((16 - PARAMS, LANES), f32)


def update_kernel(owner_ref, all_ref, jac_ref, proj_ref, fact_ref, cam_ref, clus_ref, out_ref, dots):
    clus = clus_ref[...]
    dest = jnp.zeros_like(clus)
    for c in range(16):
        dest = jnp.where(clus == c, owner_ref[c], dest)
    masks = cluster_masks(dest)
    table = [all_ref[16 * c : 16 * c + 8, :] for c in range(16)]
    last = [all_ref[pl.ds(8, 8, stride=16), :], all_ref[pl.ds(136, 8, stride=16), :]]
    lookup_dot(table, last, masks, cam_ref, jac_ref, dots)
    dot_all = dots[...]

    def fact(n):
        return fact_ref[n : n + 1, :]

    tot = [fact(6 + a) + jnp.sum(proj_ref[a] * dot_all, axis=0, keepdims=True) for a in range(3)]
    x3 = tot[2] * fact(2)
    x2 = (tot[1] - fact(5) * x3) * fact(1)
    x1 = (tot[0] - fact(3) * x2 - fact(4) * x3) * fact(0)
    out_ref[0:1, :] = -x1
    out_ref[1:2, :] = -x2
    out_ref[2:3, :] = -x3


def smem():
    return pl.BlockSpec(memory_space=pltpu.SMEM)


def vmem():
    return pl.BlockSpec(memory_space=pltpu.VMEM)


def params(mib):
    return pltpu.CompilerParams(vmem_limit_bytes=mib * MIB)


def run_points(owner_map, damping, jac, jp, res, cam_ids, obs_count, clus, prev):
    npts = 256
    return pl.pallas_call(
        points_kernel,
        out_shape=(
            jax.ShapeDtypeStruct((16, PACK, LANES), f32),
            jax.ShapeDtypeStruct((3, 16, npts), f32),
            jax.ShapeDtypeStruct((9, npts), f32),
            jax.ShapeDtypeStruct((2, 8 * PARAMS, npts), f32),
        ),
        in_specs=[smem(), smem()] + [pl.BlockSpec(memory_space=pltpu.HBM)] * 7,
        out_specs=(vmem(), vmem(), vmem(), vmem()),
        scratch_shapes=[
            pltpu.VMEM((16, npts), f32),
            pltpu.VMEM((2 * PACK, 2 * npts), f32),
            pltpu.VMEM(jac.shape, f32),
            pltpu.VMEM(jp.shape, f32),
            pltpu.VMEM(res.shape, f32),
            pltpu.VMEM(cam_ids.shape, jnp.int32),
            pltpu.VMEM(obs_count.shape, jnp.int32),
            pltpu.VMEM(clus.shape, jnp.int32),
            pltpu.VMEM(prev.shape, f32),
            pltpu.SemaphoreType.DMA((7,)),
        ],
        compiler_params=params(58),
        name="points",
    )(owner_map, damping, jac, jp, res, cam_ids, obs_count, clus, prev)


def run_band(core, recv):
    return pl.pallas_call(
        band_kernel,
        out_shape=(
            jax.ShapeDtypeStruct((HALF, LANES), f32),
            jax.ShapeDtypeStruct((HALF, LANES), f32),
        ),
        in_specs=[smem(), vmem()],
        out_specs=(vmem(), vmem()),
        scratch_shapes=[
            pltpu.VMEM((736 * 8, LANES), f32),
            pltpu.VMEM((3, 736, 1024), bf16),
            pltpu.VMEM((4, LANES, 1024), bf16),
        ],
        compiler_params=params(20),
        name="band",
    )(core, recv)


def run_solve(core, damping, mine, other):
    return pl.pallas_call(
        solve_kernel,
        out_shape=(
            jax.ShapeDtypeStruct((PARAMS, LANES), f32),
            jax.ShapeDtypeStruct((16, 16, LANES), f32),
        ),
        in_specs=[smem(), smem(), vmem(), vmem()],
        out_specs=(vmem(), vmem()),
        scratch_shapes=[
            pltpu.VMEM((4, BAND, LANES), f32),
            pltpu.VMEM((3, BAND, LANES), f32),
            pltpu.VMEM((UNK, 32, LANES), f32),
            pltpu.VMEM((UNK, 32, LANES), f32),
            pltpu.VMEM((UNK, 32, LANES), f32),
            pltpu.VMEM((UNK, 16, LANES), f32),
            pltpu.VMEM((32, LANES), f32),
            pltpu.VMEM((PARAMS, 16, LANES), f32),
            pltpu.VMEM((PARAMS, 32, LANES), f32),
            pltpu.VMEM((PARAMS, 32, LANES), f32),
        ],
        compiler_params=params(12),
        name="solve",
    )(core, damping, mine, other)


def run_update(owner_map, everything, jac, proj, fact, cam_ids, clus):
    return pl.pallas_call(
        update_kernel,
        out_shape=jax.ShapeDtypeStruct((3, 256), f32),
        in_specs=[smem()] + [vmem()] * 6,
        out_specs=vmem(),
        scratch_shapes=[pltpu.VMEM((16, 256), f32)],
        compiler_params=params(8),
        name="update",
    )(owner_map, everything, jac, proj, fact, cam_ids, clus)


def sum_over_points(keep, give, ring):
    swap = [(i, i ^ 1) for i in range(ring)]
    half = keep + lax.ppermute(give, "pt", swap)
    moved = [lax.ppermute(half, "pt", [(i, i ^ (2 * d)) for i in range(ring)]) for d in (1, 2, 3)]
    mine = (half + moved[0]) + (moved[1] + moved[2])
    return mine, lax.ppermute(mine, "pt", swap)


def per_device(
    cam_jac, pt_jac, residual, cam_ids, obs_count, clusters, owner_map, prev_step, damping
):
    npts = cam_jac.shape[-1]
    core = (lax.axis_index("pt") % 2).astype(jnp.int32).reshape(1)
    send, proj, fact, jac = run_points(
        owner_map,
        damping,
        cam_jac.transpose(0, 1, 3, 2, 4).reshape(8 * PARAMS, 2, npts),
        pt_jac.transpose(0, 1, 3, 2, 4).reshape(24, 2, npts),
        residual.reshape(8, 2, npts),
        cam_ids,
        obs_count,
        clusters.T,
        prev_step.transpose(1, 0, 2).reshape(PARAMS * 16, LANES),
    )
    recv = lax.all_to_all(send, "cl", split_axis=0, concat_axis=0, tiled=True)
    keep, give = run_band(core, recv.reshape(16 * PACK, LANES))
    mine, other = sum_over_points(keep, give, lax.axis_size("pt"))
    step, cast = run_solve(core, damping, mine, other)
    everything = lax.all_to_all(cast, "cl", split_axis=0, concat_axis=0, tiled=True)
    point_step = run_update(
        owner_map, everything.reshape(256, LANES), jac, proj, fact, cam_ids, clusters.T
    )
    return (step[None], point_step)


def solution(mesh):
    in_specs = (
        P(None, None, None, None, ("pt", "cl")),
        P(None, None, None, None, ("pt", "cl")),
        P(None, None, None, ("pt", "cl")),
        P(None, None, ("pt", "cl")),
        P(None, ("pt", "cl")),
        P(("pt", "cl"), None),
        P(),
        P(),
        P(),
    )
    out_specs = (P("cl", None, None), P(None, ("pt", "cl")))
    return jax.shard_map(
        per_device, mesh=mesh, in_specs=in_specs, out_specs=out_specs, check_vma=False
    )
```

```python
import jax
import jax.numpy as jnp
from jax import lax
from jax.experimental import pallas as pl
from jax.experimental.pallas import tpu as pltpu
from jax.sharding import PartitionSpec as P

f32 = jnp.float32
bf16 = jnp.bfloat16
LANES = 128
SLOTS = 4
PARAMS = 9
GROUPS = 32
BLOCK = 9
UNK = 27
ROW_Q = 45
ROW_D = (0, 54, 135, 216)
ROW_END = (54, 135, 216, 297)
NEEDED = ({0, 1, 2, 3}, {0, 1, 2}, {0, 1, 3}, {0, 2, 3})
BAND = 304
HALF = BAND // 2
PACK = 56
MIB = 1024 * 1024


def split3(value):
    high = value.astype(bf16)
    rest = value - high.astype(f32)
    mid = rest.astype(bf16)
    low = (rest - mid.astype(f32)).astype(bf16)
    return high, mid, low


def dot_nt(left, right):
    return lax.dot_general(left, right, (((1,), (1,)), ((), ())), preferred_element_type=f32)


def iota(shape, dim):
    return lax.broadcasted_iota(jnp.int32, shape, dim)


def lanes_from(value, index):
    return jnp.take_along_axis(value, index, axis=1)


def spread_row(chunk, row):
    return jnp.broadcast_to(chunk[row : row + 1, :], (8, LANES))


def lookup_dot(table, last, masks, cam_ref, jac_ref, out_ref):
    for half in range(2):
        cols = slice(half * LANES, (half + 1) * LANES)
        for s in range(2):
            rows, picks = masks[s][half]
            for k in range(SLOTS):
                index = jnp.broadcast_to(cam_ref[s, k : k + 1, cols], (8, LANES))
                chosen = lanes_from(table[0], index)
                for c in range(1, 16):
                    chosen = jnp.where(picks[c], lanes_from(table[c], index), chosen)
                ninth = lanes_from(last[0], index) * rows[0] + lanes_from(last[1], index) * rows[1]
                for m in range(2):
                    base = s * SLOTS * PARAMS + k * PARAMS
                    terms = chosen * jac_ref[m, base : base + 8, cols]
                    terms = terms + ninth * jac_ref[m, base + 8 : base + 9, cols]
                    row = s * 8 + m * 4 + k
                    out_ref[row : row + 1, cols] = jnp.sum(terms, axis=0, keepdims=True)


def cluster_masks(cluster_rows):
    masks = []
    for s in range(2):
        per_half = []
        for half in range(2):
            row = cluster_rows[s : s + 1, half * LANES : (half + 1) * LANES]
            row = jnp.broadcast_to(row, (8, LANES))
            rows = [(iota((8, LANES), 0) + 8 * n == row).astype(f32) for n in range(2)]
            per_half.append((rows, [row == c for c in range(16)]))
        masks.append(per_half)
    return masks


def points_kernel(
    owner_ref,
    damp_ref,
    jac_hbm,
    jp_hbm,
    res_hbm,
    cam_hbm,
    count_hbm,
    clus_hbm,
    prev_hbm,
    send_ref,
    proj_ref,
    fact_ref,
    jm_ref,
    where_ref,
    dest_ref,
    dots,
    packed,
    jac_ref,
    jp_ref,
    res_ref,
    cam_ref,
    count_ref,
    clus_ref,
    prev_ref,
    arrived,
):
    pairs = [
        (clus_hbm, clus_ref),
        (count_hbm, count_ref),
        (jp_hbm, jp_ref),
        (res_hbm, res_ref),
        (cam_hbm, cam_ref),
        (prev_hbm, prev_ref),
        (jac_hbm, jac_ref),
    ]
    copies = [
        pltpu.make_async_copy(source, target, arrived.at[n])
        for n, (source, target) in enumerate(pairs)
    ]
    for copy in copies:
        copy.start()
    for copy in copies:
        copy.wait()
    npts = 2 * LANES
    for m in range(2):
        jm_ref[m] = jac_ref[:, m, :]
    clus = clus_ref[...]
    dest = jnp.zeros_like(clus)
    for c in range(16):
        dest = jnp.where(clus == c, owner_ref[c], dest)
    dest_ref[...] = dest
    where_ref[...] = cam_ref[...]
    slot_row = iota((8, npts), 0) % 4
    live = jnp.concatenate(
        [(slot_row < count_ref[s : s + 1, :]).astype(f32) for s in range(2)], axis=0
    )

    def by_slot(ref, step, first):
        rows = [
            ref[step * (4 * s + k) + first, m : m + 1, :]
            for s in range(2)
            for m in range(2)
            for k in range(SLOTS)
        ]
        return jnp.concatenate(rows, axis=0) * live

    jp = [by_slot(jp_ref, 3, a) for a in range(3)]
    res = by_slot(res_ref, 1, 0)

    def total(value):
        return jnp.sum(value, axis=0, keepdims=True)

    damp = damp_ref[0]
    inv1 = 1.0 / jnp.sqrt(total(jp[0] * jp[0]) + damp)
    l21 = total(jp[1] * jp[0]) * inv1
    l31 = total(jp[2] * jp[0]) * inv1
    inv2 = 1.0 / jnp.sqrt(total(jp[1] * jp[1]) + damp - l21 * l21)
    l32 = (total(jp[2] * jp[1]) - l31 * l21) * inv2
    inv3 = 1.0 / jnp.sqrt(total(jp[2] * jp[2]) + damp - l31 * l31 - l32 * l32)
    p1 = jp[0] * inv1
    p2 = (jp[1] - l21 * p1) * inv2
    p3 = (jp[2] - l31 * p1 - l32 * p2) * inv3
    proj = [p1, p2, p3]
    grad = [total(jp[a] * res) for a in range(3)]
    h1 = grad[0] * inv1
    h2 = (grad[1] - l21 * h1) * inv2
    h3 = (grad[2] - l31 * h1 - l32 * h2) * inv3
    h = [h1, h2, h3]
    for a in range(3):
        proj_ref[a] = proj[a]
    for n, row in enumerate([inv1, inv2, inv3, l21, l31, l32, h1, h2, h3]):
        fact_ref[n : n + 1, :] = row

    masks = cluster_masks(clus)
    table = [prev_ref[pl.ds(c, 8, stride=16), :] for c in range(16)]
    last = [prev_ref[128:136, :], prev_ref[136:144, :]]
    lookup_dot(table, last, masks, cam_ref, jm_ref, dots)
    dot_all = dots[...]
    wt = -res
    for a in range(3):
        terms = proj[a] * dot_all
        carried = [jnp.sum(terms[8 * s : 8 * s + 8], axis=0, keepdims=True) for s in range(2)]
        mixed = jnp.concatenate(
            [jnp.broadcast_to(h[a] + carried[1 - s], (8, npts)) for s in range(2)], axis=0
        )
        wt = wt + proj[a] * mixed

    for s in range(2):
        cols = slice(s * npts, (s + 1) * npts)
        for m in range(2):
            base = m * PACK
            for k in range(SLOTS):
                on = live[s * 8 + m * 4 + k : s * 8 + m * 4 + k + 1, :]
                packed[base + 9 * k : base + 9 * k + 9, cols] = (
                    jm_ref[m, 36 * s + 9 * k : 36 * s + 9 * k + 9, :] * on
                )
            rows = slice(s * 8 + m * 4, s * 8 + m * 4 + 4)
            for a in range(3):
                packed[base + 36 + 4 * a : base + 40 + 4 * a, cols] = proj[a][rows]
            packed[base + 48 : base + 52, cols] = wt[rows]
            packed[base + 52 : base + 53, cols] = cam_ref[s, 0:1, :].astype(f32)
            packed[base + 53 : base + 56, cols] = jnp.zeros((3, npts), f32)

    dest_row = jnp.concatenate([dest[0:1], dest[1:2]], axis=1)
    hot = (iota((16, 2 * npts), 0) == dest_row).astype(f32)
    before = (iota((2 * npts, 2 * npts), 1) < iota((2 * npts, 2 * npts), 0)).astype(bf16)
    earlier = dot_nt(hot.astype(bf16), before)
    place = jnp.sum(earlier * hot, axis=0, keepdims=True)
    slot = dest_row * 64 + place.astype(jnp.int32)
    parts = split3(packed[...])
    left = jnp.concatenate(parts, axis=0)
    low_half = iota((PACK, LANES), 1) < 64
    for quad in range(4):
        slots = iota((2 * LANES, 2 * npts), 0) + quad * 2 * LANES
        pick = (slots == slot).astype(f32).astype(bf16)
        got = dot_nt(left, pick)
        full = got[0 : 2 * PACK] + got[2 * PACK : 4 * PACK] + got[4 * PACK : 6 * PACK]
        for pair in range(2):
            cols = slice(pair * LANES, (pair + 1) * LANES)
            first = full[0:PACK, cols]
            second = full[PACK : 2 * PACK, cols]
            first_r = pltpu.roll(first, 64, 1)
            second_r = pltpu.roll(second, 64, 1)
            send_ref[4 * quad + 2 * pair] = jnp.where(low_half, first, second_r)
            send_ref[4 * quad + 2 * pair + 1] = jnp.where(low_half, first_r, second)


def band_kernel(core_ref, recv_ref, keep_ref, give_ref, rows, wide, hots):
    low_half = iota((8, LANES), 1) < 64
    quant = [[], []]
    for r in range(53):
        even = recv_ref[pl.ds(r, 8, stride=2 * PACK), :]
        odd = recv_ref[pl.ds(PACK + r, 8, stride=2 * PACK), :]
        even_r = pltpu.roll(even, 64, 1)
        odd_r = pltpu.roll(odd, 64, 1)
        quant[0].append(jnp.where(low_half, even, odd_r))
        quant[1].append(jnp.where(low_half, even_r, odd))

    def jac(k, m, i):
        return quant[m][9 * k + i]

    def proj(k, m, a):
        return quant[m][36 + 4 * a + k]

    def wt(k, m):
        return quant[m][48 + k]

    cam = quant[0][52].astype(jnp.int32)
    camera_of = 4 * (iota((LANES, LANES), 0) % GROUPS) + iota((LANES, LANES), 0) // GROUPS
    for b in range(8):
        cam_b = jnp.broadcast_to(cam[b : b + 1, :], (LANES, LANES))
        for k in range(SLOTS):
            hots[k, :, b * LANES : (b + 1) * LANES] = (
                (camera_of == (cam_b + k) % LANES).astype(f32).astype(bf16)
            )

    sizes = [304, 224, 144, 64]
    starts = [0, 304, 528, 672]
    out = None
    for k in range(SLOTS):
        count = 0

        def put(row, value, k=k):
            at = 8 * (starts[k] + row)
            rows[at : at + 8, :] = value

        for dist in range(SLOTS - k):
            other = k + dist
            mix = [[None, None], [None, None]]
            for m in range(2):
                for n in range(2):
                    if dist == 0 and n < m:
                        mix[m][n] = mix[n][m]
                        continue
                    acc = proj(k, m, 0) * proj(other, n, 0)
                    acc = acc + proj(k, m, 1) * proj(other, n, 1)
                    acc = acc + proj(k, m, 2) * proj(other, n, 2)
                    same = dist == 0 and m == n
                    mix[m][n] = (1.0 - acc) if same else -acc
            for j in range(PARAMS):
                left = [
                    mix[m][0] * jac(other, 0, j) + mix[m][1] * jac(other, 1, j) for m in range(2)
                ]
                for i in range(PARAMS):
                    if dist == 0 and i > j:
                        continue
                    value = jac(k, 0, i) * left[0] + jac(k, 1, i) * left[1]
                    if dist == 0:
                        row = i * 9 - i * (i - 1) // 2 + (j - i)
                    else:
                        row = ROW_D[dist] + i * 9 + j
                    put(row, value)
                    count += 1
        for i in range(PARAMS):
            put(ROW_Q + i, jac(k, 0, i) * wt(k, 0) + jac(k, 1, i) * wt(k, 1))
            count += 1
        size = sizes[k]
        for row in range(count, size):
            put(row, jnp.zeros((8, LANES), f32))
        for b in range(8):
            piece = rows[pl.ds(8 * starts[k] + b, size, stride=8), :]
            for n, part in enumerate(split3(piece)):
                wide[n, starts[k] : starts[k] + size, b * LANES : (b + 1) * LANES] = part
        hot = hots[k]
        got = dot_nt(wide[0, starts[k] : starts[k] + size, :], hot)
        got = got + dot_nt(wide[1, starts[k] : starts[k] + size, :], hot)
        got = got + dot_nt(wide[2, starts[k] : starts[k] + size, :], hot)
        if out is None:
            out = got
        else:
            out = jnp.concatenate([out[0:size] + got, out[size:]], axis=0)
    core = core_ref[0]
    low, high = out[0:HALF], out[HALF:BAND]
    keep_ref[...] = jnp.where(core == 0, low, high)
    give_ref[...] = jnp.where(core == 0, high, low)


def factor(size, diag, side, side_chunks):
    chunks = len(diag[0])
    inverse = []
    for k in range(size):
        pivot = spread_row(diag[k][k // 8], k % 8)
        root = lax.rsqrt(pivot)
        root = root * (1.5 - 0.5 * pivot * root * root)
        inverse.append(root)
        for v in range(k // 8, chunks):
            diag[k][v] = diag[k][v] * root
        for e in side_chunks:
            side[k][e] = side[k][e] * root
        for r in range(k + 1, size):
            coef = spread_row(diag[k][r // 8], r % 8)
            for v in range(r // 8, chunks):
                diag[r][v] = diag[r][v] - coef * diag[k][v]
            for e in side_chunks:
                side[r][e] = side[r][e] - coef * side[k][e]
    return inverse


def schur(size, side, lane, whole):
    within = lane % GROUPS
    results = []
    for which in range(2):
        for r in range(size):
            for v in range(4):
                at = 32 * (which * UNK + r) + 8 * v
                whole[at : at + 8, :] = lanes_from(
                    side[r][v % 2], within + GROUPS * (2 * which + v // 2)
                )
        per_a = [[None, None] for a in range(UNK)]
        for first in range(0, UNK, BLOCK):
            for r in range(size):
                for a in range(first, min(first + BLOCK, UNK)):
                    at = 32 * (which * UNK + r) + a
                    coef = jnp.broadcast_to(whole[at : at + 1, :], (8, LANES))
                    for e in range(2):
                        term = coef * side[r][e]
                        per_a[a][e] = term if r == 0 else per_a[a][e] + term
        results.append(per_a)
    return results


def apply_schur(left, right, diag, side, lane, down, up, keep):
    within = lane % GROUPS
    part = lane // GROUPS
    from_down = (within - down + GROUPS) % GROUPS
    from_up = (within + up) % GROUPS
    pack_down = part * GROUPS + from_down
    pack_up = part * GROUPS + from_up
    is_left = part < 2
    is_rhs = jnp.logical_and(part == 1, iota((8, LANES), 0) == 3)
    for a in range(UNK):
        fresh = []
        for e in range(2):
            by_down = lanes_from(right[a][e], pack_down)
            by_up = lanes_from(left[a][e], pack_up)
            new = -jnp.where(is_left, by_down, by_up)
            if keep:
                new = new + side[a][e]
                if e == 1:
                    new = new - jnp.where(is_rhs, by_up, 0.0)
            elif e == 1:
                new = new + jnp.where(is_rhs, side[a][e] - by_up, 0.0)
            fresh.append(new)
        for v in range(a // 8, 4):
            own = lanes_from(right[a][v % 2], from_down + GROUPS * (2 + v // 2))
            other = lanes_from(left[a][v % 2], from_up + GROUPS * (v // 2))
            diag[a][v] = diag[a][v] - own - other
        side[a] = fresh


def solve_kernel(
    core_ref, damp_ref, mine_ref, other_ref, step_ref, cast_ref, rep, back, dmat, smat, xrow, whole
):
    lane = iota((8, LANES), 1)
    sub = iota((8, LANES), 0)
    within = lane % GROUPS
    part = lane // GROUPS
    core = core_ref[0]
    low = jnp.where(core == 0, mine_ref[...], other_ref[...])
    high = jnp.where(core == 0, other_ref[...], mine_ref[...])
    row = iota((HALF, LANES), 0)
    on_diag = row < 0
    for i in range(PARAMS):
        on_diag = jnp.logical_or(on_diag, row == i * 9 - i * (i - 1) // 2)
    low = low + jnp.where(on_diag, damp_ref[0], 0.0)
    first_rows = HALF // 8
    for n in range(BAND // 8):
        chunk = low[8 * n : 8 * n + 8] if n < first_rows else high[8 * n - HALF : 8 * n - HALF + 8]
        at = slice(8 * n, 8 * n + 8)
        kinds = {d for d in range(4) if ROW_D[d] < 8 * n + 8 and 8 * n < ROW_END[d]}
        for r in range(4):
            if kinds & NEEDED[r]:
                rep[r, at, :] = lanes_from(chunk, within + GROUPS * r)
            if r > 0 and kinds & set(range(4 - r, 4)):
                back[r - 1, at, :] = lanes_from(
                    chunk, (within + GROUPS - 1) % GROUPS + GROUPS * r
                )

    def tri(i):
        return i * 9 - i * (i - 1) // 2

    def line(ref, r, start):
        return jnp.broadcast_to(ref[r, start : start + 1, :], (8, LANES))

    def tail(values):
        out = jnp.zeros((8, LANES), f32)
        for n, value in values:
            out = jnp.where(sub == n, value, out)
        return out

    def forward(r, d, i):
        start = tri(i) - i if d == 0 else ROW_D[d] + 9 * i
        return rep[r, start : start + 8, :], line(rep, r, start + 8)

    def backward(r, d, i):
        start = ROW_D[d] + i
        return back[r - 1, pl.ds(start, 8, stride=9), :], line(back, r - 1, start + 72)

    def pack(lm, um):
        return [
            jnp.where(
                part == 0,
                lm[e],
                jnp.where(part == 1, lm[2 + e], jnp.where(part == 2, um[e], um[2 + e])),
            )
            for e in range(2)
        ]

    def rhs(r, i):
        return line(rep, r, ROW_Q + i)

    def chunked(value, count):
        return [value[8 * v : 8 * v + 8] for v in range(count)]

    zero = jnp.zeros((8, LANES), f32)

    diag0, side0 = [], []
    for i in range(PARAMS):
        diag0.append(list(forward(0, 0, i)))
        after = [forward(0, d, i) for d in (1, 2, 3)]
        before = [backward(4 - d, d, i) for d in (3, 2, 1)]
        lm = [p[0] for p in before]
        lm.append(tail([(n, p[1]) for n, p in enumerate(before)] + [(3, rhs(0, i))]))
        um = [p[0] for p in after]
        um.append(tail([(n, p[1]) for n, p in enumerate(after)]))
        side0.append(pack(lm, um))
    inv0 = factor(PARAMS, diag0, side0, (0, 1))
    left, right = schur(PARAMS, side0, lane, whole)

    diag, side = [], []
    for a in range(UNK):
        r, i = (a // 8 + 1, a % 8) if a < 24 else (a - 23, 8)
        own = {q: forward(r, q - r, i) for q in range(r, 4)}
        ahead = {q: forward(r, 4 + q - r, i) for q in range(1, r)}
        behind = {q: backward(q, 4 + r - q, i) for q in range(r + 1, 4)}
        diag.append([own[q][0] if q in own else zero for q in (1, 2, 3)])
        ninths = [(q - 1, p[1]) for q, p in own.items()]
        ninths += [(q - 1, line(rep, q, ROW_D[r - q] + 72 + i)) for q in range(1, r)]
        diag[a].append(tail(ninths))
        um = [ahead[q][0] if q in ahead else zero for q in (1, 2, 3)]
        um.append(tail([(q - 1, p[1]) for q, p in ahead.items()]))
        lm = [behind[q][0] if q in behind else zero for q in (1, 2, 3)]
        lm.append(tail([(q - 1, p[1]) for q, p in behind.items()] + [(3, rhs(r, i))]))
        side.append(pack(lm, um))
    apply_schur(left, right, diag, side, lane, 0, 1, True)

    def store(diag, side):
        for a in range(UNK):
            for v in range(a // 8, 4):
                dmat[a, 8 * v : 8 * v + 8, :] = diag[a][v]
            for e in range(2):
                smat[a, 8 * e : 8 * e + 8, :] = side[a][e]

    def load():
        diag = [
            [dmat[a, 8 * v : 8 * v + 8, :] if v >= a // 8 else None for v in range(4)]
            for a in range(UNK)
        ]
        return diag, [chunked(smat[a], 2) for a in range(UNK)]

    store(diag, side)

    def level(step, carry):
        stride = lax.shift_left(jnp.int32(1), step)
        diag, side = load()
        factor(UNK, diag, side, (0, 1))
        left, right = schur(UNK, side, lane, whole)
        diag, side = load()
        apply_schur(left, right, diag, side, lane, stride, stride, False)
        store(diag, side)
        return carry

    lax.fori_loop(0, 4, level, jnp.int32(0))

    diag, side = load()
    both = []
    for a in range(UNK):
        halves = []
        for base in (0, 2 * GROUPS):
            index = within + GROUPS * (part // 2) + base
            halves.append(
                jnp.where(
                    part % 2 == 0, lanes_from(side[a][0], index), lanes_from(side[a][1], index)
                )
            )
        both.append([halves[0] + halves[1]])
        right_side = lanes_from(side[a][1], within + GROUPS)
        diag[a][3] = jnp.where(sub == 3, right_side, diag[a][3])
    work = [list(line_of) for line_of in diag]
    factor(UNK, work, both, (0,))
    full = [[lanes_from(both[r][0], within + GROUPS * v) for v in range(4)] for r in range(UNK)]
    for a in range(UNK):
        acc = None
        for r in range(UNK):
            term = spread_row(full[r][a // 8], a % 8) * both[r][0]
            acc = term if acc is None else acc + term
        for v in range(a // 8, 4):
            moved = lanes_from(acc, (within + 16) % GROUPS + GROUPS * v)
            diag[a][v] = diag[a][v] - moved
    inverse = factor(UNK, diag, both, ())
    todo = [spread_row(diag[a][3], 3) for a in range(UNK)]
    value = [None] * UNK
    for k in range(UNK - 1, -1, -1):
        value[k] = todo[k] * inverse[k]
        for r in range(k):
            todo[r] = todo[r] - spread_row(diag[r][k // 8], k % 8) * value[k]
    for a in range(UNK):
        xrow[a : a + 1, :] = value[a][0:1]
    xrow[UNK:32, :] = jnp.zeros((5, LANES), f32)
    own = chunked(xrow[...], 4)
    prev = [lanes_from(c, (lane + LANES - 1) % LANES) for c in own]
    packed = pack(prev, own)
    todo0 = []
    for i in range(PARAMS):
        terms = side0[i][0] * packed[0] + side0[i][1] * packed[1]
        terms = terms + pltpu.roll(terms, 64, 1)
        terms = terms + pltpu.roll(terms, 32, 1)
        right_side = spread_row(lanes_from(side0[i][1], within + GROUPS), 3)
        summed = jnp.broadcast_to(jnp.sum(terms, axis=0, keepdims=True), (8, LANES))
        todo0.append(right_side - summed)
    value0 = [None] * PARAMS
    for k in range(PARAMS - 1, -1, -1):
        value0[k] = todo0[k] * inv0[k]
        for r in range(k):
            todo0[r] = todo0[r] - spread_row(diag0[r][k // 8], k % 8) * value0[k]
    camera = (lane % 4) * GROUPS + lane // 4
    for i in range(PARAMS):
        near = [value[8 * r + i] if i < 8 else value[24 + r] for r in range(3)]
        mixed = jnp.where(
            part == 0,
            value0[i],
            jnp.where(part == 1, near[0], jnp.where(part == 2, near[1], near[2])),
        )
        step_ref[i : i + 1, :] = lanes_from(mixed, camera)[0:1]
    for dest in range(16):
        cast_ref[dest, 0:PARAMS, :] = step_ref[...]
        cast_ref[dest, PARAMS:16, :] = jnp.zeros((16 - PARAMS, LANES), f32)


def update_kernel(all_ref, jac_ref, proj_ref, fact_ref, cam_ref, dest_ref, out_ref, dots):
    masks = cluster_masks(dest_ref[...])
    table = [all_ref[16 * c : 16 * c + 8, :] for c in range(16)]
    last = [all_ref[pl.ds(8, 8, stride=16), :], all_ref[pl.ds(136, 8, stride=16), :]]
    lookup_dot(table, last, masks, cam_ref, jac_ref, dots)
    dot_all = dots[...]

    def fact(n):
        return fact_ref[n : n + 1, :]

    tot = [fact(6 + a) + jnp.sum(proj_ref[a] * dot_all, axis=0, keepdims=True) for a in range(3)]
    x3 = tot[2] * fact(2)
    x2 = (tot[1] - fact(5) * x3) * fact(1)
    x1 = (tot[0] - fact(3) * x2 - fact(4) * x3) * fact(0)
    out_ref[0:1, :] = -x1
    out_ref[1:2, :] = -x2
    out_ref[2:3, :] = -x3


def smem():
    return pl.BlockSpec(memory_space=pltpu.SMEM)


def vmem():
    return pl.BlockSpec(memory_space=pltpu.VMEM)


def params(mib):
    return pltpu.CompilerParams(vmem_limit_bytes=mib * MIB)


def run_points(owner_map, damping, jac, jp, res, cam_ids, obs_count, clus, prev):
    npts = 256
    return pl.pallas_call(
        points_kernel,
        out_shape=(
            jax.ShapeDtypeStruct((16, PACK, LANES), f32),
            jax.ShapeDtypeStruct((3, 16, npts), f32),
            jax.ShapeDtypeStruct((9, npts), f32),
            jax.ShapeDtypeStruct((2, 8 * PARAMS, npts), f32),
            jax.ShapeDtypeStruct(cam_ids.shape, jnp.int32),
            jax.ShapeDtypeStruct(clus.shape, jnp.int32),
        ),
        in_specs=[smem(), smem()] + [pl.BlockSpec(memory_space=pltpu.HBM)] * 7,
        out_specs=(vmem(),) * 6,
        scratch_shapes=[
            pltpu.VMEM((16, npts), f32),
            pltpu.VMEM((2 * PACK, 2 * npts), f32),
            pltpu.VMEM(jac.shape, f32),
            pltpu.VMEM(jp.shape, f32),
            pltpu.VMEM(res.shape, f32),
            pltpu.VMEM(cam_ids.shape, jnp.int32),
            pltpu.VMEM(obs_count.shape, jnp.int32),
            pltpu.VMEM(clus.shape, jnp.int32),
            pltpu.VMEM(prev.shape, f32),
            pltpu.SemaphoreType.DMA((7,)),
        ],
        compiler_params=params(58),
        name="points",
    )(owner_map, damping, jac, jp, res, cam_ids, obs_count, clus, prev)


def run_band(core, recv):
    return pl.pallas_call(
        band_kernel,
        out_shape=(
            jax.ShapeDtypeStruct((HALF, LANES), f32),
            jax.ShapeDtypeStruct((HALF, LANES), f32),
        ),
        in_specs=[smem(), vmem()],
        out_specs=(vmem(), vmem()),
        scratch_shapes=[
            pltpu.VMEM((736 * 8, LANES), f32),
            pltpu.VMEM((3, 736, 1024), bf16),
            pltpu.VMEM((4, LANES, 1024), bf16),
        ],
        compiler_params=params(20),
        name="band",
    )(core, recv)


def run_solve(core, damping, mine, other):
    return pl.pallas_call(
        solve_kernel,
        out_shape=(
            jax.ShapeDtypeStruct((PARAMS, LANES), f32),
            jax.ShapeDtypeStruct((16, 16, LANES), f32),
        ),
        in_specs=[smem(), smem(), vmem(), vmem()],
        out_specs=(vmem(), vmem()),
        scratch_shapes=[
            pltpu.VMEM((4, BAND, LANES), f32),
            pltpu.VMEM((3, BAND, LANES), f32),
            pltpu.VMEM((UNK, 32, LANES), f32),
            pltpu.VMEM((UNK, 16, LANES), f32),
            pltpu.VMEM((32, LANES), f32),
            pltpu.VMEM((2 * UNK * 32, LANES), f32),
        ],
        compiler_params=params(12),
        name="solve",
    )(core, damping, mine, other)


def run_update(everything, jac, proj, fact, where, dest):
    return pl.pallas_call(
        update_kernel,
        out_shape=jax.ShapeDtypeStruct((3, 256), f32),
        in_specs=[vmem()] * 6,
        out_specs=vmem(),
        scratch_shapes=[pltpu.VMEM((16, 256), f32)],
        compiler_params=params(8),
        name="update",
    )(everything, jac, proj, fact, where, dest)


def sum_over_points(keep, give, ring):
    swap = [(i, i ^ 1) for i in range(ring)]
    half = keep + lax.ppermute(give, "pt", swap)
    moved = [lax.ppermute(half, "pt", [(i, i ^ (2 * d)) for i in range(ring)]) for d in (1, 2, 3)]
    mine = (half + moved[0]) + (moved[1] + moved[2])
    return mine, lax.ppermute(mine, "pt", swap)


def per_device(
    cam_jac, pt_jac, residual, cam_ids, obs_count, clusters, owner_map, prev_step, damping
):
    npts = cam_jac.shape[-1]
    core = (lax.axis_index("pt") % 2).astype(jnp.int32).reshape(1)
    send, proj, fact, jac, where, dest = run_points(
        owner_map,
        damping,
        cam_jac.transpose(0, 1, 3, 2, 4).reshape(8 * PARAMS, 2, npts),
        pt_jac.transpose(0, 1, 3, 2, 4).reshape(24, 2, npts),
        residual.reshape(8, 2, npts),
        cam_ids,
        obs_count,
        clusters.T,
        prev_step.transpose(1, 0, 2).reshape(PARAMS * 16, LANES),
    )
    recv = lax.all_to_all(send, "cl", split_axis=0, concat_axis=0, tiled=True)
    keep, give = run_band(core, recv.reshape(16 * PACK, LANES))
    mine, other = sum_over_points(keep, give, lax.axis_size("pt"))
    step, cast = run_solve(core, damping, mine, other)
    everything = lax.all_to_all(cast, "cl", split_axis=0, concat_axis=0, tiled=True)
    point_step = run_update(everything.reshape(256, LANES), jac, proj, fact, where, dest)
    return (step[None], point_step)


def solution(mesh):
    in_specs = (
        P(None, None, None, None, ("pt", "cl")),
        P(None, None, None, None, ("pt", "cl")),
        P(None, None, None, ("pt", "cl")),
        P(None, None, ("pt", "cl")),
        P(None, ("pt", "cl")),
        P(("pt", "cl"), None),
        P(),
        P(),
        P(),
    )
    out_specs = (P("cl", None, None), P(None, ("pt", "cl")))
    return jax.shard_map(
        per_device, mesh=mesh, in_specs=in_specs, out_specs=out_specs, check_vma=False
    )
```

```python
import jax
import jax.numpy as jnp
from jax import lax
from jax.experimental import pallas as pl
from jax.experimental.pallas import tpu as pltpu
from jax.sharding import PartitionSpec as P

f32 = jnp.float32
bf16 = jnp.bfloat16
LANES = 128
SLOTS = 4
PARAMS = 9
GROUPS = 32
BLOCK = 9
NODES = 16
UNK = 27
ROW_Q = 45
ROW_D = (0, 54, 135, 216)
ROW_END = (54, 135, 216, 297)
NEEDED = ({0, 1, 2, 3}, {0, 1, 2}, {0, 1, 3}, {0, 2, 3})
BAND = 304
HALF = BAND // 2
PACK = 56
MIB = 1024 * 1024


def split3(value):
    high = value.astype(bf16)
    rest = value - high.astype(f32)
    mid = rest.astype(bf16)
    low = (rest - mid.astype(f32)).astype(bf16)
    return high, mid, low


def dot_nt(left, right):
    return lax.dot_general(left, right, (((1,), (1,)), ((), ())), preferred_element_type=f32)


def iota(shape, dim):
    return lax.broadcasted_iota(jnp.int32, shape, dim)


def lanes_from(value, index):
    return jnp.take_along_axis(value, index, axis=1)


def spread_row(chunk, row):
    return jnp.broadcast_to(chunk[row : row + 1, :], (8, LANES))


def lookup_dot(table, last, masks, cam_ref, jac_ref, out_ref):
    for half in range(2):
        cols = slice(half * LANES, (half + 1) * LANES)
        for s in range(2):
            rows, picks = masks[s][half]
            for k in range(SLOTS):
                at = 4 * s + k
                index = jnp.broadcast_to(cam_ref[at : at + 1, cols], (8, LANES))
                chosen = lanes_from(table[0], index)
                for c in range(1, 16):
                    chosen = jnp.where(picks[c], lanes_from(table[c], index), chosen)
                ninth = lanes_from(last[0], index) * rows[0] + lanes_from(last[1], index) * rows[1]
                for m in range(2):
                    base = s * SLOTS * PARAMS + k * PARAMS
                    terms = chosen * jac_ref[m, base : base + 8, cols]
                    terms = terms + ninth * jac_ref[m, base + 8 : base + 9, cols]
                    row = s * 8 + m * 4 + k
                    out_ref[row : row + 1, cols] = jnp.sum(terms, axis=0, keepdims=True)


def cluster_masks(cluster_rows):
    masks = []
    for s in range(2):
        per_half = []
        for half in range(2):
            row = cluster_rows[s : s + 1, half * LANES : (half + 1) * LANES]
            row = jnp.broadcast_to(row, (8, LANES))
            rows = [(iota((8, LANES), 0) + 8 * n == row).astype(f32) for n in range(2)]
            per_half.append((rows, [row == c for c in range(16)]))
        masks.append(per_half)
    return masks


def points_kernel(
    owner_ref,
    damp_ref,
    jac_hbm,
    jp_hbm,
    res_hbm,
    cam_hbm,
    count_hbm,
    clus_hbm,
    prev_hbm,
    send_ref,
    real_ref,
    jm_ref,
    where_ref,
    dots,
    packed,
    jac_ref,
    jp_ref,
    res_ref,
    cam_ref,
    count_ref,
    clus_ref,
    prev_ref,
    arrived,
):
    pairs = [
        (clus_hbm, clus_ref),
        (count_hbm, count_ref),
        (jp_hbm, jp_ref),
        (res_hbm, res_ref),
        (cam_hbm, cam_ref),
        (prev_hbm, prev_ref),
        (jac_hbm, jac_ref),
    ]
    copies = [
        pltpu.make_async_copy(source, target, arrived.at[n])
        for n, (source, target) in enumerate(pairs)
    ]
    for copy in copies:
        copy.start()
    for copy in copies:
        copy.wait()
    npts = 2 * LANES
    for m in range(2):
        jm_ref[m] = jac_ref[:, m, :]
    clus = clus_ref[...]
    dest = jnp.zeros_like(clus)
    for c in range(16):
        dest = jnp.where(clus == c, owner_ref[c], dest)
    where_ref[0:4, :] = cam_ref[0]
    where_ref[4:8, :] = cam_ref[1]
    where_ref[8:10, :] = dest
    slot_row = iota((8, npts), 0) % 4
    live = jnp.concatenate(
        [(slot_row < count_ref[s : s + 1, :]).astype(f32) for s in range(2)], axis=0
    )

    def by_slot(ref, step, first):
        rows = [
            ref[step * (4 * s + k) + first, m : m + 1, :]
            for s in range(2)
            for m in range(2)
            for k in range(SLOTS)
        ]
        return jnp.concatenate(rows, axis=0) * live

    jp = [by_slot(jp_ref, 3, a) for a in range(3)]
    res = by_slot(res_ref, 1, 0)

    def total(value):
        return jnp.sum(value, axis=0, keepdims=True)

    damp = damp_ref[0]
    inv1 = 1.0 / jnp.sqrt(total(jp[0] * jp[0]) + damp)
    l21 = total(jp[1] * jp[0]) * inv1
    l31 = total(jp[2] * jp[0]) * inv1
    inv2 = 1.0 / jnp.sqrt(total(jp[1] * jp[1]) + damp - l21 * l21)
    l32 = (total(jp[2] * jp[1]) - l31 * l21) * inv2
    inv3 = 1.0 / jnp.sqrt(total(jp[2] * jp[2]) + damp - l31 * l31 - l32 * l32)
    p1 = jp[0] * inv1
    p2 = (jp[1] - l21 * p1) * inv2
    p3 = (jp[2] - l31 * p1 - l32 * p2) * inv3
    proj = [p1, p2, p3]
    grad = [total(jp[a] * res) for a in range(3)]
    h1 = grad[0] * inv1
    h2 = (grad[1] - l21 * h1) * inv2
    h3 = (grad[2] - l31 * h1 - l32 * h2) * inv3
    h = [h1, h2, h3]
    for a in range(3):
        real_ref[16 * a : 16 * a + 16, :] = proj[a]
    for n, row in enumerate([inv1, inv2, inv3, l21, l31, l32, h1, h2, h3]):
        real_ref[48 + n : 49 + n, :] = row

    masks = cluster_masks(clus)
    table = [prev_ref[pl.ds(c, 8, stride=16), :] for c in range(16)]
    last = [prev_ref[128:136, :], prev_ref[136:144, :]]
    lookup_dot(table, last, masks, where_ref, jm_ref, dots)
    dot_all = dots[...]
    wt = -res
    for a in range(3):
        terms = proj[a] * dot_all
        carried = [jnp.sum(terms[8 * s : 8 * s + 8], axis=0, keepdims=True) for s in range(2)]
        mixed = jnp.concatenate(
            [jnp.broadcast_to(h[a] + carried[1 - s], (8, npts)) for s in range(2)], axis=0
        )
        wt = wt + proj[a] * mixed

    for s in range(2):
        cols = slice(s * npts, (s + 1) * npts)
        for m in range(2):
            base = m * PACK
            for k in range(SLOTS):
                on = live[s * 8 + m * 4 + k : s * 8 + m * 4 + k + 1, :]
                packed[base + 9 * k : base + 9 * k + 9, cols] = (
                    jm_ref[m, 36 * s + 9 * k : 36 * s + 9 * k + 9, :] * on
                )
            rows = slice(s * 8 + m * 4, s * 8 + m * 4 + 4)
            for a in range(3):
                packed[base + 36 + 4 * a : base + 40 + 4 * a, cols] = proj[a][rows]
            packed[base + 48 : base + 52, cols] = wt[rows]
            packed[base + 52 : base + 53, cols] = cam_ref[s, 0:1, :].astype(f32)
            packed[base + 53 : base + 56, cols] = jnp.zeros((3, npts), f32)

    dest_row = jnp.concatenate([dest[0:1], dest[1:2]], axis=1)
    hot = (iota((16, 2 * npts), 0) == dest_row).astype(f32)
    before = (iota((2 * npts, 2 * npts), 1) < iota((2 * npts, 2 * npts), 0)).astype(bf16)
    earlier = dot_nt(hot.astype(bf16), before)
    place = jnp.sum(earlier * hot, axis=0, keepdims=True)
    slot = dest_row * 64 + place.astype(jnp.int32)
    parts = split3(packed[...])
    left = jnp.concatenate(parts, axis=0)
    low_half = iota((PACK, LANES), 1) < 64
    for quad in range(4):
        slots = iota((2 * LANES, 2 * npts), 0) + quad * 2 * LANES
        pick = (slots == slot).astype(f32).astype(bf16)
        got = dot_nt(left, pick)
        full = got[0 : 2 * PACK] + got[2 * PACK : 4 * PACK] + got[4 * PACK : 6 * PACK]
        for pair in range(2):
            cols = slice(pair * LANES, (pair + 1) * LANES)
            first = full[0:PACK, cols]
            second = full[PACK : 2 * PACK, cols]
            first_r = pltpu.roll(first, 64, 1)
            second_r = pltpu.roll(second, 64, 1)
            send_ref[4 * quad + 2 * pair] = jnp.where(low_half, first, second_r)
            send_ref[4 * quad + 2 * pair + 1] = jnp.where(low_half, first_r, second)


def band_kernel(core_ref, recv_ref, keep_ref, give_ref, rows, wide, hots):
    low_half = iota((8, LANES), 1) < 64
    quant = [[], []]
    for r in range(53):
        even = recv_ref[pl.ds(r, 8, stride=2 * PACK), :]
        odd = recv_ref[pl.ds(PACK + r, 8, stride=2 * PACK), :]
        even_r = pltpu.roll(even, 64, 1)
        odd_r = pltpu.roll(odd, 64, 1)
        quant[0].append(jnp.where(low_half, even, odd_r))
        quant[1].append(jnp.where(low_half, even_r, odd))

    def jac(k, m, i):
        return quant[m][9 * k + i]

    def proj(k, m, a):
        return quant[m][36 + 4 * a + k]

    def wt(k, m):
        return quant[m][48 + k]

    cam = quant[0][52].astype(jnp.int32)
    camera_of = 4 * (iota((LANES, LANES), 0) % GROUPS) + iota((LANES, LANES), 0) // GROUPS
    for b in range(8):
        cam_b = jnp.broadcast_to(cam[b : b + 1, :], (LANES, LANES))
        for k in range(SLOTS):
            hots[k, :, b * LANES : (b + 1) * LANES] = (
                (camera_of == (cam_b + k) % LANES).astype(f32).astype(bf16)
            )

    sizes = [304, 224, 144, 64]
    starts = [0, 304, 528, 672]
    out = None
    for k in range(SLOTS):
        count = 0

        def put(row, value, k=k):
            at = 8 * (starts[k] + row)
            rows[at : at + 8, :] = value

        for dist in range(SLOTS - k):
            other = k + dist
            mix = [[None, None], [None, None]]
            for m in range(2):
                for n in range(2):
                    if dist == 0 and n < m:
                        mix[m][n] = mix[n][m]
                        continue
                    acc = proj(k, m, 0) * proj(other, n, 0)
                    acc = acc + proj(k, m, 1) * proj(other, n, 1)
                    acc = acc + proj(k, m, 2) * proj(other, n, 2)
                    same = dist == 0 and m == n
                    mix[m][n] = (1.0 - acc) if same else -acc
            for j in range(PARAMS):
                left = [
                    mix[m][0] * jac(other, 0, j) + mix[m][1] * jac(other, 1, j) for m in range(2)
                ]
                for i in range(PARAMS):
                    if dist == 0 and i > j:
                        continue
                    value = jac(k, 0, i) * left[0] + jac(k, 1, i) * left[1]
                    if dist == 0:
                        row = i * 9 - i * (i - 1) // 2 + (j - i)
                    else:
                        row = ROW_D[dist] + i * 9 + j
                    put(row, value)
                    count += 1
        for i in range(PARAMS):
            put(ROW_Q + i, jac(k, 0, i) * wt(k, 0) + jac(k, 1, i) * wt(k, 1))
            count += 1
        size = sizes[k]
        for row in range(count, size):
            put(row, jnp.zeros((8, LANES), f32))
        for b in range(8):
            piece = rows[pl.ds(8 * starts[k] + b, size, stride=8), :]
            for n, part in enumerate(split3(piece)):
                wide[n, starts[k] : starts[k] + size, b * LANES : (b + 1) * LANES] = part
        hot = hots[k]
        got = dot_nt(wide[0, starts[k] : starts[k] + size, :], hot)
        got = got + dot_nt(wide[1, starts[k] : starts[k] + size, :], hot)
        got = got + dot_nt(wide[2, starts[k] : starts[k] + size, :], hot)
        if out is None:
            out = got
        else:
            out = jnp.concatenate([out[0:size] + got, out[size:]], axis=0)
    core = core_ref[0]
    low, high = out[0:HALF], out[HALF:BAND]
    keep_ref[...] = jnp.where(core == 0, low, high)
    give_ref[...] = jnp.where(core == 0, high, low)


def factor(size, diag, side, side_chunks):
    chunks = len(diag[0])
    inverse = []
    for k in range(size):
        pivot = spread_row(diag[k][k // 8], k % 8)
        root = lax.rsqrt(pivot)
        root = root * (1.5 - 0.5 * pivot * root * root)
        inverse.append(root)
        for v in range(k // 8, chunks):
            diag[k][v] = diag[k][v] * root
        for e in side_chunks:
            side[k][e] = side[k][e] * root
        for r in range(k + 1, size):
            coef = spread_row(diag[k][r // 8], r % 8)
            for v in range(r // 8, chunks):
                diag[r][v] = diag[r][v] - coef * diag[k][v]
            for e in side_chunks:
                side[r][e] = side[r][e] - coef * side[k][e]
    return inverse


def advance(size, work, diag, side, lane, whole):
    within = lane % GROUPS
    part = lane // GROUPS
    from_up = (within + 1) % GROUPS
    pack_up = part * GROUPS + from_up
    is_left = part < 2
    is_rhs = jnp.logical_and(part == 1, iota((8, LANES), 0) == 3)
    for which in range(2):
        for v in range(4):
            for r in range(size):
                at = 32 * (which * UNK + r) + 8 * v
                whole[at : at + 8, :] = lanes_from(
                    work[r][v % 2], within + GROUPS * (2 * which + v // 2)
                )
    for first in range(0, UNK, BLOCK):
        block = range(first, min(first + BLOCK, UNK))
        sums = []
        for which in range(2):
            acc = {}
            for r in range(size):
                for a in block:
                    at = 32 * (which * UNK + r) + a
                    coef = jnp.broadcast_to(whole[at : at + 1, :], (8, LANES))
                    for e in range(2):
                        term = coef * work[r][e]
                        acc[a, e] = term if r == 0 else acc[a, e] + term
            sums.append(acc)
        left, right = sums
        for a in block:
            for e in range(2):
                by_up = lanes_from(left[a, e], pack_up)
                new = side[a][e] - jnp.where(is_left, right[a, e], by_up)
                if e == 1:
                    new = new - jnp.where(is_rhs, by_up, 0.0)
                side[a][e] = new
        for v in range(first // 8, 4):
            for a in block:
                if v >= a // 8:
                    own = lanes_from(right[a, v % 2], within + GROUPS * (2 + v // 2))
                    diag[a][v] = diag[a][v] - own
            for a in block:
                if v >= a // 8:
                    other = lanes_from(left[a, v % 2], from_up + GROUPS * (v // 2))
                    diag[a][v] = diag[a][v] - other


def advance_wide(work, diag, side, lane, whole, down, up):
    within = lane % NODES
    part = lane // NODES
    from_down = (within - down + NODES) % NODES
    from_up = (within + up) % NODES
    pack_down = part * NODES + from_down
    pack_up = part * NODES + from_up
    is_left = part < 4
    is_rhs = jnp.logical_and(part == 3, iota((8, LANES), 0) == 3)
    for v in range(8):
        for r in range(UNK):
            at = 64 * r + 8 * v
            whole[at : at + 8, :] = lanes_from(work[r][0], within + NODES * v)
    for first in range(0, UNK, BLOCK):
        block = range(first, min(first + BLOCK, UNK))
        sums = []
        for which in range(2):
            acc = {}
            for r in range(UNK):
                for a in block:
                    at = 64 * r + 32 * which + a
                    term = jnp.broadcast_to(whole[at : at + 1, :], (8, LANES)) * work[r][0]
                    acc[a] = term if r == 0 else acc[a] + term
            sums.append(acc)
        left, right = sums
        for a in block:
            by_down = lanes_from(right[a], pack_down)
            by_up = lanes_from(left[a], pack_up)
            new = -jnp.where(is_left, by_down, by_up)
            side[a] = [new + jnp.where(is_rhs, side[a][0] - by_up, 0.0)]
        for v in range(first // 8, 4):
            for a in block:
                if v >= a // 8:
                    own = lanes_from(right[a], from_down + NODES * (4 + v))
                    diag[a][v] = diag[a][v] - own
            for a in block:
                if v >= a // 8:
                    other = lanes_from(left[a], from_up + NODES * v)
                    diag[a][v] = diag[a][v] - other


def solve_kernel(
    core_ref, damp_ref, mine_ref, other_ref, step_ref, cast_ref, rep, back, dmat, smat, xrow, whole
):
    lane = iota((8, LANES), 1)
    sub = iota((8, LANES), 0)
    within = lane % GROUPS
    part = lane // GROUPS
    core = core_ref[0]
    low = jnp.where(core == 0, mine_ref[...], other_ref[...])
    high = jnp.where(core == 0, other_ref[...], mine_ref[...])
    row = iota((HALF, LANES), 0)
    on_diag = row < 0
    for i in range(PARAMS):
        on_diag = jnp.logical_or(on_diag, row == i * 9 - i * (i - 1) // 2)
    low = low + jnp.where(on_diag, damp_ref[0], 0.0)
    first_rows = HALF // 8
    for r in range(4):
        for shift, wanted in ((0, NEEDED[r]), (1, set(range(4 - r, 4)))):
            index = (within + GROUPS - shift) % GROUPS + GROUPS * r
            for n in range(BAND // 8):
                kinds = {d for d in range(4) if ROW_D[d] < 8 * n + 8 and 8 * n < ROW_END[d]}
                if not kinds & wanted:
                    continue
                at = slice(8 * n, 8 * n + 8)
                chunk = low[at] if n < first_rows else high[8 * n - HALF : 8 * n - HALF + 8]
                if shift:
                    back[r - 1, at, :] = lanes_from(chunk, index)
                else:
                    rep[r, at, :] = lanes_from(chunk, index)

    def tri(i):
        return i * 9 - i * (i - 1) // 2

    def line(ref, r, start):
        return jnp.broadcast_to(ref[r, start : start + 1, :], (8, LANES))

    def tail(values):
        out = jnp.zeros((8, LANES), f32)
        for n, value in values:
            out = jnp.where(sub == n, value, out)
        return out

    def forward(r, d, i):
        start = tri(i) - i if d == 0 else ROW_D[d] + 9 * i
        return rep[r, start : start + 8, :], line(rep, r, start + 8)

    def backward(r, d, i):
        start = ROW_D[d] + i
        return back[r - 1, pl.ds(start, 8, stride=9), :], line(back, r - 1, start + 72)

    def pack(lm, um):
        return [
            jnp.where(
                part == 0,
                lm[e],
                jnp.where(part == 1, lm[2 + e], jnp.where(part == 2, um[e], um[2 + e])),
            )
            for e in range(2)
        ]

    def rhs(r, i):
        return line(rep, r, ROW_Q + i)

    def chunked(value, count):
        return [value[8 * v : 8 * v + 8] for v in range(count)]

    zero = jnp.zeros((8, LANES), f32)

    diag0, side0 = [], []
    for i in range(PARAMS):
        diag0.append(list(forward(0, 0, i)))
        after = [forward(0, d, i) for d in (1, 2, 3)]
        before = [backward(4 - d, d, i) for d in (3, 2, 1)]
        lm = [p[0] for p in before]
        lm.append(tail([(n, p[1]) for n, p in enumerate(before)] + [(3, rhs(0, i))]))
        um = [p[0] for p in after]
        um.append(tail([(n, p[1]) for n, p in enumerate(after)]))
        side0.append(pack(lm, um))
    inv0 = factor(PARAMS, diag0, side0, (0, 1))

    diag, side = [], []
    for a in range(UNK):
        r, i = (a // 8 + 1, a % 8) if a < 24 else (a - 23, 8)
        own = {q: forward(r, q - r, i) for q in range(r, 4)}
        ahead = {q: forward(r, 4 + q - r, i) for q in range(1, r)}
        behind = {q: backward(q, 4 + r - q, i) for q in range(r + 1, 4)}
        diag.append([own[q][0] if q in own else zero for q in (1, 2, 3)])
        ninths = [(q - 1, p[1]) for q, p in own.items()]
        ninths += [(q - 1, line(rep, q, ROW_D[r - q] + 72 + i)) for q in range(1, r)]
        diag[a].append(tail(ninths))
        um = [ahead[q][0] if q in ahead else zero for q in (1, 2, 3)]
        um.append(tail([(q - 1, p[1]) for q, p in ahead.items()]))
        lm = [behind[q][0] if q in behind else zero for q in (1, 2, 3)]
        lm.append(tail([(q - 1, p[1]) for q, p in behind.items()] + [(3, rhs(r, i))]))
        side.append(pack(lm, um))
    advance(PARAMS, side0, diag, side, lane, whole)

    few = lane % NODES
    which = lane // NODES
    odd_diag = [[None] * 4 for a in range(UNK)]
    even_diag = [[None] * 4 for a in range(UNK)]
    for n, target in enumerate((even_diag, odd_diag)):
        for a in range(UNK):
            for v in range(a // 8, 4):
                target[a][v] = lanes_from(diag[a][v], 2 * few + n)
    base = 2 * few + GROUPS * (2 * (which // 4) + (which % 4) // 2)
    split = []
    for n in range(2):
        first = [lanes_from(side[a][0], base + n) for a in range(UNK)]
        second = [lanes_from(side[a][1], base + n) for a in range(UNK)]
        split.append([[jnp.where(which % 2 == 0, p, q)] for p, q in zip(first, second)])
    diag, (side, odd_side) = even_diag, split
    odd_inverse = factor(UNK, odd_diag, odd_side, (0,))
    advance_wide(odd_side, diag, side, lane, whole, 1, 0)

    def store(diag, side):
        for a in range(UNK):
            for v in range(a // 8, 4):
                dmat[a, 8 * v : 8 * v + 8, :] = diag[a][v]
            smat[a] = side[a][0]

    def load():
        diag = [
            [dmat[a, 8 * v : 8 * v + 8, :] if v >= a // 8 else None for v in range(4)]
            for a in range(UNK)
        ]
        return diag, [[smat[a]] for a in range(UNK)]

    store(diag, side)

    def level(step, carry):
        stride = lax.shift_left(jnp.int32(1), step)
        diag, side = load()
        factor(UNK, diag, side, (0,))
        work = side
        diag, side = load()
        advance_wide(work, diag, side, lane, whole, stride, stride)
        store(diag, side)
        return carry

    lax.fori_loop(0, 3, level, jnp.int32(0))

    diag, side = load()
    from_left = [lanes_from(side[a][0], few + NODES * (which % 4)) for a in range(UNK)]
    from_right = [lanes_from(side[a][0], few + NODES * (4 + which % 4)) for a in range(UNK)]
    both = [[p + q] for p, q in zip(from_left, from_right)]
    for a in range(UNK):
        right_side = lanes_from(side[a][0], few + 3 * NODES)
        diag[a][3] = jnp.where(sub == 3, right_side, diag[a][3])
    work = [list(line_of) for line_of in diag]
    factor(UNK, work, both, (0,))
    for v in range(4):
        for r in range(UNK):
            at = 64 * r + 8 * v
            whole[at : at + 8, :] = lanes_from(both[r][0], few + NODES * v)
    for first in range(0, UNK, BLOCK):
        block = range(first, min(first + BLOCK, UNK))
        acc = {}
        for r in range(UNK):
            for a in block:
                at = 64 * r + a
                term = jnp.broadcast_to(whole[at : at + 1, :], (8, LANES)) * both[r][0]
                acc[a] = term if r == 0 else acc[a] + term
        for v in range(first // 8, 4):
            for a in block:
                if v >= a // 8:
                    moved = lanes_from(acc[a], (few + NODES // 2) % NODES + NODES * v)
                    diag[a][v] = diag[a][v] - moved
    inverse = factor(UNK, diag, both, ())

    def back_solve(size, diag, inverse, todo):
        value = [None] * size
        for k in range(size - 1, -1, -1):
            value[k] = todo[k] * inverse[k]
            for r in range(k):
                todo[r] = todo[r] - spread_row(diag[r][k // 8], k % 8) * value[k]
        return value

    def as_chunks(value):
        for a in range(UNK):
            xrow[a : a + 1, :] = value[a][0:1]
        xrow[UNK:32, :] = jnp.zeros((5, LANES), f32)
        return chunked(xrow[...], 4)

    even_steps = as_chunks(
        back_solve(UNK, diag, inverse, [spread_row(diag[a][3], 3) for a in range(UNK)])
    )
    packed = jnp.zeros((8, LANES), f32)
    for v in range(4):
        packed = jnp.where(which == v, even_steps[v], packed)
        after = lanes_from(even_steps[v], (few + 1) % NODES)
        packed = jnp.where(which == 4 + v, after, packed)
    right_sides = [lanes_from(odd_side[a][0], few + 3 * NODES) for a in range(UNK)]
    todo = []
    for a in range(UNK):
        terms = odd_side[a][0] * packed
        for shift in (64, 32, 16):
            terms = terms + pltpu.roll(terms, shift, 1)
        summed = jnp.broadcast_to(jnp.sum(terms, axis=0, keepdims=True), (8, LANES))
        todo.append(spread_row(right_sides[a], 3) - summed)
    odd_steps = as_chunks(back_solve(UNK, odd_diag, odd_inverse, todo))
    own = [
        jnp.where(
            lane % 2 == 0,
            lanes_from(even_steps[v], within // 2),
            lanes_from(odd_steps[v], within // 2),
        )
        for v in range(4)
    ]
    prev = [lanes_from(c, (lane + LANES - 1) % LANES) for c in own]
    packed = pack(prev, own)
    todo0 = []
    for i in range(PARAMS):
        terms = side0[i][0] * packed[0] + side0[i][1] * packed[1]
        terms = terms + pltpu.roll(terms, 64, 1)
        terms = terms + pltpu.roll(terms, 32, 1)
        right_side = spread_row(lanes_from(side0[i][1], within + GROUPS), 3)
        summed = jnp.broadcast_to(jnp.sum(terms, axis=0, keepdims=True), (8, LANES))
        todo0.append(right_side - summed)
    value0 = back_solve(PARAMS, diag0, inv0, todo0)
    camera = (lane % 4) * GROUPS + lane // 4
    for i in range(PARAMS):
        near = [spread_row(own[r], i) if i < 8 else spread_row(own[3], r) for r in range(3)]
        mixed = jnp.where(
            part == 0,
            value0[i],
            jnp.where(part == 1, near[0], jnp.where(part == 2, near[1], near[2])),
        )
        step_ref[i : i + 1, :] = lanes_from(mixed, camera)[0:1]
    for dest in range(16):
        cast_ref[dest, 0:PARAMS, :] = step_ref[...]
        cast_ref[dest, PARAMS:16, :] = jnp.zeros((16 - PARAMS, LANES), f32)


def update_kernel(all_ref, jac_ref, real_ref, where_ref, out_ref, dots):
    masks = cluster_masks(where_ref[8:10, :])
    table = [all_ref[16 * c : 16 * c + 8, :] for c in range(16)]
    last = [all_ref[pl.ds(8, 8, stride=16), :], all_ref[pl.ds(136, 8, stride=16), :]]
    lookup_dot(table, last, masks, where_ref, jac_ref, dots)
    dot_all = dots[...]

    def fact(n):
        return real_ref[48 + n : 49 + n, :]

    tot = []
    for a in range(3):
        terms = real_ref[16 * a : 16 * a + 16, :] * dot_all
        tot.append(fact(6 + a) + jnp.sum(terms, axis=0, keepdims=True))
    x3 = tot[2] * fact(2)
    x2 = (tot[1] - fact(5) * x3) * fact(1)
    x1 = (tot[0] - fact(3) * x2 - fact(4) * x3) * fact(0)
    out_ref[0:1, :] = -x1
    out_ref[1:2, :] = -x2
    out_ref[2:3, :] = -x3


def smem():
    return pl.BlockSpec(memory_space=pltpu.SMEM)


def vmem():
    return pl.BlockSpec(memory_space=pltpu.VMEM)


def params(mib):
    return pltpu.CompilerParams(vmem_limit_bytes=mib * MIB)


def run_points(owner_map, damping, jac, jp, res, cam_ids, obs_count, clus, prev):
    npts = 256
    return pl.pallas_call(
        points_kernel,
        out_shape=(
            jax.ShapeDtypeStruct((16, PACK, LANES), f32),
            jax.ShapeDtypeStruct((57, npts), f32),
            jax.ShapeDtypeStruct((2, 8 * PARAMS, npts), f32),
            jax.ShapeDtypeStruct((10, npts), jnp.int32),
        ),
        in_specs=[smem(), smem()] + [pl.BlockSpec(memory_space=pltpu.HBM)] * 7,
        out_specs=(vmem(),) * 4,
        scratch_shapes=[
            pltpu.VMEM((16, npts), f32),
            pltpu.VMEM((2 * PACK, 2 * npts), f32),
            pltpu.VMEM(jac.shape, f32),
            pltpu.VMEM(jp.shape, f32),
            pltpu.VMEM(res.shape, f32),
            pltpu.VMEM(cam_ids.shape, jnp.int32),
            pltpu.VMEM(obs_count.shape, jnp.int32),
            pltpu.VMEM(clus.shape, jnp.int32),
            pltpu.VMEM(prev.shape, f32),
            pltpu.SemaphoreType.DMA((7,)),
        ],
        compiler_params=params(58),
        name="points",
    )(owner_map, damping, jac, jp, res, cam_ids, obs_count, clus, prev)


def run_band(core, recv):
    return pl.pallas_call(
        band_kernel,
        out_shape=(
            jax.ShapeDtypeStruct((HALF, LANES), f32),
            jax.ShapeDtypeStruct((HALF, LANES), f32),
        ),
        in_specs=[smem(), vmem()],
        out_specs=(vmem(), vmem()),
        scratch_shapes=[
            pltpu.VMEM((736 * 8, LANES), f32),
            pltpu.VMEM((3, 736, 1024), bf16),
            pltpu.VMEM((4, LANES, 1024), bf16),
        ],
        compiler_params=params(20),
        name="band",
    )(core, recv)


def run_solve(core, damping, mine, other):
    return pl.pallas_call(
        solve_kernel,
        out_shape=(
            jax.ShapeDtypeStruct((PARAMS, LANES), f32),
            jax.ShapeDtypeStruct((16, 16, LANES), f32),
        ),
        in_specs=[smem(), smem(), vmem(), vmem()],
        out_specs=(vmem(), vmem()),
        scratch_shapes=[
            pltpu.VMEM((4, BAND, LANES), f32),
            pltpu.VMEM((3, BAND, LANES), f32),
            pltpu.VMEM((UNK, 32, LANES), f32),
            pltpu.VMEM((UNK, 8, LANES), f32),
            pltpu.VMEM((32, LANES), f32),
            pltpu.VMEM((2 * UNK * 32, LANES), f32),
        ],
        compiler_params=params(12),
        name="solve",
    )(core, damping, mine, other)


def run_update(everything, jac, real, where):
    return pl.pallas_call(
        update_kernel,
        out_shape=jax.ShapeDtypeStruct((3, 256), f32),
        in_specs=[vmem()] * 4,
        out_specs=vmem(),
        scratch_shapes=[pltpu.VMEM((16, 256), f32)],
        compiler_params=params(8),
        name="update",
    )(everything, jac, real, where)


def sum_over_points(keep, give, ring):
    swap = [(i, i ^ 1) for i in range(ring)]
    half = keep + lax.ppermute(give, "pt", swap)
    moved = [lax.ppermute(half, "pt", [(i, i ^ (2 * d)) for i in range(ring)]) for d in (1, 2, 3)]
    mine = (half + moved[0]) + (moved[1] + moved[2])
    return mine, lax.ppermute(mine, "pt", swap)


def per_device(
    cam_jac, pt_jac, residual, cam_ids, obs_count, clusters, owner_map, prev_step, damping
):
    npts = cam_jac.shape[-1]
    core = (lax.axis_index("pt") % 2).astype(jnp.int32).reshape(1)
    send, real, jac, where = run_points(
        owner_map,
        damping,
        cam_jac.transpose(0, 1, 3, 2, 4).reshape(8 * PARAMS, 2, npts),
        pt_jac.transpose(0, 1, 3, 2, 4).reshape(24, 2, npts),
        residual.reshape(8, 2, npts),
        cam_ids,
        obs_count,
        clusters.T,
        prev_step.transpose(1, 0, 2).reshape(PARAMS * 16, LANES),
    )
    recv = lax.all_to_all(send, "cl", split_axis=0, concat_axis=0, tiled=True)
    keep, give = run_band(core, recv.reshape(16 * PACK, LANES))
    mine, other = sum_over_points(keep, give, lax.axis_size("pt"))
    step, cast = run_solve(core, damping, mine, other)
    everything = lax.all_to_all(cast, "cl", split_axis=0, concat_axis=0, tiled=True)
    point_step = run_update(everything.reshape(256, LANES), jac, real, where)
    return (step[None], point_step)


def solution(mesh):
    in_specs = (
        P(None, None, None, None, ("pt", "cl")),
        P(None, None, None, None, ("pt", "cl")),
        P(None, None, None, ("pt", "cl")),
        P(None, None, ("pt", "cl")),
        P(None, ("pt", "cl")),
        P(("pt", "cl"), None),
        P(),
        P(),
        P(),
    )
    out_specs = (P("cl", None, None), P(None, ("pt", "cl")))
    return jax.shard_map(
        per_device, mesh=mesh, in_specs=in_specs, out_specs=out_specs, check_vma=False
    )
```

```python
import jax
import jax.numpy as jnp
from jax import lax
from jax.experimental import pallas as pl
from jax.experimental.pallas import tpu as pltpu
from jax.sharding import PartitionSpec as P

f32 = jnp.float32
bf16 = jnp.bfloat16
LANES = 128
SLOTS = 4
PARAMS = 9
GROUPS = 32
BLOCK = 9
NODES = 16
UNK = 27
ROW_Q = 45
ROW_D = (0, 54, 135, 216)
ROW_END = (54, 135, 216, 297)
NEEDED = ({0, 1, 2, 3}, {0, 1, 2}, {0, 1, 3}, {0, 2, 3})
BAND = 304
HALF = BAND // 2
DIAG = 45
PACK = 56
MIB = 1024 * 1024


def split3(value):
    high = value.astype(bf16)
    rest = value - high.astype(f32)
    mid = rest.astype(bf16)
    low = (rest - mid.astype(f32)).astype(bf16)
    return high, mid, low


def dot_nt(left, right):
    return lax.dot_general(left, right, (((1,), (1,)), ((), ())), preferred_element_type=f32)


def iota(shape, dim):
    return lax.broadcasted_iota(jnp.int32, shape, dim)


def lanes_from(value, index):
    return jnp.take_along_axis(value, index, axis=1)


def spread_row(chunk, row):
    return jnp.broadcast_to(chunk[row : row + 1, :], (8, LANES))


def lookup_dot(table, last, masks, cam_ref, jac_ref, out_ref):
    for half in range(2):
        cols = slice(half * LANES, (half + 1) * LANES)
        for s in range(2):
            rows, picks = masks[s][half]
            for k in range(SLOTS):
                at = 4 * s + k
                index = jnp.broadcast_to(cam_ref[at : at + 1, cols], (8, LANES))
                chosen = lanes_from(table[0], index)
                for c in range(1, 16):
                    chosen = jnp.where(picks[c], lanes_from(table[c], index), chosen)
                ninth = lanes_from(last[0], index) * rows[0] + lanes_from(last[1], index) * rows[1]
                for m in range(2):
                    base = s * SLOTS * PARAMS + k * PARAMS
                    terms = chosen * jac_ref[m, base : base + 8, cols]
                    terms = terms + ninth * jac_ref[m, base + 8 : base + 9, cols]
                    row = s * 8 + m * 4 + k
                    out_ref[row : row + 1, cols] = jnp.sum(terms, axis=0, keepdims=True)


def cluster_masks(cluster_rows):
    masks = []
    for s in range(2):
        per_half = []
        for half in range(2):
            row = cluster_rows[s : s + 1, half * LANES : (half + 1) * LANES]
            row = jnp.broadcast_to(row, (8, LANES))
            rows = [(iota((8, LANES), 0) + 8 * n == row).astype(f32) for n in range(2)]
            per_half.append((rows, [row == c for c in range(16)]))
        masks.append(per_half)
    return masks


def points_kernel(
    owner_ref,
    damp_ref,
    jac_hbm,
    jp_hbm,
    res_hbm,
    cam_hbm,
    count_hbm,
    clus_hbm,
    prev_hbm,
    send_ref,
    real_ref,
    jm_ref,
    where_ref,
    dots,
    packed,
    jac_ref,
    jp_ref,
    res_ref,
    cam_ref,
    count_ref,
    clus_ref,
    prev_ref,
    arrived,
):
    pairs = [
        (clus_hbm, clus_ref),
        (count_hbm, count_ref),
        (jp_hbm, jp_ref),
        (res_hbm, res_ref),
        (cam_hbm, cam_ref),
        (prev_hbm, prev_ref),
        (jac_hbm, jac_ref),
    ]
    copies = [
        pltpu.make_async_copy(source, target, arrived.at[n])
        for n, (source, target) in enumerate(pairs)
    ]
    for copy in copies:
        copy.start()
    for copy in copies:
        copy.wait()
    npts = 2 * LANES
    for m in range(2):
        jm_ref[m] = jac_ref[:, m, :]
    clus = clus_ref[...]
    dest = jnp.zeros_like(clus)
    for c in range(16):
        dest = jnp.where(clus == c, owner_ref[c], dest)
    where_ref[0:4, :] = cam_ref[0]
    where_ref[4:8, :] = cam_ref[1]
    where_ref[8:10, :] = dest
    slot_row = iota((8, npts), 0) % 4
    live = jnp.concatenate(
        [(slot_row < count_ref[s : s + 1, :]).astype(f32) for s in range(2)], axis=0
    )

    def by_slot(ref, step, first):
        rows = [
            ref[step * (4 * s + k) + first, m : m + 1, :]
            for s in range(2)
            for m in range(2)
            for k in range(SLOTS)
        ]
        return jnp.concatenate(rows, axis=0) * live

    jp = [by_slot(jp_ref, 3, a) for a in range(3)]
    res = by_slot(res_ref, 1, 0)

    def total(value):
        return jnp.sum(value, axis=0, keepdims=True)

    damp = damp_ref[0]
    inv1 = 1.0 / jnp.sqrt(total(jp[0] * jp[0]) + damp)
    l21 = total(jp[1] * jp[0]) * inv1
    l31 = total(jp[2] * jp[0]) * inv1
    inv2 = 1.0 / jnp.sqrt(total(jp[1] * jp[1]) + damp - l21 * l21)
    l32 = (total(jp[2] * jp[1]) - l31 * l21) * inv2
    inv3 = 1.0 / jnp.sqrt(total(jp[2] * jp[2]) + damp - l31 * l31 - l32 * l32)
    p1 = jp[0] * inv1
    p2 = (jp[1] - l21 * p1) * inv2
    p3 = (jp[2] - l31 * p1 - l32 * p2) * inv3
    proj = [p1, p2, p3]
    grad = [total(jp[a] * res) for a in range(3)]
    h1 = grad[0] * inv1
    h2 = (grad[1] - l21 * h1) * inv2
    h3 = (grad[2] - l31 * h1 - l32 * h2) * inv3
    h = [h1, h2, h3]
    for a in range(3):
        real_ref[16 * a : 16 * a + 16, :] = proj[a]
    for n, row in enumerate([inv1, inv2, inv3, l21, l31, l32, h1, h2, h3]):
        real_ref[48 + n : 49 + n, :] = row

    masks = cluster_masks(clus)
    table = [prev_ref[pl.ds(c, 8, stride=16), :] for c in range(16)]
    last = [prev_ref[128:136, :], prev_ref[136:144, :]]
    lookup_dot(table, last, masks, where_ref, jm_ref, dots)
    dot_all = dots[...]
    wt = -res
    for a in range(3):
        terms = proj[a] * dot_all
        carried = [jnp.sum(terms[8 * s : 8 * s + 8], axis=0, keepdims=True) for s in range(2)]
        mixed = jnp.concatenate(
            [jnp.broadcast_to(h[a] + carried[1 - s], (8, npts)) for s in range(2)], axis=0
        )
        wt = wt + proj[a] * mixed

    for s in range(2):
        cols = slice(s * npts, (s + 1) * npts)
        for m in range(2):
            base = m * PACK
            for k in range(SLOTS):
                on = live[s * 8 + m * 4 + k : s * 8 + m * 4 + k + 1, :]
                packed[base + 9 * k : base + 9 * k + 9, cols] = (
                    jm_ref[m, 36 * s + 9 * k : 36 * s + 9 * k + 9, :] * on
                )
            rows = slice(s * 8 + m * 4, s * 8 + m * 4 + 4)
            for a in range(3):
                packed[base + 36 + 4 * a : base + 40 + 4 * a, cols] = proj[a][rows]
            packed[base + 48 : base + 52, cols] = wt[rows]
            packed[base + 52 : base + 53, cols] = cam_ref[s, 0:1, :].astype(f32)
            packed[base + 53 : base + 56, cols] = jnp.zeros((3, npts), f32)

    dest_row = jnp.concatenate([dest[0:1], dest[1:2]], axis=1)
    hot = (iota((16, 2 * npts), 0) == dest_row).astype(f32)
    before = (iota((2 * npts, 2 * npts), 1) < iota((2 * npts, 2 * npts), 0)).astype(bf16)
    earlier = dot_nt(hot.astype(bf16), before)
    place = jnp.sum(earlier * hot, axis=0, keepdims=True)
    slot = dest_row * 64 + place.astype(jnp.int32)
    parts = split3(packed[...])
    left = jnp.concatenate(parts, axis=0)
    low_half = iota((PACK, LANES), 1) < 64
    for quad in range(4):
        slots = iota((2 * LANES, 2 * npts), 0) + quad * 2 * LANES
        pick = (slots == slot).astype(f32).astype(bf16)
        got = dot_nt(left, pick)
        full = got[0 : 2 * PACK] + got[2 * PACK : 4 * PACK] + got[4 * PACK : 6 * PACK]
        for pair in range(2):
            cols = slice(pair * LANES, (pair + 1) * LANES)
            first = full[0:PACK, cols]
            second = full[PACK : 2 * PACK, cols]
            first_r = pltpu.roll(first, 64, 1)
            second_r = pltpu.roll(second, 64, 1)
            send_ref[4 * quad + 2 * pair] = jnp.where(low_half, first, second_r)
            send_ref[4 * quad + 2 * pair + 1] = jnp.where(low_half, first_r, second)


def band_kernel(half_ref, recv_ref, out_ref, rows, wide, hots):
    low_half = iota((8, LANES), 1) < 64
    quant = [[], []]
    for r in range(53):
        even = recv_ref[pl.ds(r, 8, stride=2 * PACK), :]
        odd = recv_ref[pl.ds(PACK + r, 8, stride=2 * PACK), :]
        even_r = pltpu.roll(even, 64, 1)
        odd_r = pltpu.roll(odd, 64, 1)
        quant[0].append(jnp.where(low_half, even, odd_r))
        quant[1].append(jnp.where(low_half, even_r, odd))

    def jac(k, m, i):
        return quant[m][9 * k + i]

    def proj(k, m, a):
        return quant[m][36 + 4 * a + k]

    def wt(k, m):
        return quant[m][48 + k]

    cam = quant[0][52].astype(jnp.int32)
    camera_of = 4 * (iota((LANES, LANES), 0) % GROUPS) + iota((LANES, LANES), 0) // GROUPS

    def part_of_band(half, sizes):
        starts = [sum(sizes[:k]) for k in range(len(sizes))]
        for b in range(8):
            cam_b = jnp.broadcast_to(cam[b : b + 1, :], (LANES, LANES))
            for k in range(len(sizes)):
                hots[k, :, b * LANES : (b + 1) * LANES] = (
                    (camera_of == (cam_b + k) % LANES).astype(f32).astype(bf16)
                )
        out = None
        for k, size in enumerate(sizes):
            seen = set()

            def wanted(row):
                return 0 <= row - HALF * half < HALF

            def put(row, value, k=k, seen=seen):
                local = row - HALF * half
                seen.add(local)
                at = 8 * (starts[k] + local)
                rows[at : at + 8, :] = value

            for dist in range(SLOTS - k):
                other = k + dist
                last = DIAG if dist == 0 else ROW_D[dist] + 81
                start = 0 if dist == 0 else ROW_D[dist]
                if not any(wanted(row) for row in range(start, last)):
                    continue
                mix = [[None, None], [None, None]]
                for m in range(2):
                    for n in range(2):
                        if dist == 0 and n < m:
                            mix[m][n] = mix[n][m]
                            continue
                        acc = proj(k, m, 0) * proj(other, n, 0)
                        acc = acc + proj(k, m, 1) * proj(other, n, 1)
                        acc = acc + proj(k, m, 2) * proj(other, n, 2)
                        same = dist == 0 and m == n
                        mix[m][n] = (1.0 - acc) if same else -acc
                for j in range(PARAMS):
                    left = [
                        mix[m][0] * jac(other, 0, j) + mix[m][1] * jac(other, 1, j)
                        for m in range(2)
                    ]
                    for i in range(PARAMS):
                        if dist == 0:
                            row = i * 9 - i * (i - 1) // 2 + (j - i)
                        else:
                            row = ROW_D[dist] + i * 9 + j
                        if (dist == 0 and i > j) or not wanted(row):
                            continue
                        put(row, jac(k, 0, i) * left[0] + jac(k, 1, i) * left[1])
            for i in range(PARAMS):
                if wanted(ROW_Q + i):
                    put(ROW_Q + i, jac(k, 0, i) * wt(k, 0) + jac(k, 1, i) * wt(k, 1))
            for local in range(size):
                if local not in seen:
                    rows[8 * (starts[k] + local) : 8 * (starts[k] + local) + 8, :] = jnp.zeros(
                        (8, LANES), f32
                    )
            at = slice(starts[k], starts[k] + size)
            for b in range(8):
                piece = rows[pl.ds(8 * starts[k] + b, size, stride=8), :]
                for n, part in enumerate(split3(piece)):
                    wide[n, at, b * LANES : (b + 1) * LANES] = part
            hot = hots[k]
            got = dot_nt(wide[0, at, :], hot)
            got = got + dot_nt(wide[1, at, :], hot)
            got = got + dot_nt(wide[2, at, :], hot)
            if out is None:
                out = got
            elif size == out.shape[0]:
                out = out + got
            else:
                out = jnp.concatenate([out[:size] + got, out[size:]], axis=0)
        out_ref[...] = out[0:HALF]

    @pl.when(half_ref[0] == 0)
    def _():
        part_of_band(0, [160, 160, 144, 64])

    @pl.when(half_ref[0] == 1)
    def _():
        part_of_band(1, [160, 64])


def factor(size, diag, side, side_chunks):
    chunks = len(diag[0])
    inverse = []
    for k in range(size):
        pivot = spread_row(diag[k][k // 8], k % 8)
        root = lax.rsqrt(pivot)
        root = root * (1.5 - 0.5 * pivot * root * root)
        inverse.append(root)
        for v in range(k // 8, chunks):
            diag[k][v] = diag[k][v] * root
        for e in side_chunks:
            side[k][e] = side[k][e] * root
        for r in range(k + 1, size):
            coef = spread_row(diag[k][r // 8], r % 8)
            for v in range(r // 8, chunks):
                diag[r][v] = diag[r][v] - coef * diag[k][v]
            for e in side_chunks:
                side[r][e] = side[r][e] - coef * side[k][e]
    return inverse


def advance(size, work, diag, side, lane, whole):
    within = lane % GROUPS
    part = lane // GROUPS
    from_up = (within + 1) % GROUPS
    pack_up = part * GROUPS + from_up
    is_left = part < 2
    is_rhs = jnp.logical_and(part == 1, iota((8, LANES), 0) == 3)
    for which in range(2):
        for v in range(4):
            for r in range(size):
                at = 32 * (which * UNK + r) + 8 * v
                whole[at : at + 8, :] = lanes_from(
                    work[r][v % 2], within + GROUPS * (2 * which + v // 2)
                )
    for first in range(0, UNK, BLOCK):
        block = range(first, min(first + BLOCK, UNK))
        sums = []
        for which in range(2):
            acc = {}
            for r in range(size):
                for a in block:
                    at = 32 * (which * UNK + r) + a
                    coef = jnp.broadcast_to(whole[at : at + 1, :], (8, LANES))
                    for e in range(2):
                        term = coef * work[r][e]
                        acc[a, e] = term if r == 0 else acc[a, e] + term
            sums.append(acc)
        left, right = sums
        for a in block:
            for e in range(2):
                by_up = lanes_from(left[a, e], pack_up)
                new = side[a][e] - jnp.where(is_left, right[a, e], by_up)
                if e == 1:
                    new = new - jnp.where(is_rhs, by_up, 0.0)
                side[a][e] = new
        for v in range(first // 8, 4):
            for a in block:
                if v >= a // 8:
                    own = lanes_from(right[a, v % 2], within + GROUPS * (2 + v // 2))
                    diag[a][v] = diag[a][v] - own
            for a in block:
                if v >= a // 8:
                    other = lanes_from(left[a, v % 2], from_up + GROUPS * (v // 2))
                    diag[a][v] = diag[a][v] - other


def advance_wide(work, diag, side, lane, whole, down, up):
    within = lane % NODES
    part = lane // NODES
    from_down = (within - down + NODES) % NODES
    from_up = (within + up) % NODES
    pack_down = part * NODES + from_down
    pack_up = part * NODES + from_up
    is_left = part < 4
    is_rhs = jnp.logical_and(part == 3, iota((8, LANES), 0) == 3)
    for v in range(8):
        for r in range(UNK):
            at = 64 * r + 8 * v
            whole[at : at + 8, :] = lanes_from(work[r][0], within + NODES * v)
    for first in range(0, UNK, BLOCK):
        block = range(first, min(first + BLOCK, UNK))
        sums = []
        for which in range(2):
            acc = {}
            for r in range(UNK):
                for a in block:
                    at = 64 * r + 32 * which + a
                    term = jnp.broadcast_to(whole[at : at + 1, :], (8, LANES)) * work[r][0]
                    acc[a] = term if r == 0 else acc[a] + term
            sums.append(acc)
        left, right = sums
        for a in block:
            by_down = lanes_from(right[a], pack_down)
            by_up = lanes_from(left[a], pack_up)
            new = -jnp.where(is_left, by_down, by_up)
            side[a] = [new + jnp.where(is_rhs, side[a][0] - by_up, 0.0)]
        for v in range(first // 8, 4):
            for a in block:
                if v >= a // 8:
                    own = lanes_from(right[a], from_down + NODES * (4 + v))
                    diag[a][v] = diag[a][v] - own
            for a in block:
                if v >= a // 8:
                    other = lanes_from(left[a], from_up + NODES * v)
                    diag[a][v] = diag[a][v] - other


def solve_kernel(
    core_ref, damp_ref, mine_ref, other_ref, step_ref, cast_ref, rep, back, dmat, smat, xrow, whole
):
    lane = iota((8, LANES), 1)
    sub = iota((8, LANES), 0)
    within = lane % GROUPS
    part = lane // GROUPS
    core = core_ref[0]
    low = jnp.where(core == 0, mine_ref[...], other_ref[...])
    high = jnp.where(core == 0, other_ref[...], mine_ref[...])
    row = iota((HALF, LANES), 0)
    on_diag = row < 0
    for i in range(PARAMS):
        on_diag = jnp.logical_or(on_diag, row == i * 9 - i * (i - 1) // 2)
    low = low + jnp.where(on_diag, damp_ref[0], 0.0)
    first_rows = HALF // 8
    for r in range(4):
        for shift, wanted in ((0, NEEDED[r]), (1, set(range(4 - r, 4)))):
            index = (within + GROUPS - shift) % GROUPS + GROUPS * r
            for n in range(BAND // 8):
                kinds = {d for d in range(4) if ROW_D[d] < 8 * n + 8 and 8 * n < ROW_END[d]}
                if not kinds & wanted:
                    continue
                at = slice(8 * n, 8 * n + 8)
                chunk = low[at] if n < first_rows else high[8 * n - HALF : 8 * n - HALF + 8]
                if shift:
                    back[r - 1, at, :] = lanes_from(chunk, index)
                else:
                    rep[r, at, :] = lanes_from(chunk, index)

    def tri(i):
        return i * 9 - i * (i - 1) // 2

    def line(ref, r, start):
        return jnp.broadcast_to(ref[r, start : start + 1, :], (8, LANES))

    def tail(values):
        out = jnp.zeros((8, LANES), f32)
        for n, value in values:
            out = jnp.where(sub == n, value, out)
        return out

    def forward(r, d, i):
        start = tri(i) - i if d == 0 else ROW_D[d] + 9 * i
        return rep[r, start : start + 8, :], line(rep, r, start + 8)

    def backward(r, d, i):
        start = ROW_D[d] + i
        return back[r - 1, pl.ds(start, 8, stride=9), :], line(back, r - 1, start + 72)

    def pack(lm, um):
        return [
            jnp.where(
                part == 0,
                lm[e],
                jnp.where(part == 1, lm[2 + e], jnp.where(part == 2, um[e], um[2 + e])),
            )
            for e in range(2)
        ]

    def rhs(r, i):
        return line(rep, r, ROW_Q + i)

    def chunked(value, count):
        return [value[8 * v : 8 * v + 8] for v in range(count)]

    zero = jnp.zeros((8, LANES), f32)

    diag0, side0 = [], []
    for i in range(PARAMS):
        diag0.append(list(forward(0, 0, i)))
        after = [forward(0, d, i) for d in (1, 2, 3)]
        before = [backward(4 - d, d, i) for d in (3, 2, 1)]
        lm = [p[0] for p in before]
        lm.append(tail([(n, p[1]) for n, p in enumerate(before)] + [(3, rhs(0, i))]))
        um = [p[0] for p in after]
        um.append(tail([(n, p[1]) for n, p in enumerate(after)]))
        side0.append(pack(lm, um))
    inv0 = factor(PARAMS, diag0, side0, (0, 1))

    diag, side = [], []
    for a in range(UNK):
        r, i = (a // 8 + 1, a % 8) if a < 24 else (a - 23, 8)
        own = {q: forward(r, q - r, i) for q in range(r, 4)}
        ahead = {q: forward(r, 4 + q - r, i) for q in range(1, r)}
        behind = {q: backward(q, 4 + r - q, i) for q in range(r + 1, 4)}
        diag.append([own[q][0] if q in own else zero for q in (1, 2, 3)])
        ninths = [(q - 1, p[1]) for q, p in own.items()]
        ninths += [(q - 1, line(rep, q, ROW_D[r - q] + 72 + i)) for q in range(1, r)]
        diag[a].append(tail(ninths))
        um = [ahead[q][0] if q in ahead else zero for q in (1, 2, 3)]
        um.append(tail([(q - 1, p[1]) for q, p in ahead.items()]))
        lm = [behind[q][0] if q in behind else zero for q in (1, 2, 3)]
        lm.append(tail([(q - 1, p[1]) for q, p in behind.items()] + [(3, rhs(r, i))]))
        side.append(pack(lm, um))
    advance(PARAMS, side0, diag, side, lane, whole)

    few = lane % NODES
    which = lane // NODES
    odd_diag = [[None] * 4 for a in range(UNK)]
    even_diag = [[None] * 4 for a in range(UNK)]
    for n, target in enumerate((even_diag, odd_diag)):
        for a in range(UNK):
            for v in range(a // 8, 4):
                target[a][v] = lanes_from(diag[a][v], 2 * few + n)
    base = 2 * few + GROUPS * (2 * (which // 4) + (which % 4) // 2)
    split = []
    for n in range(2):
        first = [lanes_from(side[a][0], base + n) for a in range(UNK)]
        second = [lanes_from(side[a][1], base + n) for a in range(UNK)]
        split.append([[jnp.where(which % 2 == 0, p, q)] for p, q in zip(first, second)])
    diag, (side, odd_side) = even_diag, split
    odd_inverse = factor(UNK, odd_diag, odd_side, (0,))
    advance_wide(odd_side, diag, side, lane, whole, 1, 0)

    def store(diag, side):
        for a in range(UNK):
            for v in range(a // 8, 4):
                dmat[a, 8 * v : 8 * v + 8, :] = diag[a][v]
            smat[a] = side[a][0]

    def load():
        diag = [
            [dmat[a, 8 * v : 8 * v + 8, :] if v >= a // 8 else None for v in range(4)]
            for a in range(UNK)
        ]
        return diag, [[smat[a]] for a in range(UNK)]

    store(diag, side)

    def level(step, carry):
        stride = lax.shift_left(jnp.int32(1), step)
        diag, side = load()
        factor(UNK, diag, side, (0,))
        work = side
        diag, side = load()
        advance_wide(work, diag, side, lane, whole, stride, stride)
        store(diag, side)
        return carry

    lax.fori_loop(0, 3, level, jnp.int32(0))

    diag, side = load()
    from_left = [lanes_from(side[a][0], few + NODES * (which % 4)) for a in range(UNK)]
    from_right = [lanes_from(side[a][0], few + NODES * (4 + which % 4)) for a in range(UNK)]
    both = [[p + q] for p, q in zip(from_left, from_right)]
    for a in range(UNK):
        right_side = lanes_from(side[a][0], few + 3 * NODES)
        diag[a][3] = jnp.where(sub == 3, right_side, diag[a][3])
    work = [list(line_of) for line_of in diag]
    factor(UNK, work, both, (0,))
    for v in range(4):
        for r in range(UNK):
            at = 64 * r + 8 * v
            whole[at : at + 8, :] = lanes_from(both[r][0], few + NODES * v)
    for first in range(0, UNK, BLOCK):
        block = range(first, min(first + BLOCK, UNK))
        acc = {}
        for r in range(UNK):
            for a in block:
                at = 64 * r + a
                term = jnp.broadcast_to(whole[at : at + 1, :], (8, LANES)) * both[r][0]
                acc[a] = term if r == 0 else acc[a] + term
        for v in range(first // 8, 4):
            for a in block:
                if v >= a // 8:
                    moved = lanes_from(acc[a], (few + NODES // 2) % NODES + NODES * v)
                    diag[a][v] = diag[a][v] - moved
    inverse = factor(UNK, diag, both, ())

    def back_solve(size, diag, inverse, todo):
        value = [None] * size
        for k in range(size - 1, -1, -1):
            value[k] = todo[k] * inverse[k]
            for r in range(k):
                todo[r] = todo[r] - spread_row(diag[r][k // 8], k % 8) * value[k]
        return value

    def as_chunks(value):
        for a in range(UNK):
            xrow[a : a + 1, :] = value[a][0:1]
        xrow[UNK:32, :] = jnp.zeros((5, LANES), f32)
        return chunked(xrow[...], 4)

    even_steps = as_chunks(
        back_solve(UNK, diag, inverse, [spread_row(diag[a][3], 3) for a in range(UNK)])
    )
    packed = jnp.zeros((8, LANES), f32)
    for v in range(4):
        packed = jnp.where(which == v, even_steps[v], packed)
        after = lanes_from(even_steps[v], (few + 1) % NODES)
        packed = jnp.where(which == 4 + v, after, packed)
    right_sides = [lanes_from(odd_side[a][0], few + 3 * NODES) for a in range(UNK)]
    todo = []
    for a in range(UNK):
        terms = odd_side[a][0] * packed
        for shift in (64, 32, 16):
            terms = terms + pltpu.roll(terms, shift, 1)
        summed = jnp.broadcast_to(jnp.sum(terms, axis=0, keepdims=True), (8, LANES))
        todo.append(spread_row(right_sides[a], 3) - summed)
    odd_steps = as_chunks(back_solve(UNK, odd_diag, odd_inverse, todo))
    own = [
        jnp.where(
            lane % 2 == 0,
            lanes_from(even_steps[v], within // 2),
            lanes_from(odd_steps[v], within // 2),
        )
        for v in range(4)
    ]
    prev = [lanes_from(c, (lane + LANES - 1) % LANES) for c in own]
    packed = pack(prev, own)
    todo0 = []
    for i in range(PARAMS):
        terms = side0[i][0] * packed[0] + side0[i][1] * packed[1]
        terms = terms + pltpu.roll(terms, 64, 1)
        terms = terms + pltpu.roll(terms, 32, 1)
        right_side = spread_row(lanes_from(side0[i][1], within + GROUPS), 3)
        summed = jnp.broadcast_to(jnp.sum(terms, axis=0, keepdims=True), (8, LANES))
        todo0.append(right_side - summed)
    value0 = back_solve(PARAMS, diag0, inv0, todo0)
    camera = (lane % 4) * GROUPS + lane // 4
    for i in range(PARAMS):
        near = [spread_row(own[r], i) if i < 8 else spread_row(own[3], r) for r in range(3)]
        mixed = jnp.where(
            part == 0,
            value0[i],
            jnp.where(part == 1, near[0], jnp.where(part == 2, near[1], near[2])),
        )
        step_ref[i : i + 1, :] = lanes_from(mixed, camera)[0:1]
    for dest in range(16):
        cast_ref[dest, 0:PARAMS, :] = step_ref[...]
        cast_ref[dest, PARAMS:16, :] = jnp.zeros((16 - PARAMS, LANES), f32)


def update_kernel(all_ref, jac_ref, real_ref, where_ref, out_ref, dots):
    masks = cluster_masks(where_ref[8:10, :])
    table = [all_ref[16 * c : 16 * c + 8, :] for c in range(16)]
    last = [all_ref[pl.ds(8, 8, stride=16), :], all_ref[pl.ds(136, 8, stride=16), :]]
    lookup_dot(table, last, masks, where_ref, jac_ref, dots)
    dot_all = dots[...]

    def fact(n):
        return real_ref[48 + n : 49 + n, :]

    tot = []
    for a in range(3):
        terms = real_ref[16 * a : 16 * a + 16, :] * dot_all
        tot.append(fact(6 + a) + jnp.sum(terms, axis=0, keepdims=True))
    x3 = tot[2] * fact(2)
    x2 = (tot[1] - fact(5) * x3) * fact(1)
    x1 = (tot[0] - fact(3) * x2 - fact(4) * x3) * fact(0)
    out_ref[0:1, :] = -x1
    out_ref[1:2, :] = -x2
    out_ref[2:3, :] = -x3


def smem():
    return pl.BlockSpec(memory_space=pltpu.SMEM)


def vmem():
    return pl.BlockSpec(memory_space=pltpu.VMEM)


def params(mib):
    return pltpu.CompilerParams(vmem_limit_bytes=mib * MIB)


def run_points(owner_map, damping, jac, jp, res, cam_ids, obs_count, clus, prev):
    npts = 256
    return pl.pallas_call(
        points_kernel,
        out_shape=(
            jax.ShapeDtypeStruct((16, PACK, LANES), f32),
            jax.ShapeDtypeStruct((57, npts), f32),
            jax.ShapeDtypeStruct((2, 8 * PARAMS, npts), f32),
            jax.ShapeDtypeStruct((10, npts), jnp.int32),
        ),
        in_specs=[smem(), smem()] + [pl.BlockSpec(memory_space=pltpu.HBM)] * 7,
        out_specs=(vmem(),) * 4,
        scratch_shapes=[
            pltpu.VMEM((16, npts), f32),
            pltpu.VMEM((2 * PACK, 2 * npts), f32),
            pltpu.VMEM(jac.shape, f32),
            pltpu.VMEM(jp.shape, f32),
            pltpu.VMEM(res.shape, f32),
            pltpu.VMEM(cam_ids.shape, jnp.int32),
            pltpu.VMEM(obs_count.shape, jnp.int32),
            pltpu.VMEM(clus.shape, jnp.int32),
            pltpu.VMEM(prev.shape, f32),
            pltpu.SemaphoreType.DMA((7,)),
        ],
        compiler_params=params(58),
        name="points",
    )(owner_map, damping, jac, jp, res, cam_ids, obs_count, clus, prev)


def run_band(half, recv, name):
    return pl.pallas_call(
        band_kernel,
        out_shape=jax.ShapeDtypeStruct((HALF, LANES), f32),
        in_specs=[smem(), vmem()],
        out_specs=vmem(),
        scratch_shapes=[
            pltpu.VMEM((528 * 8, LANES), f32),
            pltpu.VMEM((3, 528, 1024), bf16),
            pltpu.VMEM((4, LANES, 1024), bf16),
        ],
        compiler_params=params(20),
        cost_estimate=pl.CostEstimate(flops=4 * 10**8, bytes_accessed=10**7, transcendentals=0),
        name=name,
    )(half, recv)


def run_solve(core, damping, mine, other):
    return pl.pallas_call(
        solve_kernel,
        out_shape=(
            jax.ShapeDtypeStruct((PARAMS, LANES), f32),
            jax.ShapeDtypeStruct((16, 16, LANES), f32),
        ),
        in_specs=[smem(), smem(), vmem(), vmem()],
        out_specs=(vmem(), vmem()),
        scratch_shapes=[
            pltpu.VMEM((4, BAND, LANES), f32),
            pltpu.VMEM((3, BAND, LANES), f32),
            pltpu.VMEM((UNK, 32, LANES), f32),
            pltpu.VMEM((UNK, 8, LANES), f32),
            pltpu.VMEM((32, LANES), f32),
            pltpu.VMEM((2 * UNK * 32, LANES), f32),
        ],
        compiler_params=params(12),
        name="solve",
    )(core, damping, mine, other)


def run_update(everything, jac, real, where):
    return pl.pallas_call(
        update_kernel,
        out_shape=jax.ShapeDtypeStruct((3, 256), f32),
        in_specs=[vmem()] * 4,
        out_specs=vmem(),
        scratch_shapes=[pltpu.VMEM((16, 256), f32)],
        compiler_params=params(8),
        name="update",
    )(everything, jac, real, where)


def sum_over_points(keep, given, ring):
    swap = [(i, i ^ 1) for i in range(ring)]
    half = keep + given
    moved = [lax.ppermute(half, "pt", [(i, i ^ (2 * d)) for i in range(ring)]) for d in (1, 2, 3)]
    mine = (half + moved[0]) + (moved[1] + moved[2])
    return mine, lax.ppermute(mine, "pt", swap)


def per_device(
    cam_jac, pt_jac, residual, cam_ids, obs_count, clusters, owner_map, prev_step, damping
):
    npts = cam_jac.shape[-1]
    core = (lax.axis_index("pt") % 2).astype(jnp.int32).reshape(1)
    send, real, jac, where = run_points(
        owner_map,
        damping,
        cam_jac.transpose(0, 1, 3, 2, 4).reshape(8 * PARAMS, 2, npts),
        pt_jac.transpose(0, 1, 3, 2, 4).reshape(24, 2, npts),
        residual.reshape(8, 2, npts),
        cam_ids,
        obs_count,
        clusters.T,
        prev_step.transpose(1, 0, 2).reshape(PARAMS * 16, LANES),
    )
    recv = lax.all_to_all(send, "cl", split_axis=0, concat_axis=0, tiled=True)
    recv = recv.reshape(16 * PACK, LANES)
    ring = lax.axis_size("pt")
    given = lax.ppermute(
        run_band(1 - core, recv, "band_give"), "pt", [(i, i ^ 1) for i in range(ring)]
    )
    mine, other = sum_over_points(run_band(core, recv, "band_keep"), given, ring)
    step, cast = run_solve(core, damping, mine, other)
    everything = lax.all_to_all(cast, "cl", split_axis=0, concat_axis=0, tiled=True)
    point_step = run_update(everything.reshape(256, LANES), jac, real, where)
    return (step[None], point_step)


def solution(mesh):
    in_specs = (
        P(None, None, None, None, ("pt", "cl")),
        P(None, None, None, None, ("pt", "cl")),
        P(None, None, None, ("pt", "cl")),
        P(None, None, ("pt", "cl")),
        P(None, ("pt", "cl")),
        P(("pt", "cl"), None),
        P(),
        P(),
        P(),
    )
    out_specs = (P("cl", None, None), P(None, ("pt", "cl")))
    return jax.shard_map(
        per_device, mesh=mesh, in_specs=in_specs, out_specs=out_specs, check_vma=False
    )
```

```python
import jax
import jax.numpy as jnp
from jax import lax
from jax.experimental import pallas as pl
from jax.experimental.pallas import tpu as pltpu
from jax.sharding import PartitionSpec as P

f32 = jnp.float32
bf16 = jnp.bfloat16
LANES = 128
SLOTS = 4
PARAMS = 9
GROUPS = 32
BLOCK = 9
NODES = 16
UNK = 27
ROW_Q = 45
ROW_D = (0, 54, 135, 216)
ROW_END = (54, 135, 216, 297)
NEEDED = ({0, 1, 2, 3}, {0, 1, 2}, {0, 1, 3}, {0, 2, 3})
BAND = 304
HALF = BAND // 2
DIAG = 45
PACK = 56
MIB = 1024 * 1024


def split3(value):
    high = value.astype(bf16)
    rest = value - high.astype(f32)
    mid = rest.astype(bf16)
    low = (rest - mid.astype(f32)).astype(bf16)
    return high, mid, low


def dot_nt(left, right):
    return lax.dot_general(left, right, (((1,), (1,)), ((), ())), preferred_element_type=f32)


def iota(shape, dim):
    return lax.broadcasted_iota(jnp.int32, shape, dim)


def lanes_from(value, index):
    return jnp.take_along_axis(value, index, axis=1)


def spread_row(chunk, row):
    return jnp.broadcast_to(chunk[row : row + 1, :], (8, LANES))


def lookup_dot(table, last, masks, cam_ref, jac_ref, out_ref):
    for half in range(2):
        cols = slice(half * LANES, (half + 1) * LANES)
        for s in range(2):
            rows, picks = masks[s][half]
            for k in range(SLOTS):
                at = 4 * s + k
                index = jnp.broadcast_to(cam_ref[at : at + 1, cols], (8, LANES))
                chosen = lanes_from(table[0], index)
                for c in range(1, 16):
                    chosen = jnp.where(picks[c], lanes_from(table[c], index), chosen)
                ninth = lanes_from(last[0], index) * rows[0] + lanes_from(last[1], index) * rows[1]
                for m in range(2):
                    base = s * SLOTS * PARAMS + k * PARAMS
                    terms = chosen * jac_ref[m, base : base + 8, cols]
                    terms = terms + ninth * jac_ref[m, base + 8 : base + 9, cols]
                    row = s * 8 + m * 4 + k
                    out_ref[row : row + 1, cols] = jnp.sum(terms, axis=0, keepdims=True)


def cluster_masks(cluster_rows):
    masks = []
    for s in range(2):
        per_half = []
        for half in range(2):
            row = cluster_rows[s : s + 1, half * LANES : (half + 1) * LANES]
            row = jnp.broadcast_to(row, (8, LANES))
            rows = [(iota((8, LANES), 0) + 8 * n == row).astype(f32) for n in range(2)]
            per_half.append((rows, [row == c for c in range(16)]))
        masks.append(per_half)
    return masks


def points_kernel(
    owner_ref,
    damp_ref,
    jac_hbm,
    jp_hbm,
    res_hbm,
    cam_hbm,
    count_hbm,
    clus_hbm,
    prev_hbm,
    send_ref,
    real_ref,
    jm_ref,
    where_ref,
    dots,
    packed,
    jac_ref,
    jp_ref,
    res_ref,
    cam_ref,
    count_ref,
    clus_ref,
    prev_ref,
    arrived,
):
    pairs = [
        (clus_hbm, clus_ref),
        (count_hbm, count_ref),
        (jp_hbm, jp_ref),
        (res_hbm, res_ref),
        (cam_hbm, cam_ref),
        (prev_hbm, prev_ref),
        (jac_hbm, jac_ref),
    ]
    copies = [
        pltpu.make_async_copy(source, target, arrived.at[n])
        for n, (source, target) in enumerate(pairs)
    ]
    for copy in copies:
        copy.start()
    for copy in copies:
        copy.wait()
    npts = 2 * LANES
    for m in range(2):
        jm_ref[m] = jac_ref[:, m, :]
    clus = clus_ref[...]
    dest = jnp.zeros_like(clus)
    for c in range(16):
        dest = jnp.where(clus == c, owner_ref[c], dest)
    where_ref[0:4, :] = cam_ref[0]
    where_ref[4:8, :] = cam_ref[1]
    where_ref[8:10, :] = dest
    slot_row = iota((8, npts), 0) % 4
    live = jnp.concatenate(
        [(slot_row < count_ref[s : s + 1, :]).astype(f32) for s in range(2)], axis=0
    )

    def by_slot(ref, step, first):
        rows = [
            ref[step * (4 * s + k) + first, m : m + 1, :]
            for s in range(2)
            for m in range(2)
            for k in range(SLOTS)
        ]
        return jnp.concatenate(rows, axis=0) * live

    jp = [by_slot(jp_ref, 3, a) for a in range(3)]
    res = by_slot(res_ref, 1, 0)

    def total(value):
        return jnp.sum(value, axis=0, keepdims=True)

    damp = damp_ref[0]
    inv1 = 1.0 / jnp.sqrt(total(jp[0] * jp[0]) + damp)
    l21 = total(jp[1] * jp[0]) * inv1
    l31 = total(jp[2] * jp[0]) * inv1
    inv2 = 1.0 / jnp.sqrt(total(jp[1] * jp[1]) + damp - l21 * l21)
    l32 = (total(jp[2] * jp[1]) - l31 * l21) * inv2
    inv3 = 1.0 / jnp.sqrt(total(jp[2] * jp[2]) + damp - l31 * l31 - l32 * l32)
    p1 = jp[0] * inv1
    p2 = (jp[1] - l21 * p1) * inv2
    p3 = (jp[2] - l31 * p1 - l32 * p2) * inv3
    proj = [p1, p2, p3]
    grad = [total(jp[a] * res) for a in range(3)]
    h1 = grad[0] * inv1
    h2 = (grad[1] - l21 * h1) * inv2
    h3 = (grad[2] - l31 * h1 - l32 * h2) * inv3
    h = [h1, h2, h3]
    for a in range(3):
        real_ref[16 * a : 16 * a + 16, :] = proj[a]
    for n, row in enumerate([inv1, inv2, inv3, l21, l31, l32, h1, h2, h3]):
        real_ref[48 + n : 49 + n, :] = row

    masks = cluster_masks(clus)
    table = [prev_ref[pl.ds(c, 8, stride=16), :] for c in range(16)]
    last = [prev_ref[128:136, :], prev_ref[136:144, :]]
    lookup_dot(table, last, masks, where_ref, jm_ref, dots)
    dot_all = dots[...]
    wt = -res
    for a in range(3):
        terms = proj[a] * dot_all
        carried = [jnp.sum(terms[8 * s : 8 * s + 8], axis=0, keepdims=True) for s in range(2)]
        mixed = jnp.concatenate(
            [jnp.broadcast_to(h[a] + carried[1 - s], (8, npts)) for s in range(2)], axis=0
        )
        wt = wt + proj[a] * mixed

    for s in range(2):
        cols = slice(s * npts, (s + 1) * npts)
        for m in range(2):
            base = m * PACK
            for k in range(SLOTS):
                on = live[s * 8 + m * 4 + k : s * 8 + m * 4 + k + 1, :]
                packed[base + 9 * k : base + 9 * k + 9, cols] = (
                    jm_ref[m, 36 * s + 9 * k : 36 * s + 9 * k + 9, :] * on
                )
            rows = slice(s * 8 + m * 4, s * 8 + m * 4 + 4)
            for a in range(3):
                packed[base + 36 + 4 * a : base + 40 + 4 * a, cols] = proj[a][rows]
            packed[base + 48 : base + 52, cols] = wt[rows]
            packed[base + 52 : base + 53, cols] = cam_ref[s, 0:1, :].astype(f32)
            packed[base + 53 : base + 56, cols] = jnp.zeros((3, npts), f32)

    dest_row = jnp.concatenate([dest[0:1], dest[1:2]], axis=1)
    hot = (iota((16, 2 * npts), 0) == dest_row).astype(f32)
    before = (iota((2 * npts, 2 * npts), 1) < iota((2 * npts, 2 * npts), 0)).astype(bf16)
    earlier = dot_nt(hot.astype(bf16), before)
    place = jnp.sum(earlier * hot, axis=0, keepdims=True)
    slot = dest_row * 64 + place.astype(jnp.int32)
    parts = split3(packed[...])
    left = jnp.concatenate(parts, axis=0)
    low_half = iota((PACK, LANES), 1) < 64
    for quad in range(4):
        slots = iota((2 * LANES, 2 * npts), 0) + quad * 2 * LANES
        pick = (slots == slot).astype(f32).astype(bf16)
        got = dot_nt(left, pick)
        full = got[0 : 2 * PACK] + got[2 * PACK : 4 * PACK] + got[4 * PACK : 6 * PACK]
        for pair in range(2):
            cols = slice(pair * LANES, (pair + 1) * LANES)
            first = full[0:PACK, cols]
            second = full[PACK : 2 * PACK, cols]
            first_r = pltpu.roll(first, 64, 1)
            second_r = pltpu.roll(second, 64, 1)
            send_ref[4 * quad + 2 * pair] = jnp.where(low_half, first, second_r)
            send_ref[4 * quad + 2 * pair + 1] = jnp.where(low_half, first_r, second)


def band_kernel(half_ref, recv_ref, out_ref, rows, wide, hots):
    low_half = iota((8, LANES), 1) < 64
    quant = [[], []]
    for r in range(53):
        even = recv_ref[pl.ds(r, 8, stride=2 * PACK), :]
        odd = recv_ref[pl.ds(PACK + r, 8, stride=2 * PACK), :]
        even_r = pltpu.roll(even, 64, 1)
        odd_r = pltpu.roll(odd, 64, 1)
        quant[0].append(jnp.where(low_half, even, odd_r))
        quant[1].append(jnp.where(low_half, even_r, odd))

    def jac(k, m, i):
        return quant[m][9 * k + i]

    def proj(k, m, a):
        return quant[m][36 + 4 * a + k]

    def wt(k, m):
        return quant[m][48 + k]

    cam = quant[0][52].astype(jnp.int32)
    camera_of = 4 * (iota((LANES, LANES), 0) % GROUPS) + iota((LANES, LANES), 0) // GROUPS

    def part_of_band(half, sizes):
        starts = [sum(sizes[:k]) for k in range(len(sizes))]
        for b in range(8):
            cam_b = jnp.broadcast_to(cam[b : b + 1, :], (LANES, LANES))
            for k in range(len(sizes)):
                hots[k, :, b * LANES : (b + 1) * LANES] = (
                    (camera_of == (cam_b + k) % LANES).astype(f32).astype(bf16)
                )
        out = None
        for k, size in enumerate(sizes):
            seen = set()

            def wanted(row):
                return 0 <= row - HALF * half < HALF

            def put(row, value, k=k, seen=seen):
                local = row - HALF * half
                seen.add(local)
                at = 8 * (starts[k] + local)
                rows[at : at + 8, :] = value

            for dist in range(SLOTS - k):
                other = k + dist
                last = DIAG if dist == 0 else ROW_D[dist] + 81
                start = 0 if dist == 0 else ROW_D[dist]
                if not any(wanted(row) for row in range(start, last)):
                    continue
                mix = [[None, None], [None, None]]
                for m in range(2):
                    for n in range(2):
                        if dist == 0 and n < m:
                            mix[m][n] = mix[n][m]
                            continue
                        acc = proj(k, m, 0) * proj(other, n, 0)
                        acc = acc + proj(k, m, 1) * proj(other, n, 1)
                        acc = acc + proj(k, m, 2) * proj(other, n, 2)
                        same = dist == 0 and m == n
                        mix[m][n] = (1.0 - acc) if same else -acc
                for j in range(PARAMS):
                    left = [
                        mix[m][0] * jac(other, 0, j) + mix[m][1] * jac(other, 1, j)
                        for m in range(2)
                    ]
                    for i in range(PARAMS):
                        if dist == 0:
                            row = i * 9 - i * (i - 1) // 2 + (j - i)
                        else:
                            row = ROW_D[dist] + i * 9 + j
                        if (dist == 0 and i > j) or not wanted(row):
                            continue
                        put(row, jac(k, 0, i) * left[0] + jac(k, 1, i) * left[1])
            for i in range(PARAMS):
                if wanted(ROW_Q + i):
                    put(ROW_Q + i, jac(k, 0, i) * wt(k, 0) + jac(k, 1, i) * wt(k, 1))
            for local in range(size):
                if local not in seen:
                    rows[8 * (starts[k] + local) : 8 * (starts[k] + local) + 8, :] = jnp.zeros(
                        (8, LANES), f32
                    )
            at = slice(starts[k], starts[k] + size)
            for b in range(8):
                piece = rows[pl.ds(8 * starts[k] + b, size, stride=8), :]
                for n, part in enumerate(split3(piece)):
                    wide[n, at, b * LANES : (b + 1) * LANES] = part
            hot = hots[k]
            got = dot_nt(wide[0, at, :], hot)
            got = got + dot_nt(wide[1, at, :], hot)
            got = got + dot_nt(wide[2, at, :], hot)
            if out is None:
                out = got
            elif size == out.shape[0]:
                out = out + got
            else:
                out = jnp.concatenate([out[:size] + got, out[size:]], axis=0)
        out_ref[...] = out[0:HALF]

    @pl.when(half_ref[0] == 0)
    def _():
        part_of_band(0, [160, 160, 144, 64])

    @pl.when(half_ref[0] == 1)
    def _():
        part_of_band(1, [160, 64])


def factor(size, diag, side, side_chunks):
    chunks = len(diag[0])
    inverse = []
    for k in range(size):
        pivot = spread_row(diag[k][k // 8], k % 8)
        root = lax.rsqrt(pivot)
        root = root * (1.5 - 0.5 * pivot * root * root)
        inverse.append(root)
        for v in range(k // 8, chunks):
            diag[k][v] = diag[k][v] * root
        for e in side_chunks:
            side[k][e] = side[k][e] * root
        for r in range(k + 1, size):
            coef = spread_row(diag[k][r // 8], r % 8)
            for v in range(r // 8, chunks):
                diag[r][v] = diag[r][v] - coef * diag[k][v]
            for e in side_chunks:
                side[r][e] = side[r][e] - coef * side[k][e]
    return inverse


def advance(size, work, diag, side, lane, whole):
    within = lane % GROUPS
    part = lane // GROUPS
    from_up = (within + 1) % GROUPS
    pack_up = part * GROUPS + from_up
    is_left = part < 2
    is_rhs = jnp.logical_and(part == 1, iota((8, LANES), 0) == 3)
    for which in range(2):
        for v in range(4):
            for r in range(size):
                at = 32 * (which * UNK + r) + 8 * v
                whole[at : at + 8, :] = lanes_from(
                    work[r][v % 2], within + GROUPS * (2 * which + v // 2)
                )
    for first in range(0, UNK, BLOCK):
        block = range(first, min(first + BLOCK, UNK))
        sums = []
        for which in range(2):
            acc = {}
            for r in range(size):
                for a in block:
                    at = 32 * (which * UNK + r) + a
                    coef = jnp.broadcast_to(whole[at : at + 1, :], (8, LANES))
                    for e in range(2):
                        term = coef * work[r][e]
                        acc[a, e] = term if r == 0 else acc[a, e] + term
            sums.append(acc)
        left, right = sums
        for a in block:
            for e in range(2):
                by_up = lanes_from(left[a, e], pack_up)
                new = side[a][e] - jnp.where(is_left, right[a, e], by_up)
                if e == 1:
                    new = new - jnp.where(is_rhs, by_up, 0.0)
                side[a][e] = new
        for v in range(first // 8, 4):
            for a in block:
                if v >= a // 8:
                    own = lanes_from(right[a, v % 2], within + GROUPS * (2 + v // 2))
                    diag[a][v] = diag[a][v] - own
            for a in block:
                if v >= a // 8:
                    other = lanes_from(left[a, v % 2], from_up + GROUPS * (v // 2))
                    diag[a][v] = diag[a][v] - other


def advance_wide(work, diag, side, lane, whole, down, up):
    within = lane % NODES
    part = lane // NODES
    from_down = (within - down + NODES) % NODES
    from_up = (within + up) % NODES
    pack_down = part * NODES + from_down
    pack_up = part * NODES + from_up
    is_left = part < 4
    is_rhs = jnp.logical_and(part == 3, iota((8, LANES), 0) == 3)
    for v in range(8):
        for r in range(UNK):
            at = 64 * r + 8 * v
            whole[at : at + 8, :] = lanes_from(work[r][0], within + NODES * v)
    for first in range(0, UNK, BLOCK):
        block = range(first, min(first + BLOCK, UNK))
        sums = []
        for which in range(2):
            acc = {}
            for r in range(UNK):
                for a in block:
                    at = 64 * r + 32 * which + a
                    term = jnp.broadcast_to(whole[at : at + 1, :], (8, LANES)) * work[r][0]
                    acc[a] = term if r == 0 else acc[a] + term
            sums.append(acc)
        left, right = sums
        for a in block:
            by_down = lanes_from(right[a], pack_down)
            by_up = lanes_from(left[a], pack_up)
            new = -jnp.where(is_left, by_down, by_up)
            side[a] = [new + jnp.where(is_rhs, side[a][0] - by_up, 0.0)]
        for v in range(first // 8, 4):
            for a in block:
                if v >= a // 8:
                    own = lanes_from(right[a], from_down + NODES * (4 + v))
                    diag[a][v] = diag[a][v] - own
            for a in block:
                if v >= a // 8:
                    other = lanes_from(left[a], from_up + NODES * v)
                    diag[a][v] = diag[a][v] - other


def solve_kernel(
    core_ref, damp_ref, mine_ref, other_ref, step_ref, cast_ref, rep, back, xrow, whole
):
    lane = iota((8, LANES), 1)
    sub = iota((8, LANES), 0)
    within = lane % GROUPS
    part = lane // GROUPS
    core = core_ref[0]
    low = jnp.where(core == 0, mine_ref[...], other_ref[...])
    high = jnp.where(core == 0, other_ref[...], mine_ref[...])
    row = iota((HALF, LANES), 0)
    on_diag = row < 0
    for i in range(PARAMS):
        on_diag = jnp.logical_or(on_diag, row == i * 9 - i * (i - 1) // 2)
    low = low + jnp.where(on_diag, damp_ref[0], 0.0)
    first_rows = HALF // 8
    for r in range(4):
        for shift, wanted in ((0, NEEDED[r]), (1, set(range(4 - r, 4)))):
            index = (within + GROUPS - shift) % GROUPS + GROUPS * r
            for n in range(BAND // 8):
                kinds = {d for d in range(4) if ROW_D[d] < 8 * n + 8 and 8 * n < ROW_END[d]}
                if not kinds & wanted:
                    continue
                at = slice(8 * n, 8 * n + 8)
                chunk = low[at] if n < first_rows else high[8 * n - HALF : 8 * n - HALF + 8]
                if shift:
                    back[r - 1, at, :] = lanes_from(chunk, index)
                else:
                    rep[r, at, :] = lanes_from(chunk, index)

    def tri(i):
        return i * 9 - i * (i - 1) // 2

    def line(ref, r, start):
        return jnp.broadcast_to(ref[r, start : start + 1, :], (8, LANES))

    def tail(values):
        out = jnp.zeros((8, LANES), f32)
        for n, value in values:
            out = jnp.where(sub == n, value, out)
        return out

    def forward(r, d, i):
        start = tri(i) - i if d == 0 else ROW_D[d] + 9 * i
        return rep[r, start : start + 8, :], line(rep, r, start + 8)

    def backward(r, d, i):
        start = ROW_D[d] + i
        return back[r - 1, pl.ds(start, 8, stride=9), :], line(back, r - 1, start + 72)

    def pack(lm, um):
        return [
            jnp.where(
                part == 0,
                lm[e],
                jnp.where(part == 1, lm[2 + e], jnp.where(part == 2, um[e], um[2 + e])),
            )
            for e in range(2)
        ]

    def rhs(r, i):
        return line(rep, r, ROW_Q + i)

    def chunked(value, count):
        return [value[8 * v : 8 * v + 8] for v in range(count)]

    zero = jnp.zeros((8, LANES), f32)

    diag0, side0 = [], []
    for i in range(PARAMS):
        diag0.append(list(forward(0, 0, i)))
        after = [forward(0, d, i) for d in (1, 2, 3)]
        before = [backward(4 - d, d, i) for d in (3, 2, 1)]
        lm = [p[0] for p in before]
        lm.append(tail([(n, p[1]) for n, p in enumerate(before)] + [(3, rhs(0, i))]))
        um = [p[0] for p in after]
        um.append(tail([(n, p[1]) for n, p in enumerate(after)]))
        side0.append(pack(lm, um))
    inv0 = factor(PARAMS, diag0, side0, (0, 1))

    diag, side = [], []
    for a in range(UNK):
        r, i = (a // 8 + 1, a % 8) if a < 24 else (a - 23, 8)
        own = {q: forward(r, q - r, i) for q in range(r, 4)}
        ahead = {q: forward(r, 4 + q - r, i) for q in range(1, r)}
        behind = {q: backward(q, 4 + r - q, i) for q in range(r + 1, 4)}
        diag.append([own[q][0] if q in own else zero for q in (1, 2, 3)])
        ninths = [(q - 1, p[1]) for q, p in own.items()]
        ninths += [(q - 1, line(rep, q, ROW_D[r - q] + 72 + i)) for q in range(1, r)]
        diag[a].append(tail(ninths))
        um = [ahead[q][0] if q in ahead else zero for q in (1, 2, 3)]
        um.append(tail([(q - 1, p[1]) for q, p in ahead.items()]))
        lm = [behind[q][0] if q in behind else zero for q in (1, 2, 3)]
        lm.append(tail([(q - 1, p[1]) for q, p in behind.items()] + [(3, rhs(r, i))]))
        side.append(pack(lm, um))
    advance(PARAMS, side0, diag, side, lane, whole)

    few = lane % NODES
    which = lane // NODES
    odd_diag = [[None] * 4 for a in range(UNK)]
    even_diag = [[None] * 4 for a in range(UNK)]
    for n, target in enumerate((even_diag, odd_diag)):
        for a in range(UNK):
            for v in range(a // 8, 4):
                target[a][v] = lanes_from(diag[a][v], 2 * few + n)
    base = 2 * few + GROUPS * (2 * (which // 4) + (which % 4) // 2)
    split = []
    for n in range(2):
        first = [lanes_from(side[a][0], base + n) for a in range(UNK)]
        second = [lanes_from(side[a][1], base + n) for a in range(UNK)]
        split.append([[jnp.where(which % 2 == 0, p, q)] for p, q in zip(first, second)])
    diag, (side, odd_side) = even_diag, split
    odd_inverse = factor(UNK, odd_diag, odd_side, (0,))
    advance_wide(odd_side, diag, side, lane, whole, 1, 0)

    for step in range(3):
        work_diag = [list(line_of) for line_of in diag]
        work = [list(line_of) for line_of in side]
        factor(UNK, work_diag, work, (0,))
        advance_wide(work, diag, side, lane, whole, 2**step, 2**step)

    from_left = [lanes_from(side[a][0], few + NODES * (which % 4)) for a in range(UNK)]
    from_right = [lanes_from(side[a][0], few + NODES * (4 + which % 4)) for a in range(UNK)]
    both = [[p + q] for p, q in zip(from_left, from_right)]
    for a in range(UNK):
        right_side = lanes_from(side[a][0], few + 3 * NODES)
        diag[a][3] = jnp.where(sub == 3, right_side, diag[a][3])
    work = [list(line_of) for line_of in diag]
    factor(UNK, work, both, (0,))
    for v in range(4):
        for r in range(UNK):
            at = 64 * r + 8 * v
            whole[at : at + 8, :] = lanes_from(both[r][0], few + NODES * v)
    for first in range(0, UNK, BLOCK):
        block = range(first, min(first + BLOCK, UNK))
        acc = {}
        for r in range(UNK):
            for a in block:
                at = 64 * r + a
                term = jnp.broadcast_to(whole[at : at + 1, :], (8, LANES)) * both[r][0]
                acc[a] = term if r == 0 else acc[a] + term
        for v in range(first // 8, 4):
            for a in block:
                if v >= a // 8:
                    moved = lanes_from(acc[a], (few + NODES // 2) % NODES + NODES * v)
                    diag[a][v] = diag[a][v] - moved
    inverse = factor(UNK, diag, both, ())

    def back_solve(size, diag, inverse, todo):
        value = [None] * size
        for k in range(size - 1, -1, -1):
            value[k] = todo[k] * inverse[k]
            for r in range(k):
                todo[r] = todo[r] - spread_row(diag[r][k // 8], k % 8) * value[k]
        return value

    def as_chunks(value):
        for a in range(UNK):
            xrow[a : a + 1, :] = value[a][0:1]
        xrow[UNK:32, :] = jnp.zeros((5, LANES), f32)
        return chunked(xrow[...], 4)

    even_steps = as_chunks(
        back_solve(UNK, diag, inverse, [spread_row(diag[a][3], 3) for a in range(UNK)])
    )
    packed = jnp.zeros((8, LANES), f32)
    for v in range(4):
        packed = jnp.where(which == v, even_steps[v], packed)
        after = lanes_from(even_steps[v], (few + 1) % NODES)
        packed = jnp.where(which == 4 + v, after, packed)
    right_sides = [lanes_from(odd_side[a][0], few + 3 * NODES) for a in range(UNK)]
    todo = []
    for a in range(UNK):
        terms = odd_side[a][0] * packed
        for shift in (64, 32, 16):
            terms = terms + pltpu.roll(terms, shift, 1)
        summed = jnp.broadcast_to(jnp.sum(terms, axis=0, keepdims=True), (8, LANES))
        todo.append(spread_row(right_sides[a], 3) - summed)
    odd_steps = as_chunks(back_solve(UNK, odd_diag, odd_inverse, todo))
    own = [
        jnp.where(
            lane % 2 == 0,
            lanes_from(even_steps[v], within // 2),
            lanes_from(odd_steps[v], within // 2),
        )
        for v in range(4)
    ]
    prev = [lanes_from(c, (lane + LANES - 1) % LANES) for c in own]
    packed = pack(prev, own)
    todo0 = []
    for i in range(PARAMS):
        terms = side0[i][0] * packed[0] + side0[i][1] * packed[1]
        terms = terms + pltpu.roll(terms, 64, 1)
        terms = terms + pltpu.roll(terms, 32, 1)
        right_side = spread_row(lanes_from(side0[i][1], within + GROUPS), 3)
        summed = jnp.broadcast_to(jnp.sum(terms, axis=0, keepdims=True), (8, LANES))
        todo0.append(right_side - summed)
    value0 = back_solve(PARAMS, diag0, inv0, todo0)
    camera = (lane % 4) * GROUPS + lane // 4
    for i in range(PARAMS):
        near = [spread_row(own[r], i) if i < 8 else spread_row(own[3], r) for r in range(3)]
        mixed = jnp.where(
            part == 0,
            value0[i],
            jnp.where(part == 1, near[0], jnp.where(part == 2, near[1], near[2])),
        )
        step_ref[i : i + 1, :] = lanes_from(mixed, camera)[0:1]
    for dest in range(16):
        cast_ref[dest, 0:PARAMS, :] = step_ref[...]
        cast_ref[dest, PARAMS:16, :] = jnp.zeros((16 - PARAMS, LANES), f32)


def update_kernel(all_ref, jac_ref, real_ref, where_ref, out_ref, dots):
    masks = cluster_masks(where_ref[8:10, :])
    table = [all_ref[16 * c : 16 * c + 8, :] for c in range(16)]
    last = [all_ref[pl.ds(8, 8, stride=16), :], all_ref[pl.ds(136, 8, stride=16), :]]
    lookup_dot(table, last, masks, where_ref, jac_ref, dots)
    dot_all = dots[...]

    def fact(n):
        return real_ref[48 + n : 49 + n, :]

    tot = []
    for a in range(3):
        terms = real_ref[16 * a : 16 * a + 16, :] * dot_all
        tot.append(fact(6 + a) + jnp.sum(terms, axis=0, keepdims=True))
    x3 = tot[2] * fact(2)
    x2 = (tot[1] - fact(5) * x3) * fact(1)
    x1 = (tot[0] - fact(3) * x2 - fact(4) * x3) * fact(0)
    out_ref[0:1, :] = -x1
    out_ref[1:2, :] = -x2
    out_ref[2:3, :] = -x3


def smem():
    return pl.BlockSpec(memory_space=pltpu.SMEM)


def vmem():
    return pl.BlockSpec(memory_space=pltpu.VMEM)


def params(mib):
    return pltpu.CompilerParams(vmem_limit_bytes=mib * MIB)


def run_points(owner_map, damping, jac, jp, res, cam_ids, obs_count, clus, prev):
    npts = 256
    return pl.pallas_call(
        points_kernel,
        out_shape=(
            jax.ShapeDtypeStruct((16, PACK, LANES), f32),
            jax.ShapeDtypeStruct((57, npts), f32),
            jax.ShapeDtypeStruct((2, 8 * PARAMS, npts), f32),
            jax.ShapeDtypeStruct((10, npts), jnp.int32),
        ),
        in_specs=[smem(), smem()] + [pl.BlockSpec(memory_space=pltpu.HBM)] * 7,
        out_specs=(vmem(),) * 4,
        scratch_shapes=[
            pltpu.VMEM((16, npts), f32),
            pltpu.VMEM((2 * PACK, 2 * npts), f32),
            pltpu.VMEM(jac.shape, f32),
            pltpu.VMEM(jp.shape, f32),
            pltpu.VMEM(res.shape, f32),
            pltpu.VMEM(cam_ids.shape, jnp.int32),
            pltpu.VMEM(obs_count.shape, jnp.int32),
            pltpu.VMEM(clus.shape, jnp.int32),
            pltpu.VMEM(prev.shape, f32),
            pltpu.SemaphoreType.DMA((7,)),
        ],
        compiler_params=params(58),
        name="points",
    )(owner_map, damping, jac, jp, res, cam_ids, obs_count, clus, prev)


def run_band(half, recv, name):
    return pl.pallas_call(
        band_kernel,
        out_shape=jax.ShapeDtypeStruct((HALF, LANES), f32),
        in_specs=[smem(), vmem()],
        out_specs=vmem(),
        scratch_shapes=[
            pltpu.VMEM((528 * 8, LANES), f32),
            pltpu.VMEM((3, 528, 1024), bf16),
            pltpu.VMEM((4, LANES, 1024), bf16),
        ],
        compiler_params=params(20),
        cost_estimate=pl.CostEstimate(flops=4 * 10**8, bytes_accessed=10**7, transcendentals=0),
        name=name,
    )(half, recv)


def run_solve(core, damping, mine, other):
    return pl.pallas_call(
        solve_kernel,
        out_shape=(
            jax.ShapeDtypeStruct((PARAMS, LANES), f32),
            jax.ShapeDtypeStruct((16, 16, LANES), f32),
        ),
        in_specs=[smem(), smem(), vmem(), vmem()],
        out_specs=(vmem(), vmem()),
        scratch_shapes=[
            pltpu.VMEM((4, BAND, LANES), f32),
            pltpu.VMEM((3, BAND, LANES), f32),
            pltpu.VMEM((32, LANES), f32),
            pltpu.VMEM((2 * UNK * 32, LANES), f32),
        ],
        compiler_params=params(12),
        name="solve",
    )(core, damping, mine, other)


def run_update(everything, jac, real, where):
    return pl.pallas_call(
        update_kernel,
        out_shape=jax.ShapeDtypeStruct((3, 256), f32),
        in_specs=[vmem()] * 4,
        out_specs=vmem(),
        scratch_shapes=[pltpu.VMEM((16, 256), f32)],
        compiler_params=params(8),
        name="update",
    )(everything, jac, real, where)


def sum_over_points(keep, given, ring):
    swap = [(i, i ^ 1) for i in range(ring)]
    half = keep + given
    moved = [lax.ppermute(half, "pt", [(i, i ^ (2 * d)) for i in range(ring)]) for d in (1, 2, 3)]
    mine = (half + moved[0]) + (moved[1] + moved[2])
    return mine, lax.ppermute(mine, "pt", swap)


def per_device(
    cam_jac, pt_jac, residual, cam_ids, obs_count, clusters, owner_map, prev_step, damping
):
    npts = cam_jac.shape[-1]
    core = (lax.axis_index("pt") % 2).astype(jnp.int32).reshape(1)
    send, real, jac, where = run_points(
        owner_map,
        damping,
        cam_jac.transpose(0, 1, 3, 2, 4).reshape(8 * PARAMS, 2, npts),
        pt_jac.transpose(0, 1, 3, 2, 4).reshape(24, 2, npts),
        residual.reshape(8, 2, npts),
        cam_ids,
        obs_count,
        clusters.T,
        prev_step.transpose(1, 0, 2).reshape(PARAMS * 16, LANES),
    )
    recv = lax.all_to_all(send, "cl", split_axis=0, concat_axis=0, tiled=True)
    recv = recv.reshape(16 * PACK, LANES)
    ring = lax.axis_size("pt")
    given = lax.ppermute(
        run_band(1 - core, recv, "band_give"), "pt", [(i, i ^ 1) for i in range(ring)]
    )
    mine, other = sum_over_points(run_band(core, recv, "band_keep"), given, ring)
    step, cast = run_solve(core, damping, mine, other)
    everything = lax.all_to_all(cast, "cl", split_axis=0, concat_axis=0, tiled=True)
    point_step = run_update(everything.reshape(256, LANES), jac, real, where)
    return (step[None], point_step)


def solution(mesh):
    in_specs = (
        P(None, None, None, None, ("pt", "cl")),
        P(None, None, None, None, ("pt", "cl")),
        P(None, None, None, ("pt", "cl")),
        P(None, None, ("pt", "cl")),
        P(None, ("pt", "cl")),
        P(("pt", "cl"), None),
        P(),
        P(),
        P(),
    )
    out_specs = (P("cl", None, None), P(None, ("pt", "cl")))
    return jax.shard_map(
        per_device, mesh=mesh, in_specs=in_specs, out_specs=out_specs, check_vma=False
    )
```
